32 devices in a mesh: seq: 8 (over y, x, core), batch: 4 (over z).
Axes of the slice: x: 2, y: 2, z: 4, core: 2. Of those that a mesh axis runs over, the one named last changes fastest.
Arguments:
- tokens: bfloat16 [4, 1024, 2048], P('batch', 'seq'), may hold values from -6 to 6
- segments: int32 [4, 1024], P('batch'), may hold values from 0 to 3, as said below
- expert_ids: int32 [4, 1024, 8], P('batch', 'seq'), may hold values from 0 to 15, all different within a row; in each aligned block of 128 rows (0 to 127, 128 to 255, ..., all dimensions but the last counted through in order) at most 96 rows name the same one
- w_query: bfloat16 [2048, 2048], P(('seq', 'batch')), may hold values from -0.125 to 0.125
- w_key: bfloat16 [2048, 2048], P(('seq', 'batch')), may hold values from -0.125 to 0.125
- w_value: bfloat16 [2048, 2048], P(('seq', 'batch')), may hold values from -0.125 to 0.125
- w_out: bfloat16 [2048, 2048], P(('seq', 'batch')), may hold values from -3 to 3
- w_router: bfloat16 [2048, 16], P(('seq', 'batch')), may hold values from -0.0625 to 0.0625
- attn_gain: bfloat16 [2048], P(('seq', 'batch')), may hold values from 0.25 to 1.75
- query_gain: bfloat16 [2048], P(('seq', 'batch')), may hold values from 0.25 to 1.75
- key_gain: bfloat16 [2048], P(('seq', 'batch')), may hold values from 0.25 to 1.75
- ffn_gain: bfloat16 [2048], P(('seq', 'batch')), may hold values from 0.25 to 1.75
- w_gate: bfloat16 [16, 2048, 1024], P('seq'), may hold values from -0.125 to 0.125
- w_up: bfloat16 [16, 2048, 1024], P('seq'), may hold values from -0.125 to 0.125
- w_down: bfloat16 [16, 1024, 2048], P('seq'), may hold values from -1 to 1
- out_grad: bfloat16 [4, 1024, 2048], P('batch', 'seq'), may hold values from -6 to 6
Outputs:
- block_out: bfloat16 [4, 1024, 2048], P('batch', 'seq')
- input_grad: float32 [4, 1024, 2048], P('batch', 'seq')
- query_grad: float32 [2048, 2048], P(('seq', 'batch'))
- key_grad: float32 [2048, 2048], P(('seq', 'batch'))
- value_grad: float32 [2048, 2048], P(('seq', 'batch'))
- out_proj_grad: float32 [2048, 2048], P(('seq', 'batch'))
- router_grad: float32 [2048, 16], P(('seq', 'batch'))
- attn_gain_grad: float32 [2048], P(('seq', 'batch'))
- query_gain_grad: float32 [2048], P(('seq', 'batch'))
- key_gain_grad: float32 [2048], P(('seq', 'batch'))
- ffn_gain_grad: float32 [2048], P(('seq', 'batch'))
- gate_grad: float32 [16, 2048, 1024], P('seq', 'batch')
- up_grad: float32 [16, 2048, 1024], P('seq', 'batch')
- down_grad: float32 [16, 1024, 2048], P('seq', 'batch')
- expert_counts: int32 [4, 16], P('batch', 'seq')
The draws below stay inside these ranges and needn't reach their ends.
Inputs may be any that keep to these rules, and one draw needn't show every extreme that they name: `segments`: along each sequence the ids start at 0 and never fall; the document with id 1 begins within the first 128 positions and ends within the last 128 positions. `expert_ids`: each token names 8 different experts. In the rows of one device no expert is named by more than 96 rows; in some devices' rows an expert is named by exactly 96.
All inputs are finite; a program needn't handle non-finite values.
Results may differ from the reference program's by a relative error of at most 0.03.
Values may be sent and summed in bfloat16 or wider, within the bound.
No kernel may reach another device: no remote copies, remote signals or barrier semaphores. Data moves between devices by JAX's collectives and lax.ppermute only.
A program may use at most 384 MiB of HBM per device.

```python
import math
import jax
import jax.numpy as jnp
import numpy as np
from jax import lax

D = 2048
HEAD_DIM = 128
FF = 1024
TOP = 8
TOK_DEV = 128
SEQS = 4
LEN = 1024
EXPERTS = 16
CAP = 96
N_SEQ = 8


def draw_segments(key, part):
    key = jax.random.fold_in(key, 7)
    first_key, second_key, third_key = jax.random.split(key, 3)
    first_cut = jax.random.randint(first_key, (SEQS, 1), 1, TOK_DEV)
    tail = jax.random.randint(second_key, (SEQS, 1), 2, TOK_DEV)
    second_cut = LEN - tail
    third_cut = second_cut + jax.random.randint(third_key, (SEQS, 1), 1, tail)
    positions = jnp.arange(LEN, dtype=jnp.int32)[None, :]
    return (positions >= first_cut).astype(jnp.int32) + (positions >= second_cut).astype(jnp.int32) + (positions >= third_cut).astype(jnp.int32)


def levels(rng, extent, cuts, least, largest):
    loudness, own = 1.0, jax.random.fold_in(rng, 6)
    for dim, shards_of in cuts:
        heights = jnp.exp(jax.random.uniform(jax.random.fold_in(own, dim), (shards_of,), jnp.float32, least / len(cuts), largest / len(cuts)))
        loudness = loudness * jnp.repeat(heights, extent[dim] // shards_of).reshape([-1 if axis == dim else 1 for axis in range(len(extent))])
    return loudness


def deal_out(key, own, number, rows, amount, top, bound, slope):
    order = jax.random.permutation(key, amount)
    packed, common = shares(amount, rows * top, bound, slope, True), shares(amount, rows * top, bound, slope, False)
    places = jnp.arange(amount)

    def named(lengths, offset_by):
        used = int((lengths > 0).sum())
        fixed = max(1, used // 4)
        shifted = fixed + (places - fixed + offset_by * (used - fixed)) % max(1, amount - fixed)
        return jnp.zeros((amount,), jnp.int32).at[order[jnp.where(places < fixed, places, shifted)]].set(jnp.asarray(lengths, jnp.int32))

    lengths = jnp.where(number % 4 == 0, named(packed, number // 4), named(common, number - number // 4 - 1))
    mixed = jax.random.permutation(jax.random.fold_in(own, 3), amount)
    donor, taker = mixed[0:amount // 2 * 2:2], mixed[1:amount // 2 * 2:2]
    slack = jnp.minimum(lengths[donor] - 1, bound - lengths[taker]) // 2
    slack = jnp.where((donor == order[0]) | (taker == order[0]) | (lengths[taker] == 0), 0, jnp.maximum(slack, 0))
    shifted = jax.random.randint(jax.random.fold_in(own, 4), (amount // 2,), 0, 1 << 20) % (slack + 1)
    lengths = lengths.at[donor].add(-shifted).at[taker].add(shifted)
    items = jnp.searchsorted(jnp.cumsum(lengths), jnp.arange(rows * top), side="right").astype(jnp.int32)
    listing = items.reshape(top, rows).T
    listing = listing[jax.random.permutation(jax.random.fold_in(own, 1), rows)]
    offset_by = jax.random.randint(jax.random.fold_in(own, 2), (rows, 1), 0, top)
    return jnp.take_along_axis(listing, (jnp.arange(top)[None, :] + offset_by) % top, axis=1)


def shares(amount, total, limit, slope, full):
    loads = [(1 << 20) // math.isqrt(grade ** slope) + 1 for grade in range(1, amount + 1)]
    largest = limit if full else min(limit, max(-(-total // amount), total * loads[0] // sum(loads)))
    least = 1 if total - largest >= amount - 1 else 0
    holding, rest = [largest] + [least] * (amount - 1), total - largest - least * (amount - 1)
    while rest > 0:
        candidates = [i for i in range(1, amount) if holding[i] < largest] or [i for i in range(1, amount) if holding[i] < limit]
        whole, remaining = sum([loads[i] for i in candidates]), rest
        for i in candidates:
            addition = min(limit - holding[i], max(1, remaining * loads[i] // whole), rest)
            holding[i] = holding[i] + addition
            rest = rest - addition
    return np.array(holding)


def gaussian(rng, extent, spread, bound, cuts=(), kind=jnp.bfloat16):
    gain = levels(rng, extent, cuts, -0.22, 0.18) if cuts else 1.0
    drawn = jax.random.normal(rng, extent, jnp.float32) * spread * gain
    return jnp.minimum(jnp.maximum(drawn, -bound), bound).astype(kind)


def setup_inputs(seed: int = 0) -> dict:
    seeds = jax.random.split(jax.random.key(seed), 17)
    tokens = gaussian(seeds[0], (SEQS, LEN, D), 1.0, 6.0, ((0, 4), (1, 8)))
    segments = draw_segments(jax.random.fold_in(seeds[16], 71), 0)
    expert_ids_keys = jax.random.split(jax.random.fold_in(seeds[2], 1), SEQS * LEN // TOK_DEV)
    expert_ids_turns = jax.random.permutation(jax.random.fold_in(seeds[2], 3), SEQS * LEN // TOK_DEV)
    expert_ids = jax.vmap(lambda own, number: deal_out(jax.random.fold_in(seeds[2], 2), own, number, TOK_DEV, EXPERTS, TOP, CAP, 1))(expert_ids_keys, expert_ids_turns).reshape((SEQS, LEN, TOP))
    w_query = gaussian(seeds[3], (D, D), D ** -0.5, 0.125, ((0, 32),))
    w_key = gaussian(seeds[4], (D, D), D ** -0.5, 0.125, ((0, 32),))
    w_value = gaussian(seeds[5], (D, D), D ** -0.5, 0.125, ((0, 32),))
    w_out = gaussian(seeds[6], (D, D), (max(D // 512, 1)) ** -0.5, 3.0, ((0, 32),))
    w_router = gaussian(seeds[7], (D, EXPERTS), (4 * D) ** -0.5, 0.0625, ((0, 32),))
    attn_gain = jnp.clip(1.0 + 0.15 * jax.random.normal(seeds[8], (D,), jnp.float32), 0.25, 1.75).astype(jnp.bfloat16)
    query_gain = jnp.clip(1.0 + 0.15 * jax.random.normal(seeds[9], (D,), jnp.float32), 0.25, 1.75).astype(jnp.bfloat16)
    key_gain = jnp.clip(1.0 + 0.15 * jax.random.normal(seeds[10], (D,), jnp.float32), 0.25, 1.75).astype(jnp.bfloat16)
    ffn_gain = jnp.clip(1.0 + 0.15 * jax.random.normal(seeds[11], (D,), jnp.float32), 0.25, 1.75).astype(jnp.bfloat16)
    w_gate = gaussian(seeds[12], (EXPERTS, D, FF), D ** -0.5, 0.125, ((0, 8),))
    w_up = gaussian(seeds[13], (EXPERTS, D, FF), D ** -0.5, 0.125, ((0, 8),))
    w_down = gaussian(seeds[14], (EXPERTS, FF, D), (max(FF // 32, 1)) ** -0.5, 1.0, ((0, 8),))
    out_grad = gaussian(seeds[15], (SEQS, LEN, D), 1.0, 6.0, ((0, 4), (1, 8)))
    return dict(tokens=tokens, segments=segments, expert_ids=expert_ids, w_query=w_query, w_key=w_key, w_value=w_value, w_out=w_out, w_router=w_router, attn_gain=attn_gain, query_gain=query_gain, key_gain=key_gain, ffn_gain=ffn_gain, w_gate=w_gate, w_up=w_up, w_down=w_down, out_grad=out_grad)


EPSILON = 1e-05
ROTARY_BASE = 10000.0
MASKED = -1e+30
HIGH = lax.Precision.HIGHEST

@jax.custom_vjp
def low(v):
    return lax.optimization_barrier(v.astype(jnp.bfloat16)).astype(jnp.float32)

@jax.custom_vjp
def low_back(v):
    return v

def low_keep(v):
    return (low(v), None)

def low_pass(kept, grad):
    return (grad,)

def back_keep(v):
    return (v, None)

def back_low(kept, grad):
    return (low(grad),)
low.defvjp(low_keep, low_pass)
low_back.defvjp(back_keep, back_low)

def rms_unit(values):
    return values * lax.rsqrt(lax.optimization_barrier(jnp.mean(values * values, axis=-1, keepdims=True)) + EPSILON)

def matmul(left, right):
    return jnp.dot(left, right, precision=HIGH)

def rotary_tables(positions, head_dim):
    half = head_dim // 2
    rates = jnp.power(ROTARY_BASE, -jnp.arange(half, dtype=jnp.float32) * (2.0 / head_dim))
    angles = positions.astype(jnp.float32)[:, None] * rates[None, :]
    return (jnp.cos(angles)[:, None, :], jnp.sin(angles)[:, None, :])

def rotate(values, cosine, sine):
    half = values.shape[-1] // 2
    first, second = (values[..., :half], values[..., half:])
    return jnp.concatenate([first * cosine - second * sine, second * cosine + first * sine], axis=-1)

def sequence_forward(params, inputs, docs, choose):
    w_query, w_key, w_value, w_out, w_router, attn_gain, query_gain, key_gain, ffn_gain, w_gate, w_up, w_down = params
    length, width = inputs.shape
    heads = width // HEAD_DIM
    positions = jnp.arange(length, dtype=jnp.int32)
    cosine, sine = rotary_tables(positions, HEAD_DIM)
    normed = low(rms_unit(inputs) * attn_gain)
    query_proj = low_back(matmul(normed, w_query))
    key_proj = low_back(matmul(normed, w_key))
    value_proj = low_back(matmul(normed, w_value))
    queries = low(rotate((rms_unit(query_proj) * query_gain).reshape(length, heads, HEAD_DIM), cosine, sine))
    keys = low(rotate((rms_unit(key_proj) * key_gain).reshape(length, heads, HEAD_DIM), cosine, sine))
    values = low(value_proj).reshape(length, heads, HEAD_DIM)
    block = min(512, length)
    factor = 1.0 / math.sqrt(HEAD_DIM)

    @jax.checkpoint
    def attend(item):
        query_block, query_pos, query_doc = item
        scores = low_back(jnp.einsum('qhd,khd->hqk', query_block, keys, precision=HIGH) * factor)
        allowed = (positions[None, :] <= query_pos[:, None]) & (docs[None, :] == query_doc[:, None])
        scores = jnp.where(allowed[None], scores, MASKED)
        highest = lax.optimization_barrier(jnp.max(scores, axis=-1, keepdims=True))
        raised = jnp.exp(scores - highest)
        chances = raised / lax.optimization_barrier(jnp.sum(raised, axis=-1, keepdims=True))
        return jnp.einsum('hqk,khd->qhd', low(chances), values, precision=HIGH)
    mixed = lax.map(attend, (queries.reshape(-1, block, heads, HEAD_DIM), positions.reshape(-1, block), docs.reshape(-1, block)))
    mixed_low = low(low_back(mixed.reshape(length, width)))
    residual = inputs + low_back(matmul(mixed_low, w_out))
    ffn_in = low(rms_unit(residual) * ffn_gain)
    logits = low_back(matmul(ffn_in, w_router))
    chances = jax.nn.softmax(logits, axis=-1)
    gates = jnp.take_along_axis(chances, choose, axis=-1)
    picks = choose.reshape(-1)
    experts_all = w_router.shape[1]
    chosen = (picks[:, None] == jnp.arange(experts_all, dtype=jnp.int32)[None, :]).astype(jnp.int32)
    ranks = lax.optimization_barrier(jnp.sum((jnp.cumsum(chosen, axis=0) - 1) * chosen, axis=1))
    slots = N_SEQ * CAP
    target = picks * slots + ranks
    owners = jnp.arange(picks.shape[0], dtype=jnp.int32) // TOP
    source = jnp.zeros((experts_all * slots,), jnp.int32).at[target].set(owners)
    rows = low_back(ffn_in[source]).reshape(experts_all, slots, width)
    gate_act = low_back(jnp.einsum('end,edf->enf', rows, w_gate, precision=HIGH))
    up_act = low_back(jnp.einsum('end,edf->enf', rows, w_up, precision=HIGH))
    hidden = low(jax.nn.silu(gate_act) * up_act)
    expert_out = low(low_back(jnp.einsum('enf,efd->end', hidden, w_down, precision=HIGH)))
    picked = expert_out.reshape(experts_all * slots, width)[target].reshape(length, TOP, width)
    return residual + lax.optimization_barrier(jnp.sum(gates[..., None] * picked, axis=1))

def reference(tokens, segments, expert_ids, w_query, w_key, w_value, w_out, w_router, attn_gain, query_gain, key_gain, ffn_gain, w_gate, w_up, w_down, out_grad):
    params = tuple((item.astype(jnp.float32) for item in (w_query, w_key, w_value, w_out, w_router, attn_gain, query_gain, key_gain, ffn_gain, w_gate, w_up, w_down)))

    def step(totals, item):
        inputs, docs, choose, upstream = item

        def forward(weights, values):
            return sequence_forward(weights, values, docs, choose)
        result, pull = jax.vjp(forward, params, inputs.astype(jnp.float32))
        gradients, grad_input = pull(upstream.astype(jnp.float32))
        totals = jax.tree.map(jnp.add, totals, gradients)
        picks = choose.reshape(-1)
        counts = lax.optimization_barrier(jnp.sum((picks[:, None] == jnp.arange(EXPERTS, dtype=jnp.int32)[None, :]).astype(jnp.int32), axis=0))
        return (totals, (result.astype(jnp.bfloat16), grad_input, counts))
    start = tuple((jnp.zeros_like(item) for item in params))
    totals, (block_out, input_grad, counts) = lax.scan(step, start, (tokens, segments, expert_ids, out_grad))
    return (block_out, input_grad, totals[0], totals[1], totals[2], totals[3], totals[4], totals[5], totals[6], totals[7], totals[8], totals[9], totals[10], totals[11], counts)
```

```python
import functools
import math

import jax
import jax.numpy as jnp
from jax import lax
from jax.experimental import pallas as pl
from jax.experimental.pallas import tpu as pltpu
from jax.sharding import PartitionSpec as P

HEAD_DIM = 128
EPSILON = 1e-05
ROTARY_BASE = 10000.0
MASKED = -1e30
BF16 = jnp.bfloat16
F32 = jnp.float32
VMEM_BYTES = 60 * 1024 * 1024


def dot(left, right):
    return lax.dot_general(left, right, (((1,), (0,)), ((), ())), preferred_element_type=F32)


def dot_nt(left, right):
    return lax.dot_general(left, right, (((1,), (1,)), ((), ())), preferred_element_type=F32)


def dot_tn(left, right):
    return lax.dot_general(left, right, (((0,), (0,)), ((), ())), preferred_element_type=F32)


def norm_scale(values):
    return lax.rsqrt(jnp.mean(values * values, axis=-1, keepdims=True) + EPSILON)


def hop(values, axis, mask):
    size = lax.axis_size(axis)
    return lax.ppermute(values, axis, [(i, i ^ mask) for i in range(size)])


def masks_of(size):
    return [2 * m for m in range(size // 2)] + [2 * m + 1 for m in range(size // 2)]


def gather_seq(values):
    size = lax.axis_size("seq")
    near = [values] + [hop(values, "seq", 2 * m) for m in range(1, size // 2)]
    return near + [hop(piece, "seq", 1) for piece in near]


def scatter_seq(parts):
    chips = parts.shape[0] // 2
    both = parts[:chips].astype(F32) + hop(parts[chips:], "seq", 1).astype(F32)
    low = both.astype(BF16)
    total = both[0]
    for m in range(1, chips):
        total = total + hop(low[m], "seq", 2 * m).astype(F32)
    return total


def sum_seq(values, rows):
    size = lax.axis_size("seq")
    masks = masks_of(size)
    place = {mask: r for r, mask in enumerate(masks)}
    total = values
    for mask in range(1, size):
        moved = hop(values, "seq", mask)
        order = [place[masks[r] ^ mask] for r in range(size)]
        total = total + jnp.concatenate([moved[:, o * rows : (o + 1) * rows] for o in order], axis=1)
    return total


def gather_batch(values):
    pieces = [values]
    for t in range(1, lax.axis_size("batch")):
        pieces.append(hop(pieces[t - 1], "batch", 1) if t % 2 and t > 1 else hop(values, "batch", t))
    return pieces


def take_block(values, index):
    return lax.dynamic_index_in_dim(values, index, 0, keepdims=False)


def scatter_batch(blocks, me):
    size = blocks.shape[0]
    if size == 1:
        return blocks[0].astype(F32)
    theirs = jnp.stack([take_block(blocks, me ^ t ^ 1) for t in range(0, size, 2)])
    mine = jnp.stack([take_block(blocks, me ^ t) for t in range(0, size, 2)])
    pair = mine.astype(F32) + hop(theirs, "batch", 1).astype(F32)
    low = pair.astype(BF16)
    total = pair[0]
    for i in range(1, size // 2):
        total = total + hop(low[i], "batch", 2 * i).astype(F32)
    return total


def reorder_kernel(at_ref, *refs):
    *pieces, out_ref, sems = refs
    size = out_ref.shape[0]
    masks = masks_of(size)
    copies = []
    for t, piece in enumerate(pieces):
        for r, mask in enumerate(masks):
            copies.append(
                pltpu.make_async_copy(
                    piece.at[r], out_ref.at[at_ref[0] ^ mask, at_ref[1] ^ t], sems.at[t, r]
                )
            )
    for copy in copies:
        copy.start()
    for copy in copies:
        copy.wait()


def reorder(pieces, here):
    size, rows, columns = pieces[0].shape
    return pl.pallas_call(
        reorder_kernel,
        in_specs=[pl.BlockSpec(memory_space=pltpu.SMEM)]
        + [pl.BlockSpec(memory_space=pl.ANY)] * len(pieces),
        out_specs=pl.BlockSpec(memory_space=pl.ANY),
        out_shape=jax.ShapeDtypeStruct((size, len(pieces), rows, columns), pieces[0].dtype),
        scratch_shapes=[pltpu.SemaphoreType.DMA((len(pieces), size))],
        cost_estimate=pl.CostEstimate(
            flops=0, bytes_accessed=4 * size * len(pieces) * rows * columns, transcendentals=0
        ),
    )(here, *pieces)


def load_heads(place, refs, tables, blocks, rows, queries, keys, values):
    q_ref, k_ref, v_ref, scale_ref, gain_ref = refs
    cos_ref, sin_ref = tables
    for a in range(blocks):
        at = pl.ds(pl.multiple_of(place[a] * rows, rows), rows)
        to = slice(a * rows, (a + 1) * rows)
        cosine, sine = cos_ref[to, :], sin_ref[to, :]
        for i, (source, target) in enumerate(((q_ref, queries), (k_ref, keys))):
            normed = source[at, :] * scale_ref[at, i : i + 1] * gain_ref[i : i + 1, :]
            turned = pltpu.roll(normed, HEAD_DIM // 2, 1)
            target[to, :] = (normed * cosine + turned * sine).astype(BF16)
        values[to, :] = v_ref[at, :].astype(BF16)


def raised_scores(queries, keys, row_ref, col_ref, start, size, factor):
    stop = start + size
    scores = dot_nt(queries[start:stop, :], keys[:stop, :]) * factor
    query_at = lax.broadcasted_iota(jnp.int32, (size, stop), 0) + start
    key_at = lax.broadcasted_iota(jnp.int32, (size, stop), 1)
    allowed = (key_at <= query_at) & (row_ref[start:stop, :] == col_ref[:, :stop])
    scores = jnp.where(allowed, scores, MASKED)
    raised = jnp.exp(scores - jnp.max(scores, axis=-1, keepdims=True))
    return raised, jnp.sum(raised, axis=-1, keepdims=True)


def attend_kernel(
    blocks, size, place, q_ref, k_ref, v_ref, scale_ref, gain_ref, cos_ref, sin_ref, row_ref, col_ref,
    out_ref, queries, keys, values,
):
    total = q_ref.shape[0]
    rows = total // blocks
    refs, tables = (q_ref, k_ref, v_ref, scale_ref, gain_ref), (cos_ref, sin_ref)
    load_heads(place, refs, tables, blocks, rows, queries, keys, values)
    factor = 1.0 / math.sqrt(HEAD_DIM)
    for start in range(0, total, size):
        raised, sums = raised_scores(queries, keys, row_ref, col_ref, start, size, factor)
        mixed = dot(raised.astype(BF16), values[: start + size, :]) / sums
        for i in range(size // rows):
            at = pl.multiple_of(place[start // rows + i] * rows, rows)
            out_ref[pl.ds(at, rows), :] = mixed[i * rows : (i + 1) * rows].astype(BF16)


def attend_back_kernel(
    blocks, size, place, q_ref, k_ref, v_ref, scale_ref, gain_ref, cos_ref, sin_ref, row_ref, col_ref,
    grad_ref, gq_ref, gk_ref, gv_ref, inner_ref, gain_grad_ref, queries, keys, values, key_sum, value_sum,
):
    total = q_ref.shape[0]
    rows = total // blocks
    refs, tables = (q_ref, k_ref, v_ref, scale_ref, gain_ref), (cos_ref, sin_ref)
    load_heads(place, refs, tables, blocks, rows, queries, keys, values)
    factor = 1.0 / math.sqrt(HEAD_DIM)
    key_sum[...] = jnp.zeros_like(key_sum)
    value_sum[...] = jnp.zeros_like(value_sum)
    gain_rows = [jnp.zeros((1, HEAD_DIM), F32), jnp.zeros((1, HEAD_DIM), F32)]

    def finish(i, at, to, gradient, target):
        turned = pltpu.roll(gradient, HEAD_DIM // 2, 1)
        normed = gradient * cos_ref[to, :] - turned * sin_ref[to, :]
        unit = (q_ref, k_ref)[i][at, :] * scale_ref[at, i : i + 1]
        scaled = normed * gain_ref[i : i + 1, :]
        target[at, :] = scaled
        inner_ref[at, i : i + 1] += jnp.sum(scaled * unit, axis=-1, keepdims=True)
        gain_rows[i] += jnp.sum(normed * unit, axis=0, keepdims=True)

    @pl.when(pl.program_id(0) == 0)
    def _():
        inner_ref[...] = jnp.zeros_like(inner_ref)

    for start in range(0, total, size):
        stop = start + size
        raised, sums = raised_scores(queries, keys, row_ref, col_ref, start, size, factor)
        probs = raised * (1.0 / sums)
        pieces = []
        for i in range(size // rows):
            at = pl.multiple_of(place[start // rows + i] * rows, rows)
            pieces.append(grad_ref[pl.ds(at, rows), :])
        grad_mixed = jnp.concatenate(pieces, axis=0) if len(pieces) > 1 else pieces[0]
        grad_weights = dot_nt(grad_mixed, values[:stop, :])
        delta = jnp.sum(probs * grad_weights, axis=-1, keepdims=True)
        grad_scores = (probs * (grad_weights - delta)).astype(BF16)
        grad_queries = dot(grad_scores, keys[:stop, :]) * factor
        key_sum[:stop, :] += dot_tn(grad_scores, queries[start:stop, :])
        value_sum[:stop, :] += dot_tn(probs.astype(BF16), grad_mixed)
        for i in range(size // rows):
            at = pl.ds(pl.multiple_of(place[start // rows + i] * rows, rows), rows)
            to = slice(start + i * rows, start + (i + 1) * rows)
            finish(0, at, to, grad_queries[i * rows : (i + 1) * rows], gq_ref)
    for a in range(blocks):
        at = pl.ds(pl.multiple_of(place[a] * rows, rows), rows)
        to = slice(a * rows, (a + 1) * rows)
        finish(1, at, to, key_sum[to, :] * factor, gk_ref)
        gv_ref[at, :] = value_sum[to, :].astype(BF16)
    gain_grad_ref[0:1, :] = gain_rows[0]
    gain_grad_ref[1:2, :] = gain_rows[1]


def attention(place, qkv, scales, gains, tables, row_docs, col_docs, blocks, grad_mixed=None):
    total = qkv.shape[0]
    heads = qkv.shape[1] // (3 * HEAD_DIM)
    size = min(256, total)
    whole = lambda h: (0, 0)
    column = lambda h: (0, h)
    in_specs = [
        pl.BlockSpec(memory_space=pltpu.SMEM),
        pl.BlockSpec((total, HEAD_DIM), lambda h: (0, h)),
        pl.BlockSpec((total, HEAD_DIM), lambda h: (0, heads + h)),
        pl.BlockSpec((total, HEAD_DIM), lambda h: (0, 2 * heads + h)),
        pl.BlockSpec((total, 2), whole),
        pl.BlockSpec((2, HEAD_DIM), column),
        pl.BlockSpec((total, HEAD_DIM), whole),
        pl.BlockSpec((total, HEAD_DIM), whole),
        pl.BlockSpec((total, 1), whole),
        pl.BlockSpec((1, total), whole),
    ]
    operands = [place, qkv, qkv, qkv, scales, gains, *tables, row_docs, col_docs]
    held = [pltpu.VMEM((total, HEAD_DIM), BF16)] * 3
    params = pltpu.CompilerParams(vmem_limit_bytes=VMEM_BYTES)
    work = total * total * HEAD_DIM * heads
    if grad_mixed is None:
        return pl.pallas_call(
            functools.partial(attend_kernel, blocks, size),
            grid=(heads,),
            in_specs=in_specs,
            out_specs=pl.BlockSpec((total, HEAD_DIM), column),
            out_shape=jax.ShapeDtypeStruct((total, heads * HEAD_DIM), BF16),
            scratch_shapes=held,
            compiler_params=params,
            cost_estimate=pl.CostEstimate(
                flops=4 * work, bytes_accessed=qkv.size * 4, transcendentals=total * total
            ),
        )(*operands)
    return pl.pallas_call(
        functools.partial(attend_back_kernel, blocks, size),
        grid=(heads,),
        in_specs=in_specs + [pl.BlockSpec((total, HEAD_DIM), column)],
        out_specs=[pl.BlockSpec((total, HEAD_DIM), column)] * 3
        + [pl.BlockSpec((total, 2), whole), pl.BlockSpec((2, HEAD_DIM), column)],
        out_shape=[
            jax.ShapeDtypeStruct((total, heads * HEAD_DIM), F32),
            jax.ShapeDtypeStruct((total, heads * HEAD_DIM), F32),
            jax.ShapeDtypeStruct((total, heads * HEAD_DIM), BF16),
            jax.ShapeDtypeStruct((total, 2), F32),
            jax.ShapeDtypeStruct((2, heads * HEAD_DIM), F32),
        ],
        scratch_shapes=held + [pltpu.VMEM((total, HEAD_DIM), F32)] * 2,
        compiler_params=params,
        cost_estimate=pl.CostEstimate(
            flops=10 * work, bytes_accessed=qkv.size * 8, transcendentals=total * total
        ),
    )(*operands, grad_mixed)


def experts_kernel(
    experts, at_ref, x_ref, u_ref, gate_ref, wg_ref, wu_ref, wd_ref,
    out_ref, back_ref, hidden_ref, gate_grad_ref, up_grad_ref,
):
    owned = wg_ref.shape[0]
    rows, width = x_ref.shape
    inputs, upstream = x_ref[...], u_ref[...]
    extra = back_ref.shape[1] - width
    column = lax.broadcasted_iota(jnp.int32, (rows, extra), 1)
    sums = jnp.zeros((rows, extra), F32)
    for e in range(owned):
        gate_act = dot(inputs, wg_ref[e])
        up_act = dot(inputs, wu_ref[e])
        grad_raw = dot_nt(upstream, wd_ref[e])
        gate = gate_ref[:, e : e + 1]
        sigma = jax.nn.sigmoid(gate_act)
        active = gate_act * sigma
        hidden = active * up_act
        grad_gate = jnp.sum(hidden * grad_raw, axis=-1, keepdims=True)
        high = grad_gate.astype(BF16).astype(F32)
        expert = at_ref[0] * owned + e
        sums = jnp.where(column == expert, high, sums)
        sums = jnp.where(column == expert + experts, grad_gate - high, sums)
        grad_hidden = grad_raw * gate
        hidden_ref[e] = (hidden * gate).astype(BF16)
        gate_grad_ref[e] = (grad_hidden * up_act * sigma * (1.0 + gate_act * (1.0 - sigma))).astype(BF16)
        up_grad_ref[e] = (grad_hidden * active).astype(BF16)
    out = dot(hidden_ref[0], wd_ref[0])
    back = dot_nt(gate_grad_ref[0], wg_ref[0]) + dot_nt(up_grad_ref[0], wu_ref[0])
    for e in range(1, owned):
        out += dot(hidden_ref[e], wd_ref[e])
        back += dot_nt(gate_grad_ref[e], wg_ref[e]) + dot_nt(up_grad_ref[e], wu_ref[e])
    out_ref[...] = out.astype(BF16)
    back_ref[:, :width] = back.astype(BF16)
    back_ref[:, width:] = sums.astype(BF16)


def run_experts(at, inputs, upstream, gates, w_gate, w_up, w_down, experts, parts):
    total, width = inputs.shape
    owned, _, hidden = w_gate.shape
    piece = hidden // parts
    size = min(256, total)
    extra = 128 * -(-2 * experts // 128)
    token = lambda i, at: (i, 0)
    once = pl.Buffered(1)
    acts = jax.ShapeDtypeStruct((owned, total, piece), BF16)
    return pl.pallas_call(
        functools.partial(experts_kernel, experts),
        grid_spec=pltpu.PrefetchScalarGridSpec(
            num_scalar_prefetch=1,
            grid=(total // size,),
            in_specs=[
                pl.BlockSpec((size, width), token),
                pl.BlockSpec((size, width), token),
                pl.BlockSpec((size, owned), token),
                pl.BlockSpec((owned, width, piece), lambda i, at: (0, 0, at[1]), pipeline_mode=once),
                pl.BlockSpec((owned, width, piece), lambda i, at: (0, 0, at[1]), pipeline_mode=once),
                pl.BlockSpec((owned, piece, width), lambda i, at: (0, at[1], 0), pipeline_mode=once),
            ],
            out_specs=[
                pl.BlockSpec((size, width), token),
                pl.BlockSpec((size, width + extra), token),
            ]
            + [pl.BlockSpec((owned, size, piece), lambda i, at: (0, i, 0))] * 3,
        ),
        out_shape=[
            jax.ShapeDtypeStruct((total, width), BF16),
            jax.ShapeDtypeStruct((total, width + extra), BF16),
            acts,
            acts,
            acts,
        ],
        compiler_params=pltpu.CompilerParams(vmem_limit_bytes=VMEM_BYTES),
        cost_estimate=pl.CostEstimate(
            flops=12 * total * width * piece * owned,
            bytes_accessed=2 * (4 * total * width + 3 * owned * piece * (total + width)),
            transcendentals=total * piece * owned,
        ),
    )(at, inputs, upstream, gates, w_gate, w_up, w_down)


def on_device(
    tokens,
    segments,
    expert_ids,
    w_query,
    w_key,
    w_value,
    w_out,
    w_router,
    attn_gain,
    query_gain,
    key_gain,
    ffn_gain,
    w_gate,
    w_up,
    w_down,
    out_grad,
):
    seq_size, batch_size = lax.axis_size("seq"), lax.axis_size("batch")
    seq_at, batch_at = lax.axis_index("seq"), lax.axis_index("batch")
    parts = 2 if batch_size % 2 == 0 else 1
    half = batch_size // parts
    part_at = batch_at // half
    here = jnp.stack([seq_at, batch_at]).astype(jnp.int32)
    low_tokens = tokens[0]
    inputs = low_tokens.astype(F32)
    rows, width = inputs.shape
    total = rows * seq_size
    masks = masks_of(seq_size)
    order = seq_at ^ jnp.array(masks, jnp.int32)
    place = jnp.array([masks.index(m) for m in range(seq_size)], jnp.int32)[
        jnp.arange(seq_size, dtype=jnp.int32) ^ seq_at
    ]
    experts = w_router.shape[1]
    owned = w_gate.shape[0]
    wide = width // seq_size
    shard = w_query.shape[0]

    small = jnp.concatenate(
        [w_router] + [g[:, None] for g in (attn_gain, query_gain, key_gain, ffn_gain)], axis=1
    )
    small = jnp.stack([small] + [hop(small, "batch", t) for t in range(1, batch_size)])
    small = jnp.stack([small] + [hop(small, "seq", j) for j in range(1, seq_size)])
    small = small[
        (jnp.arange(seq_size) ^ seq_at)[:, None], (jnp.arange(batch_size) ^ batch_at)[None, :]
    ].reshape(width, experts + 4)
    router = small[:, :experts]
    gains = small[:, experts:].astype(F32).T
    attn_norm_gain, ffn_norm_gain = gains[0], gains[3]
    head_gains = lax.dynamic_slice_in_dim(gains[1:3], seq_at * wide, wide, 1)

    all_tokens = jnp.concatenate(gather_seq(low_tokens), axis=0)
    cut = jnp.concatenate(
        [w.reshape(shard, seq_size, wide).transpose(1, 0, 2) for w in (w_query, w_key, w_value)],
        axis=2,
    )
    moved = jnp.stack(
        [take_block(cut, seq_at)]
        + [hop(take_block(cut, seq_at ^ j), "seq", j) for j in masks[1:]]
    )
    w_heads = reorder(gather_batch(moved), here).reshape(width, 3 * wide)
    out_pieces = gather_batch(w_out)
    w_mix = jnp.stack(out_pieces)[jnp.arange(batch_size) ^ batch_at].reshape(wide, width)

    ids = expert_ids[0].T
    sets = [(out_grad[0], ids)]
    if parts == 2:
        sets.append((hop(out_grad[0], "batch", half), hop(ids, "batch", half)))
    upstreams = [jnp.concatenate(gather_seq(item[0]), axis=0) for item in sets]
    all_ids = [jnp.concatenate(gather_seq(item[1]), axis=1) for item in sets]
    mine = seq_at * owned + jnp.arange(owned, dtype=jnp.int32)
    selected = [jnp.any(item[:, :, None] == mine, axis=0) for item in all_ids]
    counts_here = jnp.sum(selected[0].astype(jnp.int32), axis=0)

    all_inputs = all_tokens.astype(F32)
    normed = (all_inputs * norm_scale(all_inputs) * attn_norm_gain).astype(BF16)
    qkv = dot(normed, w_heads)
    squares = jnp.stack(
        [jnp.sum(jnp.square(qkv[:, i * wide : (i + 1) * wide]), axis=1) for i in range(2)]
    )
    scales = lax.rsqrt(sum_seq(squares, rows) / width + EPSILON).T
    rates = jnp.power(
        ROTARY_BASE, -jnp.arange(HEAD_DIM // 2, dtype=F32) * (2.0 / HEAD_DIM)
    )
    angles = jnp.arange(total, dtype=F32)[:, None] * rates[None, :]
    cosine, sine = jnp.cos(angles), jnp.sin(angles)
    tables = (
        jnp.concatenate([cosine, cosine], axis=1),
        jnp.concatenate([-sine, sine], axis=1),
    )
    attend = functools.partial(
        attention,
        place,
        qkv,
        scales,
        head_gains,
        tables,
        segments[0][:, None],
        segments[0][None, :],
        seq_size,
    )
    mixed_low = attend()
    residual = inputs + scatter_seq(
        dot(mixed_low, w_mix).astype(BF16).reshape(seq_size, rows, width)
    )
    ffn_scale = norm_scale(residual)
    ffn_unit = residual * ffn_scale
    ffn_in = (ffn_unit * ffn_norm_gain).astype(BF16)

    shards = [ffn_in] + ([hop(ffn_in, "batch", half)] if parts == 2 else [])
    at = jnp.stack([seq_at, part_at]).astype(jnp.int32)
    results, all_ffn = [], []
    for values, upstream, chosen in zip(shards, upstreams, selected):
        gathered = jnp.concatenate(gather_seq(values), axis=0)
        chances_all = jax.nn.softmax(dot(gathered, router), axis=-1)
        gates = lax.dynamic_slice_in_dim(chances_all, seq_at * owned, owned, 1) * chosen
        all_ffn.append(gathered)
        results.append(
            run_experts(at, gathered, upstream, gates, w_gate, w_up, w_down, experts, parts)
        )
    back = scatter_seq(results[0][1].reshape(seq_size, rows, -1))
    if parts == 2:
        other = scatter_seq(results[1][1].reshape(seq_size, rows, -1))
        back = back + hop(other.astype(BF16), "batch", half).astype(F32)
    mix = scatter_seq(results[0][0].reshape(seq_size, rows, -1))
    if parts == 2:
        other = scatter_seq(results[1][0].reshape(seq_size, rows, -1))
        mix = mix + hop(other.astype(BF16), "batch", half).astype(F32)
    block_out = (residual + mix).astype(BF16)

    def over_tokens(equation, lefts, rights):
        terms = [
            jnp.einsum(equation, left, right, preferred_element_type=F32)
            for left, right in zip(lefts, rights)
        ]
        return sum(terms[1:], terms[0]).astype(BF16)

    down_term = over_tokens("etf,td->efd", [r[2] for r in results], upstreams)
    gate_term = over_tokens("td,etf->edf", all_ffn, [r[3] for r in results])
    up_term = over_tokens("td,etf->edf", all_ffn, [r[4] for r in results])

    def group_sum(blocks, lead):
        total = take_block(blocks, lead).astype(F32)
        for t in range(1, half):
            total = total + hop(take_block(blocks, lead ^ t), "batch", t).astype(F32)
        return total

    in_group = batch_at % half
    deep = down_term.shape[1] // half
    down_grad = group_sum(
        down_term.reshape(owned, half, deep, width).transpose(1, 0, 2, 3), in_group
    )

    def spread(term):
        deep = width // batch_size
        blocks = term.reshape(owned, parts, half, deep, -1).transpose(2, 1, 0, 3, 4)
        mine = group_sum(blocks, in_group)
        if parts == 1:
            return mine[0]
        keep = take_block(mine, part_at)
        other = hop(take_block(mine, 1 - part_at).astype(BF16), "batch", half).astype(F32)
        return jnp.where(
            part_at == 0,
            jnp.concatenate([keep, other], axis=-1),
            jnp.concatenate([other, keep], axis=-1),
        )

    gate_grad = spread(gate_term)
    up_grad = spread(up_term)

    grad_ffn_in = back[:, :width]
    choices = jnp.any(
        ids[:, :, None] == jnp.arange(experts, dtype=jnp.int32), axis=0
    )
    grad_chances = choices * (
        back[:, width : width + experts] + back[:, width + experts : width + 2 * experts]
    )
    chances = jax.nn.softmax(dot(ffn_in, router), axis=-1)
    grad_logits = (
        chances * (grad_chances - jnp.sum(chances * grad_chances, axis=-1, keepdims=True))
    ).astype(BF16)
    grad_ffn_in = grad_ffn_in + dot_nt(grad_logits, router)
    scaled = grad_ffn_in * ffn_norm_gain
    inner = jnp.mean(scaled * ffn_unit, axis=-1, keepdims=True)
    grad_residual = out_grad[0].astype(F32) + ffn_scale * (scaled - ffn_unit * inner)
    grad_attn = grad_residual.astype(BF16)

    router_term = jnp.concatenate(
        [dot_tn(ffn_in, grad_logits), jnp.sum(grad_ffn_in * ffn_unit, axis=0)[:, None]], axis=1
    ).reshape(seq_size, batch_size, shard, experts + 1)
    router_sum = take_block(router_term, seq_at)
    for j in range(1, seq_size):
        router_sum = router_sum + hop(take_block(router_term, seq_at ^ j), "seq", j)
    router_total = take_block(router_sum, batch_at)
    for t in range(1, batch_size):
        router_total = router_total + hop(take_block(router_sum, batch_at ^ t), "batch", t)
    router_grad, ffn_gain_grad = router_total[:, :experts], router_total[:, experts]

    all_grad = jnp.concatenate(gather_seq(grad_attn), axis=0)
    grad_mixed = dot_nt(all_grad, w_mix).astype(BF16)
    out_proj_grad = scatter_batch(
        dot_tn(mixed_low, all_grad).astype(BF16).reshape(batch_size, shard, width), batch_at
    )
    scaled_q, scaled_k, value_low, inner, gain_terms = attend(grad_mixed=grad_mixed)
    inner = sum_seq(inner.T, rows).T / width
    lows = []
    for i, item in enumerate((scaled_q, scaled_k)):
        scale = scales[:, i : i + 1]
        unit = qkv[:, i * wide : (i + 1) * wide] * scale
        lows.append((scale * (item - unit * inner[:, i : i + 1])).astype(BF16))
    low = jnp.concatenate(lows + [value_low], axis=1)
    grad_normed = scatter_seq(
        dot_nt(low, w_heads).astype(BF16).reshape(seq_size, rows, width)
    )
    heads_term = dot_tn(normed, low).astype(BF16)
    heads_term = heads_term.reshape(seq_size, batch_size, shard, 3 * wide).transpose(1, 0, 2, 3)
    heads_sum = scatter_batch(heads_term, batch_at).astype(BF16)
    pieces = [take_block(heads_sum, seq_at)] + [
        hop(take_block(heads_sum, seq_at ^ j), "seq", j) for j in masks[1:]
    ]
    heads_grad = jnp.stack(pieces)[place].astype(F32)
    query_grad, key_grad, value_grad = (
        heads_grad[:, :, i * wide : (i + 1) * wide].transpose(1, 0, 2).reshape(shard, width)
        for i in range(3)
    )
    gain_blocks = gain_terms.reshape(2, batch_size, shard).transpose(1, 0, 2)
    gain_sum = take_block(gain_blocks, batch_at)
    for t in range(1, batch_size):
        gain_sum = gain_sum + hop(take_block(gain_blocks, batch_at ^ t), "batch", t)

    attn_scale = norm_scale(inputs)
    attn_unit = inputs * attn_scale
    scaled = grad_normed * attn_norm_gain
    inner = jnp.mean(scaled * attn_unit, axis=-1, keepdims=True)
    grad_input = grad_residual + attn_scale * (scaled - attn_unit * inner)
    attn_gain_grad = (
        jnp.sum(
            query_grad * w_query.astype(F32)
            + key_grad * w_key.astype(F32)
            + value_grad * w_value.astype(F32),
            axis=1,
        )
        / attn_gain.astype(F32)
    )
    return (
        block_out[None],
        grad_input[None],
        query_grad,
        key_grad,
        value_grad,
        out_proj_grad,
        router_grad,
        attn_gain_grad,
        gain_sum[0],
        gain_sum[1],
        ffn_gain_grad,
        gate_grad,
        up_grad,
        down_grad,
        counts_here[None],
    )


def solution(mesh):
    in_specs = (
        P("batch", "seq", None),
        P("batch", None),
        P("batch", "seq", None),
        P(("seq", "batch"), None),
        P(("seq", "batch"), None),
        P(("seq", "batch"), None),
        P(("seq", "batch"), None),
        P(("seq", "batch"), None),
        P(("seq", "batch")),
        P(("seq", "batch")),
        P(("seq", "batch")),
        P(("seq", "batch")),
        P("seq", None, None),
        P("seq", None, None),
        P("seq", None, None),
        P("batch", "seq", None),
    )
    out_specs = (
        P("batch", "seq", None),
        P("batch", "seq", None),
        P(("seq", "batch"), None),
        P(("seq", "batch"), None),
        P(("seq", "batch"), None),
        P(("seq", "batch"), None),
        P(("seq", "batch"), None),
        P(("seq", "batch")),
        P(("seq", "batch")),
        P(("seq", "batch")),
        P(("seq", "batch")),
        P("seq", "batch", None),
        P("seq", "batch", None),
        P("seq", "batch", None),
        P("batch", "seq"),
    )
    return jax.shard_map(
        on_device, mesh=mesh, in_specs=in_specs, out_specs=out_specs, check_vma=False
    )
```

```python
import functools
import math

import jax
import jax.numpy as jnp
from jax import lax
from jax.experimental import pallas as pl
from jax.experimental.pallas import tpu as pltpu
from jax.sharding import PartitionSpec as P

HEAD_DIM = 128
EPSILON = 1e-05
ROTARY_BASE = 10000.0
MASKED = -1e30
BF16 = jnp.bfloat16
F32 = jnp.float32
VMEM_BYTES = 60 * 1024 * 1024


def dot(left, right):
    return lax.dot_general(left, right, (((1,), (0,)), ((), ())), preferred_element_type=F32)


def dot_nt(left, right):
    return lax.dot_general(left, right, (((1,), (1,)), ((), ())), preferred_element_type=F32)


def dot_tn(left, right):
    return lax.dot_general(left, right, (((0,), (0,)), ((), ())), preferred_element_type=F32)


def norm_scale(values):
    return lax.rsqrt(jnp.mean(values * values, axis=-1, keepdims=True) + EPSILON)


def hop(values, axis, mask):
    size = lax.axis_size(axis)
    return lax.ppermute(values, axis, [(i, i ^ mask) for i in range(size)])


def take_block(values, index, axis=0):
    return lax.dynamic_index_in_dim(values, index, axis, keepdims=False)


def put(buffer, values, starts):
    return lax.dynamic_update_slice(buffer, values, starts)


def after(values, *earlier):
    return lax.optimization_barrier((values, *earlier))[0]


def masks_of(size):
    return [2 * m for m in range(size // 2)] + [2 * m + 1 for m in range(size // 2)]


def gather_near(values):
    return [values] + [hop(values, "seq", 2 * m) for m in range(1, lax.axis_size("seq") // 2)]


def gather_seq(values):
    near = gather_near(values)
    return near + [hop(piece, "seq", 1) for piece in near]


def scatter_seq(near, far):
    chips = lax.axis_size("seq") // 2
    rows = near.shape[0] // chips
    moved = hop(far, "seq", 1)

    def both(m):
        at = slice(m * rows, (m + 1) * rows)
        return near[at].astype(F32) + moved[at].astype(F32)

    sent = [both(m).astype(BF16) for m in range(1, chips)]
    total = both(0)
    for m in range(1, chips):
        total = total + hop(sent[m - 1], "seq", 2 * m).astype(F32)
    return total, sent


def gather_batch(values):
    pieces = [values]
    for t in range(1, lax.axis_size("batch")):
        pieces.append(hop(pieces[t - 1], "batch", 1) if t % 2 and t > 1 else hop(values, "batch", t))
    return pieces


def scatter_batch(blocks, me, kind, *pins):
    size = blocks.shape[0]
    if size == 1:
        return blocks[0].astype(F32)
    theirs = jnp.stack([take_block(blocks, me ^ t ^ 1) for t in range(0, size, 2)])
    moved = after(hop(theirs, "batch", 1), pins[0])
    total = take_block(blocks, me).astype(F32) + moved[0].astype(F32)
    for i in range(1, size // 2):
        pair = take_block(blocks, me ^ (2 * i)).astype(F32) + moved[i].astype(F32)
        total = total + after(hop(pair.astype(kind), "batch", 2 * i), pins[1]).astype(F32)
    return total


def piece_copies(refs, block, per, buffer, slot, sems, first):
    rows = buffer.shape[1] // per
    return [
        pltpu.make_async_copy(
            refs[block * per + i],
            buffer.at[slot, pl.ds(i * rows, rows), :],
            sems.at[slot, first + i],
        )
        for i in range(per)
    ]


def stream(blocks, copies_of):
    step = pl.program_id(0)
    for block in range(blocks):

        @pl.when(step == block)
        def _():
            if block == 0:
                for copy in copies_of(0):
                    copy.start()
            if block + 1 < blocks:
                for copy in copies_of(block + 1):
                    copy.start()
            for copy in copies_of(block):
                copy.wait()


def weight_copies(at_ref, pieces, target, sems):
    return [
        pltpu.make_async_copy(piece, target.at[:, at_ref[1] ^ t], sems.at[t])
        for t, piece in enumerate(pieces)
    ]


def project_pairs_kernel(blocks, per, at_ref, *refs):
    count = blocks * per
    pieces, w_pieces = refs[:count], refs[count : -8]
    gain_ref, normed_ref, pair_ref, square_ref, weight_ref, buffer, sems, w_sems = refs[-8:]
    step = pl.program_id(0)

    @pl.when(step == 0)
    def _():
        for copy in weight_copies(at_ref, w_pieces, weight_ref, w_sems):
            copy.start()

    stream(blocks, lambda block: piece_copies(pieces, block, per, buffer, block % 2, sems, 0))

    @pl.when(step == 0)
    def _():
        for copy in weight_copies(at_ref, w_pieces, weight_ref, w_sems):
            copy.wait()

    values = buffer[step % 2].astype(F32)
    normed = (values * norm_scale(values) * gain_ref[...]).astype(BF16)
    normed_ref[...] = normed
    width = normed.shape[1]
    pair = dot(normed, weight_ref[...].reshape(width, -1))
    pair_ref[...] = pair
    wide = pair.shape[1] // 2
    squared = pair * pair
    high = squared.astype(BF16)
    low = (squared - high.astype(F32)).astype(BF16)
    lane = lax.broadcasted_iota(jnp.int32, (8, 2 * wide), 1)
    line = lax.broadcasted_iota(jnp.int32, (8, 2 * wide), 0)
    pick = (lane // wide == line).astype(BF16)
    sums = (dot_nt(pick, high) + dot_nt(pick, low))[:2]
    rows = normed.shape[0] // per
    for i in range(per):
        at = pl.multiple_of(at_ref[2 + step * per + i] * rows, rows)
        square_ref[:, pl.ds(at, rows)] = sums[:, i * rows : (i + 1) * rows]


def project_pairs(here, pieces, w_pieces, gain):
    rows, width = pieces[0].shape
    seq_size, shard, columns = w_pieces[0].shape
    batch_size = len(w_pieces)
    per = max(1, 256 // rows)
    blocks = len(pieces) // per
    total, size = rows * len(pieces), rows * per
    return pl.pallas_call(
        functools.partial(project_pairs_kernel, blocks, per),
        grid_spec=pltpu.PrefetchScalarGridSpec(
            num_scalar_prefetch=1,
            grid=(blocks,),
            in_specs=[pl.BlockSpec(memory_space=pl.ANY)] * (len(pieces) + batch_size)
            + [pl.BlockSpec((1, width), lambda i, at: (0, 0))],
            out_specs=[
                pl.BlockSpec((size, width), lambda i, at: (i, 0)),
                pl.BlockSpec((size, columns), lambda i, at: (i, 0)),
                pl.BlockSpec((2, total), lambda i, at: (0, 0)),
                pl.BlockSpec((seq_size, batch_size, shard, columns), lambda i, at: (0, 0, 0, 0)),
            ],
            scratch_shapes=[
                pltpu.VMEM((2, size, width), BF16),
                pltpu.SemaphoreType.DMA((2, per)),
                pltpu.SemaphoreType.DMA((batch_size,)),
            ],
        ),
        out_shape=[
            jax.ShapeDtypeStruct((total, width), BF16),
            jax.ShapeDtypeStruct((total, columns), F32),
            jax.ShapeDtypeStruct((2, total), F32),
            jax.ShapeDtypeStruct((seq_size, batch_size, shard, columns), BF16),
        ],
        compiler_params=pltpu.CompilerParams(vmem_limit_bytes=VMEM_BYTES),
        cost_estimate=pl.CostEstimate(
            flops=2 * total * width * columns, bytes_accessed=8 * total * width, transcendentals=0
        ),
    )(here, *pieces, *w_pieces, gain)


def project_values_kernel(at_ref, normed_ref, *refs):
    *w_pieces, value_ref, weight_ref, w_sems = refs

    @pl.when(pl.program_id(0) == 0)
    def _():
        copies = weight_copies(at_ref, w_pieces, weight_ref, w_sems)
        for copy in copies:
            copy.start()
        for copy in copies:
            copy.wait()

    width = normed_ref.shape[1]
    value_ref[...] = dot(normed_ref[...], weight_ref[...].reshape(width, -1)).astype(BF16)


def project_values(here, normed, w_pieces):
    total, width = normed.shape
    seq_size, shard, columns = w_pieces[0].shape
    batch_size = len(w_pieces)
    size = min(512, total)
    return pl.pallas_call(
        project_values_kernel,
        grid_spec=pltpu.PrefetchScalarGridSpec(
            num_scalar_prefetch=1,
            grid=(total // size,),
            in_specs=[pl.BlockSpec((size, width), lambda i, at: (i, 0))]
            + [pl.BlockSpec(memory_space=pl.ANY)] * batch_size,
            out_specs=[
                pl.BlockSpec((size, columns), lambda i, at: (i, 0)),
                pl.BlockSpec((seq_size, batch_size, shard, columns), lambda i, at: (0, 0, 0, 0)),
            ],
            scratch_shapes=[pltpu.SemaphoreType.DMA((batch_size,))],
        ),
        out_shape=[
            jax.ShapeDtypeStruct((total, columns), BF16),
            jax.ShapeDtypeStruct((seq_size, batch_size, shard, columns), BF16),
        ],
        compiler_params=pltpu.CompilerParams(vmem_limit_bytes=VMEM_BYTES),
        cost_estimate=pl.CostEstimate(
            flops=2 * total * width * columns, bytes_accessed=2 * total * width, transcendentals=0
        ),
    )(here, normed, *w_pieces)


def mix_back_kernel(blocks, per, *refs):
    pieces = refs[: blocks * per]
    mixed_ref, weight_ref, back_ref, grad_ref, buffer, total, sems = refs[blocks * per :]
    step = pl.program_id(0)
    stream(blocks, lambda block: piece_copies(pieces, block, per, buffer, block % 2, sems, 0))
    gradient = buffer[step % 2]
    back_ref[...] = dot_nt(gradient, weight_ref[...]).astype(BF16)
    term = dot_tn(mixed_ref[...], gradient)

    @pl.when(step == 0)
    def _():
        total[...] = term

    @pl.when(step > 0)
    def _():
        total[...] += term

    @pl.when(step == blocks - 1)
    def _():
        grad_ref[...] = total[...].astype(BF16)


def mix_back(pieces, mixed, weight):
    rows, width = pieces[0].shape
    wide = weight.shape[0]
    per = max(1, 256 // rows)
    blocks = len(pieces) // per
    total, size = rows * len(pieces), rows * per
    return pl.pallas_call(
        functools.partial(mix_back_kernel, blocks, per),
        grid=(blocks,),
        in_specs=[pl.BlockSpec(memory_space=pl.ANY)] * len(pieces)
        + [
            pl.BlockSpec((size, wide), lambda i: (i, 0)),
            pl.BlockSpec((wide, width), lambda i: (0, 0)),
        ],
        out_specs=[
            pl.BlockSpec((size, wide), lambda i: (i, 0)),
            pl.BlockSpec((wide, width), lambda i: (0, 0)),
        ],
        out_shape=[
            jax.ShapeDtypeStruct((total, wide), BF16),
            jax.ShapeDtypeStruct((wide, width), BF16),
        ],
        scratch_shapes=[
            pltpu.VMEM((2, size, width), BF16),
            pltpu.VMEM((wide, width), F32),
            pltpu.SemaphoreType.DMA((2, per)),
        ],
        compiler_params=pltpu.CompilerParams(vmem_limit_bytes=VMEM_BYTES),
        cost_estimate=pl.CostEstimate(
            flops=4 * total * width * wide, bytes_accessed=4 * total * width, transcendentals=0
        ),
    )(*pieces, mixed, weight)


def load_heads(place, blocks, refs, tables, queries, keys, values):
    q_ref, k_ref, v_ref, scale_ref, gain_ref = refs
    cos_ref, sin_ref = tables
    rows = q_ref.shape[0] // blocks
    for a in range(blocks):
        at = pl.ds(pl.multiple_of(place[a] * rows, rows), rows)
        to = slice(a * rows, (a + 1) * rows)
        for i, (source, target) in enumerate(((q_ref, queries), (k_ref, keys))):
            normed = source[at, :] * scale_ref[to, i : i + 1] * gain_ref[i : i + 1, :]
            turned = pltpu.roll(normed, HEAD_DIM // 2, 1)
            target[to, :] = (normed * cos_ref[to, :] + turned * sin_ref[to, :]).astype(BF16)
        values[to, :] = v_ref[at, :]


def raised_scores(queries, keys, row_ref, col_ref, start, size, factor):
    stop = start + size
    scores = dot_nt(queries[start:stop, :], keys[:stop, :]) * factor
    query_at = lax.broadcasted_iota(jnp.int32, (size, stop), 0) + start
    key_at = lax.broadcasted_iota(jnp.int32, (size, stop), 1)
    allowed = (key_at <= query_at) & (row_ref[start:stop, :] == col_ref[:, :stop])
    scores = jnp.where(allowed, scores, MASKED)
    raised = jnp.exp(scores - jnp.max(scores, axis=-1, keepdims=True))
    return raised, jnp.sum(raised, axis=-1, keepdims=True)


def attend_kernel(
    blocks, size, place, q_ref, k_ref, v_ref, scale_ref, gain_ref, cos_ref, sin_ref, row_ref, col_ref,
    out_ref, queries, keys, values,
):
    total = q_ref.shape[0]
    rows = total // blocks
    refs, tables = (q_ref, k_ref, v_ref, scale_ref, gain_ref), (cos_ref, sin_ref)
    load_heads(place, blocks, refs, tables, queries, keys, values)
    factor = 1.0 / math.sqrt(HEAD_DIM)
    for start in range(0, total, size):
        raised, sums = raised_scores(queries, keys, row_ref, col_ref, start, size, factor)
        mixed = dot(raised.astype(BF16), values[: start + size, :]) / sums
        for i in range(size // rows):
            at = pl.multiple_of(place[start // rows + i] * rows, rows)
            out_ref[pl.ds(at, rows), :] = mixed[i * rows : (i + 1) * rows].astype(BF16)


def attend_back_kernel(
    blocks, size, place, q_ref, k_ref, v_ref, scale_ref, gain_ref, cos_ref, sin_ref, row_ref, col_ref,
    grad_ref, gq_ref, gk_ref, gv_ref, inner_ref, gain_grad_ref, queries, keys, values, key_sum, value_sum,
):
    total = q_ref.shape[0]
    rows = total // blocks
    refs, tables = (q_ref, k_ref, v_ref, scale_ref, gain_ref), (cos_ref, sin_ref)
    load_heads(place, blocks, refs, tables, queries, keys, values)
    factor = 1.0 / math.sqrt(HEAD_DIM)
    key_sum[...] = jnp.zeros_like(key_sum)
    value_sum[...] = jnp.zeros_like(value_sum)
    gain_rows = [jnp.zeros((1, HEAD_DIM), F32), jnp.zeros((1, HEAD_DIM), F32)]

    def finish(i, a, gradient, target):
        at = pl.ds(pl.multiple_of(place[a] * rows, rows), rows)
        to = slice(a * rows, (a + 1) * rows)
        turned = pltpu.roll(gradient, HEAD_DIM // 2, 1)
        normed = gradient * cos_ref[to, :] - turned * sin_ref[to, :]
        unit = (q_ref, k_ref)[i][at, :] * scale_ref[to, i : i + 1]
        scaled = normed * gain_ref[i : i + 1, :]
        target[at, :] = scaled
        inner_ref[to, i : i + 1] += jnp.sum(scaled * unit, axis=-1, keepdims=True)
        gain_rows[i] += jnp.sum(normed * unit, axis=0, keepdims=True)

    @pl.when(pl.program_id(0) == 0)
    def _():
        inner_ref[...] = jnp.zeros_like(inner_ref)

    for start in range(0, total, size):
        stop = start + size
        raised, sums = raised_scores(queries, keys, row_ref, col_ref, start, size, factor)
        probs = raised * (1.0 / sums)
        pieces = []
        for i in range(size // rows):
            at = pl.multiple_of(place[start // rows + i] * rows, rows)
            pieces.append(grad_ref[pl.ds(at, rows), :])
        grad_mixed = jnp.concatenate(pieces, axis=0) if len(pieces) > 1 else pieces[0]
        grad_weights = dot_nt(grad_mixed, values[:stop, :])
        delta = jnp.sum(probs * grad_weights, axis=-1, keepdims=True)
        grad_scores = (probs * (grad_weights - delta)).astype(BF16)
        grad_queries = dot(grad_scores, keys[:stop, :]) * factor
        key_sum[:stop, :] += dot_tn(grad_scores, queries[start:stop, :])
        value_sum[:stop, :] += dot_tn(probs.astype(BF16), grad_mixed)
        for i in range(size // rows):
            finish(0, start // rows + i, grad_queries[i * rows : (i + 1) * rows], gq_ref)
    for a in range(blocks):
        to = slice(a * rows, (a + 1) * rows)
        finish(1, a, key_sum[to, :] * factor, gk_ref)
        gv_ref[pl.ds(pl.multiple_of(place[a] * rows, rows), rows), :] = value_sum[to, :].astype(BF16)
    gain_grad_ref[0:1, :] = gain_rows[0]
    gain_grad_ref[1:2, :] = gain_rows[1]


def attention(place, pairs, values, scales, gains, tables, row_docs, col_docs, grad_mixed=None):
    total = pairs.shape[0]
    blocks = place.shape[0]
    heads = values.shape[1] // HEAD_DIM
    size = max(256, total // blocks)
    whole = lambda h: (0, 0)
    column = lambda h: (0, h)
    in_specs = [
        pl.BlockSpec(memory_space=pltpu.SMEM),
        pl.BlockSpec((total, HEAD_DIM), lambda h: (0, h)),
        pl.BlockSpec((total, HEAD_DIM), lambda h: (0, heads + h)),
        pl.BlockSpec((total, HEAD_DIM), column),
        pl.BlockSpec((total, 2), whole),
        pl.BlockSpec((2, HEAD_DIM), column),
        pl.BlockSpec((total, HEAD_DIM), whole),
        pl.BlockSpec((total, HEAD_DIM), whole),
        pl.BlockSpec((total, 1), whole),
        pl.BlockSpec((1, total), whole),
    ]
    operands = [place, pairs, pairs, values, scales, gains, *tables, row_docs, col_docs]
    held = [pltpu.VMEM((total, HEAD_DIM), BF16)] * 3
    params = pltpu.CompilerParams(vmem_limit_bytes=VMEM_BYTES)
    work = total * total * HEAD_DIM * heads
    if grad_mixed is None:
        return pl.pallas_call(
            functools.partial(attend_kernel, blocks, size),
            grid=(heads,),
            in_specs=in_specs,
            out_specs=pl.BlockSpec((total, HEAD_DIM), column),
            out_shape=jax.ShapeDtypeStruct((total, heads * HEAD_DIM), BF16),
            scratch_shapes=held,
            compiler_params=params,
            cost_estimate=pl.CostEstimate(
                flops=4 * work, bytes_accessed=pairs.size * 8, transcendentals=total * total
            ),
        )(*operands)
    return pl.pallas_call(
        functools.partial(attend_back_kernel, blocks, size),
        grid=(heads,),
        in_specs=in_specs + [pl.BlockSpec((total, HEAD_DIM), column)],
        out_specs=[pl.BlockSpec((total, HEAD_DIM), column)] * 3
        + [pl.BlockSpec((total, 2), whole), pl.BlockSpec((2, HEAD_DIM), column)],
        out_shape=[
            jax.ShapeDtypeStruct((total, heads * HEAD_DIM), F32),
            jax.ShapeDtypeStruct((total, heads * HEAD_DIM), F32),
            jax.ShapeDtypeStruct((total, heads * HEAD_DIM), BF16),
            jax.ShapeDtypeStruct((total, 2), F32),
            jax.ShapeDtypeStruct((2, heads * HEAD_DIM), F32),
        ],
        scratch_shapes=held + [pltpu.VMEM((total, HEAD_DIM), F32)] * 2,
        compiler_params=params,
        cost_estimate=pl.CostEstimate(
            flops=10 * work, bytes_accessed=pairs.size * 16, transcendentals=total * total
        ),
    )(*operands, grad_mixed)


def router_chances(inputs, router, experts):
    logits = dot(inputs, router)
    column = lax.broadcasted_iota(jnp.int32, logits.shape, 1)
    logits = jnp.where(column < experts, logits, MASKED)
    raised = jnp.exp(logits - jnp.max(logits, axis=-1, keepdims=True))
    return raised / jnp.sum(raised, axis=-1, keepdims=True)


def acts_kernel(experts, blocks, per, k, at_ref, *refs):
    count = blocks * per
    pieces = refs[:count]
    (
        side_ref, router_ref, wg_ref, wu_ref, wd_ref,
        x_out, u_out, hidden_ref, gate_grad_ref, up_grad_ref, sums_ref, x_buffer, u_buffer, sems,
    ) = refs[count:]
    step = pl.program_id(0)
    sides = [side_ref.at[at_ref[2 + r], k] for r in range(count)]

    def copies_of(block):
        slot = block % 2
        return piece_copies(pieces, block, per, x_buffer, slot, sems, 0) + piece_copies(
            sides, block, per, u_buffer, slot, sems, per
        )

    stream(blocks, copies_of)
    owned, width, _ = wg_ref.shape
    inputs, upstream = x_buffer[step % 2], u_buffer[step % 2, :, :width]
    chosen = u_buffer[step % 2, :, width:].astype(F32)
    x_out[...] = inputs
    u_out[...] = upstream
    gates = router_chances(inputs, router_ref[...], experts) * chosen
    gate_at = lax.broadcasted_iota(jnp.int32, gates.shape, 1)
    column = lax.broadcasted_iota(jnp.int32, sums_ref.shape, 1)
    sums = jnp.zeros(sums_ref.shape, F32)
    for e in range(owned):
        gate_act = dot(inputs, wg_ref[e])
        up_act = dot(inputs, wu_ref[e])
        grad_raw = dot_nt(upstream, wd_ref[e])
        expert = at_ref[0] * owned + e
        gate = jnp.sum(jnp.where(gate_at == expert, gates, 0.0), axis=-1, keepdims=True)
        sigma = jax.nn.sigmoid(gate_act)
        active = gate_act * sigma
        hidden = active * up_act
        grad_gate = jnp.sum(hidden * grad_raw, axis=-1, keepdims=True)
        high = grad_gate.astype(BF16).astype(F32)
        sums = jnp.where(column == expert, high, sums)
        sums = jnp.where(column == expert + experts, grad_gate - high, sums)
        grad_hidden = grad_raw * gate
        hidden_ref[e] = (hidden * gate).astype(BF16)
        gate_grad_ref[e] = (grad_hidden * up_act * sigma * (1.0 + gate_act * (1.0 - sigma))).astype(BF16)
        up_grad_ref[e] = (grad_hidden * active).astype(BF16)
    sums_ref[...] = sums.astype(BF16)


def run_acts(at, pieces, sides, k, router, w_gate, w_up, w_down, experts, parts):
    rows, width = pieces[0].shape
    total = rows * len(pieces)
    owned, _, hidden = w_gate.shape
    piece = hidden // parts
    per = max(1, 256 // rows)
    blocks, size = len(pieces) // per, rows * per
    extra = 128 * -(-2 * experts // 128)
    lanes = router.shape[1]
    token = lambda i, at: (i, 0)
    once = pl.Buffered(1)
    acts = jax.ShapeDtypeStruct((owned, total, piece), BF16)
    act_spec = pl.BlockSpec((owned, size, piece), lambda i, at: (0, i, 0))
    return pl.pallas_call(
        functools.partial(acts_kernel, experts, blocks, per, k),
        grid_spec=pltpu.PrefetchScalarGridSpec(
            num_scalar_prefetch=1,
            grid=(blocks,),
            in_specs=[pl.BlockSpec(memory_space=pl.ANY)] * (len(pieces) + 1)
            + [
                pl.BlockSpec((width, lanes), lambda i, at: (0, 0), pipeline_mode=once),
                pl.BlockSpec((owned, width, piece), lambda i, at: (0, 0, at[1]), pipeline_mode=once),
                pl.BlockSpec((owned, width, piece), lambda i, at: (0, 0, at[1]), pipeline_mode=once),
                pl.BlockSpec((owned, piece, width), lambda i, at: (0, at[1], 0), pipeline_mode=once),
            ],
            out_specs=[pl.BlockSpec((size, width), token)] * 2
            + [act_spec] * 3
            + [pl.BlockSpec((size, extra), token)],
            scratch_shapes=[
                pltpu.VMEM((2, size, width), BF16),
                pltpu.VMEM((2, size, width + lanes), BF16),
                pltpu.SemaphoreType.DMA((2, 2 * per)),
            ],
        ),
        out_shape=[
            jax.ShapeDtypeStruct((total, width), BF16),
            jax.ShapeDtypeStruct((total, width), BF16),
            acts,
            acts,
            acts,
            jax.ShapeDtypeStruct((total, extra), BF16),
        ],
        compiler_params=pltpu.CompilerParams(vmem_limit_bytes=VMEM_BYTES),
        cost_estimate=pl.CostEstimate(
            flops=6 * total * width * piece * owned,
            bytes_accessed=2 * (4 * total * width + 3 * owned * piece * (total + width)),
            transcendentals=total * piece * owned,
        ),
    )(at, *pieces, sides, router, w_gate, w_up, w_down)


def split_store(values, near_ref, far_ref):
    middle = pl.num_programs(0) // 2

    @pl.when(pl.program_id(0) < middle)
    def _():
        near_ref[...] = values

    @pl.when(pl.program_id(0) >= middle)
    def _():
        far_ref[...] = values


def rows_back_kernel(at_ref, gate_ref, up_ref, sums_ref, wg_ref, wu_ref, near_ref, far_ref):
    back = dot_nt(gate_ref[0], wg_ref[0]) + dot_nt(up_ref[0], wu_ref[0])
    for e in range(1, wg_ref.shape[0]):
        back += dot_nt(gate_ref[e], wg_ref[e]) + dot_nt(up_ref[e], wu_ref[e])
    split_store(jnp.concatenate([back.astype(BF16), sums_ref[...]], axis=1), near_ref, far_ref)


def rows_out_kernel(sets, blocks, per, at_ref, *refs):
    *hidden_refs, wd_ref, out_ref = refs
    step = pl.program_id(0)
    rows = out_ref.shape[4]
    for k, hidden_ref in enumerate(hidden_refs):

        @pl.when(step // blocks == k)
        def _():
            out = dot(hidden_ref[0], wd_ref[0])
            for e in range(1, wd_ref.shape[0]):
                out += dot(hidden_ref[e], wd_ref[e])
            for i in range(per):
                at = at_ref[2 + (step - k * blocks) * per + i] // 2 % per
                out_ref[0, at, 0, 0] = out[i * rows : (i + 1) * rows].astype(BF16)


def run_out(at, hiddens, w_down, rows):
    owned, total, piece = hiddens[0].shape
    sets, width = len(hiddens), w_down.shape[2]
    seq_size = total // rows
    per = max(1, 256 // rows)
    size, blocks = rows * per, seq_size // per

    def hidden_at(k):
        return lambda i, at: (0, jnp.clip(i - k * blocks, 0, blocks - 1), 0)

    def out_at(i, at):
        first = at[2 + (i % blocks) * per]
        return (first // (2 * per), 0, first % 2, i // blocks, 0, 0)

    out = pl.pallas_call(
        functools.partial(rows_out_kernel, sets, blocks, per),
        grid_spec=pltpu.PrefetchScalarGridSpec(
            num_scalar_prefetch=1,
            grid=(sets * blocks,),
            in_specs=[pl.BlockSpec((owned, size, piece), hidden_at(k)) for k in range(sets)]
            + [
                pl.BlockSpec(
                    (owned, piece, width), lambda i, at: (0, at[1], 0), pipeline_mode=pl.Buffered(1)
                )
            ],
            out_specs=pl.BlockSpec((1, per, 1, 1, rows, width), out_at),
        ),
        out_shape=jax.ShapeDtypeStruct((seq_size // (2 * per), per, 2, sets, rows, width), BF16),
        compiler_params=pltpu.CompilerParams(vmem_limit_bytes=VMEM_BYTES),
        cost_estimate=pl.CostEstimate(
            flops=2 * sets * total * width * piece * owned,
            bytes_accessed=2 * sets * total * (width + owned * piece),
            transcendentals=0,
        ),
    )(at, *hiddens, w_down)
    return out.reshape(seq_size, sets, rows, width)


def run_back(at, gates, ups, sums, w_gate, w_up):
    owned, total, piece = gates.shape
    size = min(256, total // 2)
    middle = total // (2 * size)
    width, extra = w_gate.shape[1], sums.shape[1]
    act_spec = pl.BlockSpec((owned, size, piece), lambda i, at: (0, i, 0))
    weight_spec = pl.BlockSpec(
        (owned, width, piece), lambda i, at: (0, 0, at[1]), pipeline_mode=pl.Buffered(1)
    )
    out = jax.ShapeDtypeStruct((total // 2, width + extra), BF16)
    return pl.pallas_call(
        rows_back_kernel,
        grid_spec=pltpu.PrefetchScalarGridSpec(
            num_scalar_prefetch=1,
            grid=(total // size,),
            in_specs=[act_spec] * 2
            + [pl.BlockSpec((size, extra), lambda i, at: (i, 0))]
            + [weight_spec] * 2,
            out_specs=[
                pl.BlockSpec((size, width + extra), lambda i, at: (jnp.minimum(i, middle - 1), 0)),
                pl.BlockSpec((size, width + extra), lambda i, at: (jnp.maximum(i - middle, 0), 0)),
            ],
        ),
        out_shape=[out, out],
        compiler_params=pltpu.CompilerParams(vmem_limit_bytes=VMEM_BYTES),
        cost_estimate=pl.CostEstimate(
            flops=4 * total * width * piece * owned,
            bytes_accessed=2 * (total * width + 2 * owned * piece * (total + width)),
            transcendentals=0,
        ),
    )(at, gates, ups, sums, w_gate, w_up)


def down_kernel(sets, at_ref, *refs):
    out_ref = refs[-1]
    for e in range(out_ref.shape[1]):
        term = dot_tn(refs[0][e], refs[sets][...])
        for i in range(1, sets):
            term += dot_tn(refs[i][e], refs[sets + i][...])
        out_ref[0, e] = term.astype(BF16)


def down_blocks(targets, hiddens, upstreams, group, width):
    owned, total, piece = hiddens[0].shape
    deep = piece // group
    sets, count = len(hiddens), targets.shape[0]
    wide = min(512, width)
    return pl.pallas_call(
        functools.partial(down_kernel, sets),
        grid_spec=pltpu.PrefetchScalarGridSpec(
            num_scalar_prefetch=1,
            grid=(count, width // wide),
            in_specs=[pl.BlockSpec((owned, total, deep), lambda g, j, at: (0, 0, at[g]))] * sets
            + [pl.BlockSpec((total, wide), lambda g, j, at: (0, j))] * sets,
            out_specs=pl.BlockSpec((1, owned, deep, wide), lambda g, j, at: (g, 0, 0, j)),
        ),
        out_shape=jax.ShapeDtypeStruct((count, owned, deep, width), BF16),
        compiler_params=pltpu.CompilerParams(vmem_limit_bytes=VMEM_BYTES),
        cost_estimate=pl.CostEstimate(
            flops=2 * sets * count * owned * total * deep * width,
            bytes_accessed=2 * sets * total * (width + owned * deep),
            transcendentals=0,
        ),
    )(targets, *hiddens, *upstreams)


def in_kernel(sets, at_ref, *refs):
    out_ref = refs[-1]
    for e in range(out_ref.shape[2]):
        term = dot_tn(refs[0][...], refs[sets][e])
        for i in range(1, sets):
            term += dot_tn(refs[i][...], refs[sets + i][e])
        out_ref[0, 0, e] = term.astype(BF16)


def in_blocks(targets, inputs, acts, group, parts):
    owned, total, piece = acts[0].shape
    width = inputs[0].shape[1]
    deep = width // (group * parts)
    sets, count = len(inputs), targets.shape[0]
    held = pl.BlockSpec((owned, total, piece), lambda g, p, at: (0, 0, 0), pipeline_mode=pl.Buffered(1))
    return pl.pallas_call(
        functools.partial(in_kernel, sets),
        grid_spec=pltpu.PrefetchScalarGridSpec(
            num_scalar_prefetch=1,
            grid=(count, parts),
            in_specs=[pl.BlockSpec((total, deep), lambda g, p, at: (0, p * group + at[g]))] * sets
            + [held] * sets,
            out_specs=pl.BlockSpec((1, 1, owned, deep, piece), lambda g, p, at: (g, p, 0, 0, 0)),
        ),
        out_shape=jax.ShapeDtypeStruct((count, parts, owned, deep, piece), BF16),
        compiler_params=pltpu.CompilerParams(vmem_limit_bytes=VMEM_BYTES),
        cost_estimate=pl.CostEstimate(
            flops=2 * sets * count * parts * owned * total * deep * piece,
            bytes_accessed=4 * sets * owned * total * piece,
            transcendentals=0,
        ),
    )(targets, *inputs, *acts)


def on_device(
    tokens,
    segments,
    expert_ids,
    w_query,
    w_key,
    w_value,
    w_out,
    w_router,
    attn_gain,
    query_gain,
    key_gain,
    ffn_gain,
    w_gate,
    w_up,
    w_down,
    out_grad,
):
    seq_size, batch_size = lax.axis_size("seq"), lax.axis_size("batch")
    seq_at, batch_at = lax.axis_index("seq"), lax.axis_index("batch")
    parts = 2 if batch_size % 2 == 0 else 1
    half = batch_size // parts
    part_at, in_group = batch_at // half, batch_at % half
    low_tokens = tokens[0]
    inputs = low_tokens.astype(F32)
    rows, width = inputs.shape
    total = rows * seq_size
    experts = w_router.shape[1]
    owned = w_gate.shape[0]
    wide = width // seq_size
    shard = w_query.shape[0]

    masks = masks_of(seq_size)
    order = seq_at ^ jnp.array(masks, jnp.int32)
    place = jnp.array([masks.index(m) for m in range(seq_size)], jnp.int32)[
        jnp.arange(seq_size, dtype=jnp.int32) ^ seq_at
    ]

    def reordered(values, by):
        return values.reshape(-1, seq_size, rows)[:, by].reshape(values.shape)

    masks = masks_of(seq_size)
    order = seq_at ^ jnp.array(masks, jnp.int32)
    place = jnp.array([masks.index(m) for m in range(seq_size)], jnp.int32)[
        jnp.arange(seq_size, dtype=jnp.int32) ^ seq_at
    ]
    here = jnp.concatenate([jnp.stack([seq_at, batch_at]).astype(jnp.int32), order])

    def reordered(values, by):
        return values.reshape(-1, seq_size, rows)[:, by].reshape(values.shape)

    masks = masks_of(seq_size)
    order = seq_at ^ jnp.array(masks, jnp.int32)
    place = jnp.array([masks.index(m) for m in range(seq_size)], jnp.int32)[
        jnp.arange(seq_size, dtype=jnp.int32) ^ seq_at
    ]
    here = jnp.concatenate([jnp.stack([seq_at, batch_at]).astype(jnp.int32), order])
    at = jnp.concatenate([jnp.stack([seq_at, part_at]).astype(jnp.int32), order])

    def reordered(values, by):
        return values.reshape(-1, seq_size, rows)[:, by].reshape(values.shape)

    near_tokens = gather_near(low_tokens)

    def columns_of(*weights):
        cut = [w.reshape(shard, seq_size, wide).transpose(1, 0, 2) for w in weights]
        return lax.all_to_all(jnp.concatenate(cut, axis=2), "seq", split_axis=0, concat_axis=0, tiled=True)

    pair_cut = columns_of(w_query, w_key)

    lanes = 128 * -(-(experts + 4) // 128)
    gains = jnp.stack([attn_gain, query_gain, key_gain, ffn_gain], axis=1)
    small = jnp.zeros((shard, lanes), BF16)
    small = put(put(small, w_router, (0, 0)), gains, (0, experts))
    small = lax.all_gather(small, "batch", axis=0, tiled=True)
    router = lax.all_gather(small, "seq", axis=0, tiled=True)
    gains = router[:, experts : experts + 4].astype(F32).T
    attn_norm_gain, ffn_norm_gain = gains[0], gains[3]
    head_gains = lax.dynamic_slice_in_dim(gains[1:3], seq_at * wide, wide, 1)

    pair_pieces = gather_batch(after(pair_cut, router))
    value_cut = columns_of(after(w_value, pair_cut))
    value_pieces = gather_batch(after(value_cut, *pair_pieces[2:3]))
    token_pieces = near_tokens + [hop(piece, "seq", 1) for piece in near_tokens]
    w_mix = jnp.zeros((batch_size, shard, width), BF16)
    for t, piece in enumerate(gather_batch(after(w_out, *value_pieces[2:3]))):
        w_mix = put(w_mix, piece[None], (batch_at ^ t, 0, 0))
    w_mix = w_mix.reshape(wide, width)

    ids = expert_ids[0]
    choices = jnp.any(ids[:, :, None] == jnp.arange(lanes, dtype=jnp.int32), axis=1)
    side = jnp.concatenate([out_grad[0], choices.astype(BF16)], axis=1)
    sides = jnp.stack([side] + ([hop(side, "batch", half)] if parts == 2 else []))
    sides = lax.all_gather(after(sides, *near_tokens), "seq", axis=0)
    counts = jnp.sum(sides[:, 0, :, width:].astype(F32), axis=(0, 1)).astype(jnp.int32)
    counts_here = lax.dynamic_slice_in_dim(counts, seq_at * owned, owned, 0)

    normed, pairs, squares, pair_weights = project_pairs(
        here, token_pieces, pair_pieces, attn_norm_gain[None]
    )
    values, value_weights = project_values(here, normed, value_pieces)
    pair_weights, value_weights = (w.reshape(width, -1) for w in (pair_weights, value_weights))

    def sum_seq(values):
        return jnp.sum(lax.all_gather(values, "seq", axis=0), axis=0)

    scales = lax.rsqrt(sum_seq(squares) / width + EPSILON)
    rates = jnp.power(
        ROTARY_BASE, -jnp.arange(HEAD_DIM // 2, dtype=F32) * (2.0 / HEAD_DIM)
    )
    angles = jnp.arange(total, dtype=F32)[:, None] * rates[None, :]
    cosine, sine = jnp.cos(angles), jnp.sin(angles)
    tables = (
        jnp.concatenate([cosine, cosine], axis=1),
        jnp.concatenate([-sine, sine], axis=1),
    )
    attend = functools.partial(
        attention,
        place,
        pairs,
        values,
        scales.T,
        head_gains,
        tables,
        segments[0][:, None],
        segments[0][None, :],
    )
    mixed_low = attend()
    middle = total // 2
    far = dot(mixed_low[middle:], w_mix).astype(BF16)
    residual = inputs + scatter_seq(dot(mixed_low[:middle], w_mix).astype(BF16), far)[0]
    ffn_scale = norm_scale(residual)
    ffn_unit = residual * ffn_scale
    ffn_in = (ffn_unit * ffn_norm_gain).astype(BF16)

    def acts_of(k, pieces):
        return run_acts(at, pieces, sides, k, router, w_gate, w_up, w_down, experts, parts)

    ffn_pieces = gather_seq(ffn_in)
    results = [acts_of(0, ffn_pieces)]
    if parts == 2:
        partner = hop(ffn_in, "batch", half)
        near = gather_near(after(partner, *ffn_pieces))
        near = [after(piece, results[0][0]) for piece in near]
        results.append(acts_of(1, near + [hop(piece, "seq", 1) for piece in near]))
    all_ffn, upstreams, hiddens, gate_acts, up_acts, sums = zip(*results)
    own = in_group[None].astype(jnp.int32)
    others = jnp.stack([in_group ^ t for t in range(1, half)]).astype(jnp.int32) if half > 1 else None
    down = functools.partial(down_blocks, hiddens=hiddens, upstreams=upstreams, group=half, width=width)
    into = functools.partial(in_blocks, inputs=all_ffn, group=half, parts=parts)

    def send_group(theirs):
        return [hop(theirs[t - 1], "batch", t) for t in range(1, half)]

    def group_sum(mine, moved):
        total = mine[0].astype(F32)
        for item in moved:
            total = total + item.astype(F32)
        return total

    def swap_part(summed):
        return hop(take_block(summed, 1 - part_at).astype(BF16), "batch", half)

    gate_moved = up_moved = down_moved = ()
    at_back = at
    if half > 1:
        gate_theirs = into(others, acts=gate_acts)
        gate_moved = send_group(gate_theirs)
        at_back = after(at, gate_theirs)
    backs, sent = [], []
    for k in reversed(range(parts)):
        pair = run_back(at_back, gate_acts[k], up_acts[k], sums[k], w_gate, w_up)
        summed, low = scatter_seq(*pair)
        backs.insert(0, summed)
        sent += low
        at_back = after(at, *pair)
    back = backs[0]
    if parts == 2:
        back = back + hop(backs[1].astype(BF16), "batch", half).astype(F32)

    grad_ffn_in = back[:, :width]
    grad_chances = choices[:, :experts] * (
        back[:, width : width + experts] + back[:, width + experts : width + 2 * experts]
    )
    chances = router_chances(ffn_in, router, experts)[:, :experts]
    grad_logits = (
        chances * (grad_chances - jnp.sum(chances * grad_chances, axis=-1, keepdims=True))
    ).astype(BF16)
    grad_ffn_in = grad_ffn_in + dot_nt(grad_logits, router[:, :experts])
    scaled = grad_ffn_in * ffn_norm_gain
    inner = jnp.mean(scaled * ffn_unit, axis=-1, keepdims=True)
    grad_residual = out_grad[0].astype(F32) + ffn_scale * (scaled - ffn_unit * inner)
    grad_attn = grad_residual.astype(BF16)

    later = own
    if half > 1:
        up_theirs = into(after(others, *sent), acts=up_acts)
        down_theirs = down(after(others, up_theirs))
        up_moved = send_group(after(up_theirs, grad_attn))
        later = after(own, down_theirs)
    mix = run_out(after(at, *sent, later), hiddens, w_down, rows)
    later = after(later, mix)
    gate_mine = into(later, acts=gate_acts)
    up_mine = into(later, acts=up_acts)
    down_mine = down(later)
    gate_sum = group_sum(gate_mine, [after(item, grad_attn) for item in gate_moved])
    gate_other = swap_part(gate_sum) if parts == 2 else None
    mix = lax.psum_scatter(mix, "seq", scatter_dimension=0)

    grad_pieces = gather_seq(grad_attn)
    grad_mixed, out_term = mix_back(grad_pieces, mixed_low, w_mix)
    scaled_q, scaled_k, value_low, inner, gain_terms = attend(grad_mixed=grad_mixed)
    inner = reordered(sum_seq(inner.T), order).T / width
    rel_scales = reordered(scales, order).T
    lows = []
    for i, item in enumerate((scaled_q, scaled_k)):
        scale = rel_scales[:, i : i + 1]
        unit = pairs[:, i * wide : (i + 1) * wide] * scale
        lows.append((scale * (item - unit * inner[:, i : i + 1])).astype(BF16))
    pair_low = jnp.concatenate(lows, axis=1)

    def rows_of(at):
        return (dot_nt(pair_low[at], pair_weights) + dot_nt(value_low[at], value_weights)).astype(BF16)

    far = rows_of(slice(middle, total))
    grad_normed, sent = scatter_seq(rows_of(slice(0, middle)), far)

    def head_sums(values):
        term = dot_tn(normed, values).astype(BF16).reshape(seq_size * batch_size, shard, -1)
        term = lax.all_to_all(term, ("seq", "batch"), split_axis=0, concat_axis=0, tiled=True)
        term = after(term, grad_normed).reshape(seq_size, batch_size, shard, -1)
        return jnp.sum(term.astype(F32), axis=1)

    value_sums = head_sums(value_low)
    pair_sums = head_sums(after(pair_low, far))
    query_grad, key_grad, value_grad = (
        item.transpose(1, 0, 2).reshape(shard, width)
        for item in (pair_sums[:, :, :wide], pair_sums[:, :, wide:], value_sums)
    )

    def spread(summed, other):
        if parts == 1:
            return summed[0]
        keep, other = take_block(summed, part_at), after(other, grad_normed).astype(F32)
        return jnp.where(
            part_at == 0,
            jnp.concatenate([keep, other], axis=-1),
            jnp.concatenate([other, keep], axis=-1),
        )

    up_sum = group_sum(up_mine, [after(item, value_low) for item in up_moved])
    up_other = swap_part(up_sum) if parts == 2 else None
    if half > 1:
        down_moved = [
            after(item, grad_normed) for item in send_group(after(down_theirs, value_low, *up_moved))
        ]
    down_grad = group_sum(down_mine, down_moved)
    gate_grad = spread(gate_sum, gate_other)
    up_grad = spread(up_sum, up_other)
    out_proj_grad = scatter_batch(
        out_term.reshape(batch_size, shard, width), batch_at, BF16, value_low, grad_normed
    )
    gain_blocks = gain_terms.reshape(2, batch_size, shard).transpose(1, 0, 2)
    gain_sum = scatter_batch(gain_blocks, batch_at, F32, pair_low, grad_normed)

    mine = mix[0].astype(F32)
    if parts == 2:
        mine = mine + after(hop(after(mix[1], value_low), "batch", half), grad_normed).astype(F32)
    block_out = (residual + mine).astype(BF16)

    router_term = jnp.concatenate(
        [dot_tn(grad_logits, ffn_in), jnp.sum(grad_ffn_in * ffn_unit, axis=0)[None]], axis=0
    )
    router_term = router_term.reshape(experts + 1, seq_size * batch_size, shard).transpose(1, 0, 2)
    router_sum = lax.all_to_all(router_term, ("seq", "batch"), split_axis=0, concat_axis=0, tiled=True)
    router_sum = jnp.sum(after(router_sum, value_low), axis=0)
    router_grad, ffn_gain_grad = router_sum[:experts].T, router_sum[experts]

    attn_scale = norm_scale(inputs)
    attn_unit = inputs * attn_scale
    scaled = grad_normed * attn_norm_gain
    inner = jnp.mean(scaled * attn_unit, axis=-1, keepdims=True)
    grad_input = grad_residual + attn_scale * (scaled - attn_unit * inner)
    attn_gain_grad = (
        jnp.sum(
            query_grad * w_query.astype(F32)
            + key_grad * w_key.astype(F32)
            + value_grad * w_value.astype(F32),
            axis=1,
        )
        / attn_gain.astype(F32)
    )
    return (
        block_out[None],
        grad_input[None],
        query_grad,
        key_grad,
        value_grad,
        out_proj_grad,
        router_grad,
        attn_gain_grad,
        gain_sum[0],
        gain_sum[1],
        ffn_gain_grad,
        gate_grad,
        up_grad,
        down_grad,
        counts_here[None],
    )


def solution(mesh):
    in_specs = (
        P("batch", "seq", None),
        P("batch", None),
        P("batch", "seq", None),
        P(("seq", "batch"), None),
        P(("seq", "batch"), None),
        P(("seq", "batch"), None),
        P(("seq", "batch"), None),
        P(("seq", "batch"), None),
        P(("seq", "batch")),
        P(("seq", "batch")),
        P(("seq", "batch")),
        P(("seq", "batch")),
        P("seq", None, None),
        P("seq", None, None),
        P("seq", None, None),
        P("batch", "seq", None),
    )
    out_specs = (
        P("batch", "seq", None),
        P("batch", "seq", None),
        P(("seq", "batch"), None),
        P(("seq", "batch"), None),
        P(("seq", "batch"), None),
        P(("seq", "batch"), None),
        P(("seq", "batch"), None),
        P(("seq", "batch")),
        P(("seq", "batch")),
        P(("seq", "batch")),
        P(("seq", "batch")),
        P("seq", "batch", None),
        P("seq", "batch", None),
        P("seq", "batch", None),
        P("batch", "seq"),
    )
    return jax.shard_map(
        on_device, mesh=mesh, in_specs=in_specs, out_specs=out_specs, check_vma=False
    )
```

```python
import functools
import math

import jax
import jax.numpy as jnp
from jax import lax
from jax.experimental import pallas as pl
from jax.experimental.pallas import tpu as pltpu
from jax.sharding import PartitionSpec as P

HEAD_DIM = 128
EPSILON = 1e-05
ROTARY_BASE = 10000.0
MASKED = -1e30
BF16 = jnp.bfloat16
F32 = jnp.float32
VMEM_BYTES = 60 * 1024 * 1024


def dot(left, right):
    return lax.dot_general(left, right, (((1,), (0,)), ((), ())), preferred_element_type=F32)


def dot_nt(left, right):
    return lax.dot_general(left, right, (((1,), (1,)), ((), ())), preferred_element_type=F32)


def dot_tn(left, right):
    return lax.dot_general(left, right, (((0,), (0,)), ((), ())), preferred_element_type=F32)


def norm_scale(values):
    return lax.rsqrt(jnp.mean(values * values, axis=-1, keepdims=True) + EPSILON)


def hop(values, axis, mask):
    size = lax.axis_size(axis)
    return lax.ppermute(values, axis, [(i, i ^ mask) for i in range(size)])


def take_block(values, index, axis=0):
    return lax.dynamic_index_in_dim(values, index, axis, keepdims=False)


def put(buffer, values, starts):
    return lax.dynamic_update_slice(buffer, values, starts)


def after(values, *earlier):
    return lax.optimization_barrier((values, *earlier))[0]


def masks_of(size):
    return [2 * m for m in range(size // 2)] + [2 * m + 1 for m in range(size // 2)]


def gather_near(values):
    return [values] + [hop(values, "seq", 2 * m) for m in range(1, lax.axis_size("seq") // 2)]


def gather_seq(values):
    near = gather_near(values)
    near[0] = after(values, *near[1:2])
    return near + [hop(piece, "seq", 1) for piece in near]


def scatter_seq(near, far):
    chips = lax.axis_size("seq") // 2
    rows = near.shape[0] // chips
    moved = hop(far, "seq", 1)

    def both(m):
        at = slice(m * rows, (m + 1) * rows)
        return near[at].astype(F32) + moved[at].astype(F32)

    sent = [both(m).astype(BF16) for m in range(1, chips)]
    total = both(0)
    for m in range(1, chips):
        total = total + hop(sent[m - 1], "seq", 2 * m).astype(F32)
    return total, sent


def scatter_chips(near, far):
    size = lax.axis_size("seq")
    sent = (near.astype(F32) + hop(far, "seq", 1).astype(F32)).astype(BF16)
    groups = [list(range(core, size, 2)) for core in range(2)]
    moved = lax.all_to_all(
        sent, "seq", split_axis=0, concat_axis=0, axis_index_groups=groups, tiled=True
    )
    return jnp.sum(moved.astype(F32), axis=0), sent


def gather_batch(values, *pins):
    pieces = [values]
    for t in range(1, lax.axis_size("batch")):
        if t % 2 and t > 1:
            pieces.append(hop(after(pieces[t - 1], *pieces[1 : t - 1], *pins), "batch", 1))
        else:
            pieces.append(hop(values, "batch", t))
    return pieces


def scatter_batch(blocks, me, kind, *pins):
    size = blocks.shape[0]
    if size == 1:
        return blocks[0].astype(F32)
    theirs = jnp.stack([take_block(blocks, me ^ t ^ 1) for t in range(0, size, 2)])
    moved = after(hop(theirs, "batch", 1), pins[0])
    total = take_block(blocks, me).astype(F32) + moved[0].astype(F32)
    for i in range(1, size // 2):
        pair = take_block(blocks, me ^ (2 * i)).astype(F32) + moved[i].astype(F32)
        total = total + after(hop(pair.astype(kind), "batch", 2 * i), pins[1]).astype(F32)
    return total


def piece_copies(refs, block, per, buffer, slot, sems, first):
    rows = buffer.shape[1] // per
    return [
        pltpu.make_async_copy(
            refs[block * per + i],
            buffer.at[slot, pl.ds(i * rows, rows), :],
            sems.at[slot, first + i],
        )
        for i in range(per)
    ]


def stream(blocks, copies_of):
    step = pl.program_id(0)
    for block in range(blocks):

        @pl.when(step == block)
        def _():
            if block == 0:
                for copy in copies_of(0):
                    copy.start()
            if block + 1 < blocks:
                for copy in copies_of(block + 1):
                    copy.start()
            for copy in copies_of(block):
                copy.wait()


def weight_copies(at_ref, pieces, target, sems):
    shard = target.shape[2]
    return [
        pltpu.make_async_copy(piece.at[:, pl.ds(0, shard)], target.at[:, at_ref[1] ^ t], sems.at[t])
        for t, piece in enumerate(pieces)
    ]


def project_pairs_kernel(blocks, per, at_ref, *refs):
    count = blocks * per
    pieces, w_pieces = refs[:count], refs[count : -8]
    gain_ref, normed_ref, pair_ref, square_ref, weight_ref, buffer, sems, w_sems = refs[-8:]
    step = pl.program_id(0)

    @pl.when(step == 0)
    def _():
        for copy in weight_copies(at_ref, w_pieces, weight_ref, w_sems):
            copy.start()

    stream(blocks, lambda block: piece_copies(pieces, block, per, buffer, block % 2, sems, 0))

    @pl.when(step == 0)
    def _():
        for copy in weight_copies(at_ref, w_pieces, weight_ref, w_sems):
            copy.wait()

    values = buffer[step % 2].astype(F32)
    normed = (values * norm_scale(values) * gain_ref[...]).astype(BF16)
    normed_ref[...] = normed
    width = normed.shape[1]
    pair = dot(normed, weight_ref[...].reshape(width, -1))
    pair_ref[...] = pair
    wide = pair.shape[1] // 2
    squared = pair * pair
    high = squared.astype(BF16)
    low = (squared - high.astype(F32)).astype(BF16)
    lane = lax.broadcasted_iota(jnp.int32, (8, 2 * wide), 1)
    line = lax.broadcasted_iota(jnp.int32, (8, 2 * wide), 0)
    pick = (lane // wide == line).astype(BF16)
    sums = (dot_nt(pick, high) + dot_nt(pick, low))[:2]
    rows = normed.shape[0] // per
    for i in range(per):
        at = pl.multiple_of(at_ref[2 + step * per + i] * rows, rows)
        square_ref[:, pl.ds(at, rows)] = sums[:, i * rows : (i + 1) * rows]


def project_pairs(here, pieces, w_pieces, shard, gain):
    rows, width = pieces[0].shape
    seq_size, _, columns = w_pieces[0].shape
    batch_size = len(w_pieces)
    per = max(1, 256 // rows)
    blocks = len(pieces) // per
    total, size = rows * len(pieces), rows * per
    return pl.pallas_call(
        functools.partial(project_pairs_kernel, blocks, per),
        grid_spec=pltpu.PrefetchScalarGridSpec(
            num_scalar_prefetch=1,
            grid=(blocks,),
            in_specs=[pl.BlockSpec(memory_space=pl.ANY)] * (len(pieces) + batch_size)
            + [pl.BlockSpec((1, width), lambda i, at: (0, 0))],
            out_specs=[
                pl.BlockSpec((size, width), lambda i, at: (i, 0)),
                pl.BlockSpec((size, columns), lambda i, at: (i, 0)),
                pl.BlockSpec((2, total), lambda i, at: (0, 0)),
                pl.BlockSpec((seq_size, batch_size, shard, columns), lambda i, at: (0, 0, 0, 0)),
            ],
            scratch_shapes=[
                pltpu.VMEM((2, size, width), BF16),
                pltpu.SemaphoreType.DMA((2, per)),
                pltpu.SemaphoreType.DMA((batch_size,)),
            ],
        ),
        out_shape=[
            jax.ShapeDtypeStruct((total, width), BF16),
            jax.ShapeDtypeStruct((total, columns), F32),
            jax.ShapeDtypeStruct((2, total), F32),
            jax.ShapeDtypeStruct((seq_size, batch_size, shard, columns), BF16),
        ],
        compiler_params=pltpu.CompilerParams(vmem_limit_bytes=VMEM_BYTES),
        cost_estimate=pl.CostEstimate(
            flops=2 * total * width * columns, bytes_accessed=8 * total * width, transcendentals=0
        ),
    )(here, *pieces, *w_pieces, gain)


def project_values_kernel(at_ref, normed_ref, *refs):
    *w_pieces, value_ref, weight_ref, w_sems = refs

    @pl.when(pl.program_id(0) == 0)
    def _():
        copies = weight_copies(at_ref, w_pieces, weight_ref, w_sems)
        for copy in copies:
            copy.start()
        for copy in copies:
            copy.wait()

    width = normed_ref.shape[1]
    value_ref[...] = dot(normed_ref[...], weight_ref[...].reshape(width, -1)).astype(BF16)


def project_values(here, normed, w_pieces):
    total, width = normed.shape
    seq_size, shard, columns = w_pieces[0].shape
    batch_size = len(w_pieces)
    size = min(512, total)
    return pl.pallas_call(
        project_values_kernel,
        grid_spec=pltpu.PrefetchScalarGridSpec(
            num_scalar_prefetch=1,
            grid=(total // size,),
            in_specs=[pl.BlockSpec((size, width), lambda i, at: (i, 0))]
            + [pl.BlockSpec(memory_space=pl.ANY)] * batch_size,
            out_specs=[
                pl.BlockSpec((size, columns), lambda i, at: (i, 0)),
                pl.BlockSpec((seq_size, batch_size, shard, columns), lambda i, at: (0, 0, 0, 0)),
            ],
            scratch_shapes=[pltpu.SemaphoreType.DMA((batch_size,))],
        ),
        out_shape=[
            jax.ShapeDtypeStruct((total, columns), BF16),
            jax.ShapeDtypeStruct((seq_size, batch_size, shard, columns), BF16),
        ],
        compiler_params=pltpu.CompilerParams(vmem_limit_bytes=VMEM_BYTES),
        cost_estimate=pl.CostEstimate(
            flops=2 * total * width * columns, bytes_accessed=2 * total * width, transcendentals=0
        ),
    )(here, normed, *w_pieces)


def mix_back_kernel(blocks, per, *refs):
    pieces = refs[: blocks * per]
    mixed_ref, weight_ref, back_ref, grad_ref, buffer, total, sems = refs[blocks * per :]
    step = pl.program_id(0)
    stream(blocks, lambda block: piece_copies(pieces, block, per, buffer, block % 2, sems, 0))
    gradient = buffer[step % 2]
    back_ref[...] = dot_nt(gradient, weight_ref[...]).astype(BF16)
    term = dot_tn(mixed_ref[...], gradient)

    @pl.when(step == 0)
    def _():
        total[...] = term

    @pl.when(step > 0)
    def _():
        total[...] += term

    @pl.when(step == blocks - 1)
    def _():
        grad_ref[...] = total[...].astype(BF16)


def mix_back(pieces, mixed, weight):
    rows, width = pieces[0].shape
    wide = weight.shape[0]
    per = max(1, 256 // rows)
    blocks = len(pieces) // per
    total, size = rows * len(pieces), rows * per
    return pl.pallas_call(
        functools.partial(mix_back_kernel, blocks, per),
        grid=(blocks,),
        in_specs=[pl.BlockSpec(memory_space=pl.ANY)] * len(pieces)
        + [
            pl.BlockSpec((size, wide), lambda i: (i, 0)),
            pl.BlockSpec((wide, width), lambda i: (0, 0)),
        ],
        out_specs=[
            pl.BlockSpec((size, wide), lambda i: (i, 0)),
            pl.BlockSpec((wide, width), lambda i: (0, 0)),
        ],
        out_shape=[
            jax.ShapeDtypeStruct((total, wide), BF16),
            jax.ShapeDtypeStruct((wide, width), BF16),
        ],
        scratch_shapes=[
            pltpu.VMEM((2, size, width), BF16),
            pltpu.VMEM((wide, width), F32),
            pltpu.SemaphoreType.DMA((2, per)),
        ],
        compiler_params=pltpu.CompilerParams(vmem_limit_bytes=VMEM_BYTES),
        cost_estimate=pl.CostEstimate(
            flops=4 * total * width * wide, bytes_accessed=4 * total * width, transcendentals=0
        ),
    )(*pieces, mixed, weight)


def load_heads(place, blocks, refs, tables, queries, keys, values):
    q_ref, k_ref, v_ref, scale_ref, gain_ref = refs
    cos_ref, sin_ref = tables
    rows = q_ref.shape[0] // blocks
    for a in range(blocks):
        at = pl.ds(pl.multiple_of(place[a] * rows, rows), rows)
        to = slice(a * rows, (a + 1) * rows)
        for i, (source, target) in enumerate(((q_ref, queries), (k_ref, keys))):
            normed = source[at, :] * scale_ref[to, i : i + 1] * gain_ref[i : i + 1, :]
            turned = pltpu.roll(normed, HEAD_DIM // 2, 1)
            target[to, :] = (normed * cos_ref[to, :] + turned * sin_ref[to, :]).astype(BF16)
        values[to, :] = v_ref[at, :]


def raised_scores(queries, keys, row_ref, col_ref, start, size, factor):
    stop = start + size
    scores = dot_nt(queries[start:stop, :], keys[:stop, :]) * factor
    query_at = lax.broadcasted_iota(jnp.int32, (size, stop), 0) + start
    key_at = lax.broadcasted_iota(jnp.int32, (size, stop), 1)
    allowed = (key_at <= query_at) & (row_ref[start:stop, :] == col_ref[:, :stop])
    scores = jnp.where(allowed, scores, MASKED)
    raised = jnp.exp(scores - jnp.max(scores, axis=-1, keepdims=True))
    return raised, jnp.sum(raised, axis=-1, keepdims=True)


def attend_kernel(
    blocks, size, place, q_ref, k_ref, v_ref, scale_ref, gain_ref, cos_ref, sin_ref, row_ref, col_ref,
    out_ref, queries, keys, values,
):
    total = q_ref.shape[0]
    rows = total // blocks
    refs, tables = (q_ref, k_ref, v_ref, scale_ref, gain_ref), (cos_ref, sin_ref)
    load_heads(place, blocks, refs, tables, queries, keys, values)
    factor = 1.0 / math.sqrt(HEAD_DIM)
    for start in range(0, total, size):
        raised, sums = raised_scores(queries, keys, row_ref, col_ref, start, size, factor)
        mixed = dot(raised.astype(BF16), values[: start + size, :]) / sums
        for i in range(size // rows):
            at = pl.multiple_of(place[start // rows + i] * rows, rows)
            out_ref[pl.ds(at, rows), :] = mixed[i * rows : (i + 1) * rows].astype(BF16)


def attend_back_kernel(
    blocks, size, place, q_ref, k_ref, v_ref, scale_ref, gain_ref, cos_ref, sin_ref, row_ref, col_ref,
    grad_ref, gq_ref, gk_ref, gv_ref, inner_ref, gain_grad_ref, queries, keys, values, key_sum, value_sum,
):
    total = q_ref.shape[0]
    rows = total // blocks
    refs, tables = (q_ref, k_ref, v_ref, scale_ref, gain_ref), (cos_ref, sin_ref)
    load_heads(place, blocks, refs, tables, queries, keys, values)
    factor = 1.0 / math.sqrt(HEAD_DIM)
    key_sum[...] = jnp.zeros_like(key_sum)
    value_sum[...] = jnp.zeros_like(value_sum)
    gain_rows = [jnp.zeros((1, HEAD_DIM), F32), jnp.zeros((1, HEAD_DIM), F32)]

    def finish(i, a, gradient, target):
        at = pl.ds(pl.multiple_of(place[a] * rows, rows), rows)
        to = slice(a * rows, (a + 1) * rows)
        turned = pltpu.roll(gradient, HEAD_DIM // 2, 1)
        normed = gradient * cos_ref[to, :] - turned * sin_ref[to, :]
        unit = (q_ref, k_ref)[i][at, :] * scale_ref[to, i : i + 1]
        scaled = normed * gain_ref[i : i + 1, :]
        target[at, :] = scaled
        inner_ref[to, i : i + 1] += jnp.sum(scaled * unit, axis=-1, keepdims=True)
        gain_rows[i] += jnp.sum(normed * unit, axis=0, keepdims=True)

    @pl.when(pl.program_id(0) == 0)
    def _():
        inner_ref[...] = jnp.zeros_like(inner_ref)

    for start in range(0, total, size):
        stop = start + size
        raised, sums = raised_scores(queries, keys, row_ref, col_ref, start, size, factor)
        probs = raised * (1.0 / sums)
        pieces = []
        for i in range(size // rows):
            at = pl.multiple_of(place[start // rows + i] * rows, rows)
            pieces.append(grad_ref[pl.ds(at, rows), :])
        grad_mixed = jnp.concatenate(pieces, axis=0) if len(pieces) > 1 else pieces[0]
        grad_weights = dot_nt(grad_mixed, values[:stop, :])
        delta = jnp.sum(probs * grad_weights, axis=-1, keepdims=True)
        grad_scores = (probs * (grad_weights - delta)).astype(BF16)
        grad_queries = dot(grad_scores, keys[:stop, :]) * factor
        key_sum[:stop, :] += dot_tn(grad_scores, queries[start:stop, :])
        value_sum[:stop, :] += dot_tn(probs.astype(BF16), grad_mixed)
        for i in range(size // rows):
            finish(0, start // rows + i, grad_queries[i * rows : (i + 1) * rows], gq_ref)
    for a in range(blocks):
        to = slice(a * rows, (a + 1) * rows)
        finish(1, a, key_sum[to, :] * factor, gk_ref)
        gv_ref[pl.ds(pl.multiple_of(place[a] * rows, rows), rows), :] = value_sum[to, :].astype(BF16)
    gain_grad_ref[0:1, :] = gain_rows[0]
    gain_grad_ref[1:2, :] = gain_rows[1]


def attention(place, pairs, values, scales, gains, tables, row_docs, col_docs, grad_mixed=None):
    total = pairs.shape[0]
    blocks = place.shape[0]
    heads = values.shape[1] // HEAD_DIM
    size = max(256, total // blocks)
    whole = lambda h: (0, 0)
    column = lambda h: (0, h)
    in_specs = [
        pl.BlockSpec(memory_space=pltpu.SMEM),
        pl.BlockSpec((total, HEAD_DIM), lambda h: (0, h)),
        pl.BlockSpec((total, HEAD_DIM), lambda h: (0, heads + h)),
        pl.BlockSpec((total, HEAD_DIM), column),
        pl.BlockSpec((total, 2), whole),
        pl.BlockSpec((2, HEAD_DIM), column),
        pl.BlockSpec((total, HEAD_DIM), whole),
        pl.BlockSpec((total, HEAD_DIM), whole),
        pl.BlockSpec((total, 1), whole),
        pl.BlockSpec((1, total), whole),
    ]
    operands = [place, pairs, pairs, values, scales, gains, *tables, row_docs, col_docs]
    held = [pltpu.VMEM((total, HEAD_DIM), BF16)] * 3
    params = pltpu.CompilerParams(vmem_limit_bytes=VMEM_BYTES)
    work = total * total * HEAD_DIM * heads
    if grad_mixed is None:
        return pl.pallas_call(
            functools.partial(attend_kernel, blocks, size),
            grid=(heads,),
            in_specs=in_specs,
            out_specs=pl.BlockSpec((total, HEAD_DIM), column),
            out_shape=jax.ShapeDtypeStruct((total, heads * HEAD_DIM), BF16),
            scratch_shapes=held,
            compiler_params=params,
            cost_estimate=pl.CostEstimate(
                flops=4 * work, bytes_accessed=pairs.size * 8, transcendentals=total * total
            ),
        )(*operands)
    return pl.pallas_call(
        functools.partial(attend_back_kernel, blocks, size),
        grid=(heads,),
        in_specs=in_specs + [pl.BlockSpec((total, HEAD_DIM), column)],
        out_specs=[pl.BlockSpec((total, HEAD_DIM), column)] * 3
        + [pl.BlockSpec((total, 2), whole), pl.BlockSpec((2, HEAD_DIM), column)],
        out_shape=[
            jax.ShapeDtypeStruct((total, heads * HEAD_DIM), F32),
            jax.ShapeDtypeStruct((total, heads * HEAD_DIM), F32),
            jax.ShapeDtypeStruct((total, heads * HEAD_DIM), BF16),
            jax.ShapeDtypeStruct((total, 2), F32),
            jax.ShapeDtypeStruct((2, heads * HEAD_DIM), F32),
        ],
        scratch_shapes=held + [pltpu.VMEM((total, HEAD_DIM), F32)] * 2,
        compiler_params=params,
        cost_estimate=pl.CostEstimate(
            flops=10 * work, bytes_accessed=pairs.size * 16, transcendentals=total * total
        ),
    )(*operands, grad_mixed)


def router_chances(inputs, router, experts):
    logits = dot_nt(inputs, router)
    column = lax.broadcasted_iota(jnp.int32, logits.shape, 1)
    logits = jnp.where(column < experts, logits, MASKED)
    raised = jnp.exp(logits - jnp.max(logits, axis=-1, keepdims=True))
    return raised / jnp.sum(raised, axis=-1, keepdims=True)


def acts_kernel(experts, blocks, per, at_ref, *refs):
    count = blocks * per
    pieces = refs[:count]
    (
        side_ref, router_ref, wg_ref, wu_ref, wd_ref,
        x_out, u_out, hidden_ref, gate_grad_ref, up_grad_ref, sums_ref, x_buffer, u_buffer, sems,
    ) = refs[count:]
    step = pl.program_id(0)
    sides = [side_ref.at[at_ref[2 + r]] for r in range(count)]

    def copies_of(block):
        slot = block % 2
        return piece_copies(pieces, block, per, x_buffer, slot, sems, 0) + piece_copies(
            sides, block, per, u_buffer, slot, sems, per
        )

    stream(blocks, copies_of)
    owned, width, _ = wg_ref.shape
    inputs, upstream = x_buffer[step % 2], u_buffer[step % 2, :, :width]
    chosen = u_buffer[step % 2, :, width:].astype(F32)
    x_out[...] = inputs
    u_out[...] = upstream
    gates = router_chances(inputs, router_ref[...], experts) * chosen
    gate_at = lax.broadcasted_iota(jnp.int32, gates.shape, 1)
    column = lax.broadcasted_iota(jnp.int32, sums_ref.shape, 1)
    sums = jnp.zeros(sums_ref.shape, F32)
    for e in range(owned):
        gate_act = dot(inputs, wg_ref[e])
        up_act = dot(inputs, wu_ref[e])
        grad_raw = dot_nt(upstream, wd_ref[e])
        expert = at_ref[0] * owned + e
        gate = jnp.sum(jnp.where(gate_at == expert, gates, 0.0), axis=-1, keepdims=True)
        sigma = jax.nn.sigmoid(gate_act)
        active = gate_act * sigma
        hidden = active * up_act
        grad_gate = jnp.sum(hidden * grad_raw, axis=-1, keepdims=True)
        high = grad_gate.astype(BF16).astype(F32)
        sums = jnp.where(column == expert, high, sums)
        sums = jnp.where(column == expert + experts, grad_gate - high, sums)
        grad_hidden = grad_raw * gate
        hidden_ref[e] = (hidden * gate).astype(BF16)
        gate_grad_ref[e] = (grad_hidden * up_act * sigma * (1.0 + gate_act * (1.0 - sigma))).astype(BF16)
        up_grad_ref[e] = (grad_hidden * active).astype(BF16)
    sums_ref[...] = sums.astype(BF16)


def run_acts(at, pieces, sides, router, w_gate, w_up, w_down, experts, parts):
    rows, width = pieces[0].shape
    total = rows * len(pieces)
    owned, _, hidden = w_gate.shape
    piece = hidden // parts
    per = max(1, 256 // rows)
    blocks, size = len(pieces) // per, rows * per
    extra = 128 * -(-2 * experts // 128)
    lanes = router.shape[0]
    token = lambda i, at: (i, 0)
    once = pl.Buffered(1)
    acts = jax.ShapeDtypeStruct((owned, total, piece), BF16)
    act_spec = pl.BlockSpec((owned, size, piece), lambda i, at: (0, i, 0))
    return pl.pallas_call(
        functools.partial(acts_kernel, experts, blocks, per),
        grid_spec=pltpu.PrefetchScalarGridSpec(
            num_scalar_prefetch=1,
            grid=(blocks,),
            in_specs=[pl.BlockSpec(memory_space=pl.ANY)] * (len(pieces) + 1)
            + [
                pl.BlockSpec((lanes, width), lambda i, at: (0, 0), pipeline_mode=once),
                pl.BlockSpec((owned, width, piece), lambda i, at: (0, 0, at[1]), pipeline_mode=once),
                pl.BlockSpec((owned, width, piece), lambda i, at: (0, 0, at[1]), pipeline_mode=once),
                pl.BlockSpec((owned, piece, width), lambda i, at: (0, at[1], 0), pipeline_mode=once),
            ],
            out_specs=[pl.BlockSpec((size, width), token)] * 2
            + [act_spec] * 3
            + [pl.BlockSpec((size, extra), token)],
            scratch_shapes=[
                pltpu.VMEM((2, size, width), BF16),
                pltpu.VMEM((2, size, width + lanes), BF16),
                pltpu.SemaphoreType.DMA((2, 2 * per)),
            ],
        ),
        out_shape=[
            jax.ShapeDtypeStruct((total, width), BF16),
            jax.ShapeDtypeStruct((total, width), BF16),
            acts,
            acts,
            acts,
            jax.ShapeDtypeStruct((total, extra), BF16),
        ],
        compiler_params=pltpu.CompilerParams(vmem_limit_bytes=VMEM_BYTES),
        cost_estimate=pl.CostEstimate(
            flops=6 * total * width * piece * owned,
            bytes_accessed=2 * (4 * total * width + 3 * owned * piece * (total + width)),
            transcendentals=total * piece * owned,
        ),
    )(at, *pieces, sides, router, w_gate, w_up, w_down)


def rows_back_kernel(blocks, per, at_ref, gate_ref, up_ref, sums_ref, wg_ref, wu_ref, near_ref, far_ref):
    back = dot_nt(gate_ref[0], wg_ref[0]) + dot_nt(up_ref[0], wu_ref[0])
    for e in range(1, wg_ref.shape[0]):
        back += dot_nt(gate_ref[e], wg_ref[e]) + dot_nt(up_ref[e], wu_ref[e])
    back = back.astype(BF16)
    step = pl.program_id(0)
    rows, width = near_ref.shape[2], back.shape[1]

    def store(out_ref):
        for i in range(per):
            at = at_ref[2 + step * per + i] // 2 % per
            part = slice(i * rows, (i + 1) * rows)
            out_ref[0, at, :, :width] = back[part]
            out_ref[0, at, :, width:] = sums_ref[part, :]

    pl.when(step < blocks // 2)(lambda: store(near_ref))
    pl.when(step >= blocks // 2)(lambda: store(far_ref))


def rows_out_kernel(sets, blocks, per, at_ref, *refs):
    *hidden_refs, wd_ref, out_ref = refs
    step = pl.program_id(0)
    rows = out_ref.shape[4]
    for k, hidden_ref in enumerate(hidden_refs):

        @pl.when(step // blocks == k)
        def _():
            out = dot(hidden_ref[0], wd_ref[0])
            for e in range(1, wd_ref.shape[0]):
                out += dot(hidden_ref[e], wd_ref[e])
            for i in range(per):
                at = at_ref[2 + (step - k * blocks) * per + i] // 2 % per
                out_ref[0, at, 0, 0] = out[i * rows : (i + 1) * rows].astype(BF16)


def run_out(at, hiddens, w_down, rows):
    owned, total, piece = hiddens[0].shape
    sets, width = len(hiddens), w_down.shape[2]
    seq_size = total // rows
    per = max(1, 256 // rows)
    size, blocks = rows * per, seq_size // per

    def hidden_at(k):
        return lambda i, at: (0, jnp.clip(i - k * blocks, 0, blocks - 1), 0)

    def out_at(i, at):
        first = at[2 + (i % blocks) * per]
        return (first // (2 * per), 0, first % 2, i // blocks, 0, 0)

    out = pl.pallas_call(
        functools.partial(rows_out_kernel, sets, blocks, per),
        grid_spec=pltpu.PrefetchScalarGridSpec(
            num_scalar_prefetch=1,
            grid=(sets * blocks,),
            in_specs=[pl.BlockSpec((owned, size, piece), hidden_at(k)) for k in range(sets)]
            + [
                pl.BlockSpec(
                    (owned, piece, width), lambda i, at: (0, at[1], 0), pipeline_mode=pl.Buffered(1)
                )
            ],
            out_specs=pl.BlockSpec((1, per, 1, 1, rows, width), out_at),
        ),
        out_shape=jax.ShapeDtypeStruct((seq_size // (2 * per), per, 2, sets, rows, width), BF16),
        compiler_params=pltpu.CompilerParams(vmem_limit_bytes=VMEM_BYTES),
        cost_estimate=pl.CostEstimate(
            flops=2 * sets * total * width * piece * owned,
            bytes_accessed=2 * sets * total * (width + owned * piece),
            transcendentals=0,
        ),
    )(at, *hiddens, w_down)
    return out.reshape(seq_size, sets, rows, width)


def run_back(at, gates, ups, sums, w_gate, w_up, rows):
    owned, total, piece = gates.shape
    chips = total // (2 * rows)
    per = max(1, 256 // rows)
    size, blocks = rows * per, total // (rows * per)
    middle = blocks // 2
    width, extra = w_gate.shape[1], sums.shape[1]
    act_spec = pl.BlockSpec((owned, size, piece), lambda i, at: (0, i, 0))
    weight_spec = pl.BlockSpec(
        (owned, width, piece), lambda i, at: (0, 0, at[1]), pipeline_mode=pl.Buffered(1)
    )

    def out_spec(first, last):
        return pl.BlockSpec(
            (1, per, rows, width + extra),
            lambda i, at: (at[2 + jnp.clip(i, first, last) * per] // (2 * per), 0, 0, 0),
        )

    out = jax.ShapeDtypeStruct((chips // per, per, rows, width + extra), BF16)
    results = pl.pallas_call(
        functools.partial(rows_back_kernel, blocks, per),
        grid_spec=pltpu.PrefetchScalarGridSpec(
            num_scalar_prefetch=1,
            grid=(blocks,),
            in_specs=[act_spec] * 2
            + [pl.BlockSpec((size, extra), lambda i, at: (i, 0))]
            + [weight_spec] * 2,
            out_specs=[out_spec(0, middle - 1), out_spec(middle, blocks - 1)],
        ),
        out_shape=[out, out],
        compiler_params=pltpu.CompilerParams(vmem_limit_bytes=VMEM_BYTES),
        cost_estimate=pl.CostEstimate(
            flops=4 * total * width * piece * owned,
            bytes_accessed=2 * (total * width + 2 * owned * piece * (total + width)),
            transcendentals=0,
        ),
    )(at, gates, ups, sums, w_gate, w_up)
    return [item.reshape(chips, rows, width + extra) for item in results]


def down_kernel(sets, at_ref, *refs):
    out_ref = refs[-1]
    for e in range(out_ref.shape[1]):
        term = dot_tn(refs[0][e], refs[sets][...])
        for i in range(1, sets):
            term += dot_tn(refs[i][e], refs[sets + i][...])
        out_ref[0, e] = term.astype(BF16)


def down_blocks(targets, hiddens, upstreams, group, width):
    owned, total, piece = hiddens[0].shape
    deep = piece // group
    sets, count = len(hiddens), targets.shape[0]
    wide = min(512, width)
    return pl.pallas_call(
        functools.partial(down_kernel, sets),
        grid_spec=pltpu.PrefetchScalarGridSpec(
            num_scalar_prefetch=1,
            grid=(count, width // wide),
            in_specs=[pl.BlockSpec((owned, total, deep), lambda g, j, at: (0, 0, at[g]))] * sets
            + [pl.BlockSpec((total, wide), lambda g, j, at: (0, j))] * sets,
            out_specs=pl.BlockSpec((1, owned, deep, wide), lambda g, j, at: (g, 0, 0, j)),
        ),
        out_shape=jax.ShapeDtypeStruct((count, owned, deep, width), BF16),
        compiler_params=pltpu.CompilerParams(vmem_limit_bytes=VMEM_BYTES),
        cost_estimate=pl.CostEstimate(
            flops=2 * sets * count * owned * total * deep * width,
            bytes_accessed=2 * sets * total * (width + owned * deep),
            transcendentals=0,
        ),
    )(targets, *hiddens, *upstreams)


def in_kernel(sets, at_ref, *refs):
    out_ref = refs[-1]
    for e in range(out_ref.shape[2]):
        term = dot_tn(refs[0][...], refs[sets][e])
        for i in range(1, sets):
            term += dot_tn(refs[i][...], refs[sets + i][e])
        out_ref[0, 0, e] = term.astype(BF16)


def in_blocks(targets, inputs, acts, group, parts):
    owned, total, piece = acts[0].shape
    width = inputs[0].shape[1]
    deep = width // (group * parts)
    sets, count = len(inputs), targets.shape[0]
    held = pl.BlockSpec((owned, total, piece), lambda g, p, at: (0, 0, 0), pipeline_mode=pl.Buffered(1))
    return pl.pallas_call(
        functools.partial(in_kernel, sets),
        grid_spec=pltpu.PrefetchScalarGridSpec(
            num_scalar_prefetch=1,
            grid=(count, parts),
            in_specs=[pl.BlockSpec((total, deep), lambda g, p, at: (0, p * group + at[g]))] * sets
            + [held] * sets,
            out_specs=pl.BlockSpec((1, 1, owned, deep, piece), lambda g, p, at: (g, p, 0, 0, 0)),
        ),
        out_shape=jax.ShapeDtypeStruct((count, parts, owned, deep, piece), BF16),
        compiler_params=pltpu.CompilerParams(vmem_limit_bytes=VMEM_BYTES),
        cost_estimate=pl.CostEstimate(
            flops=2 * sets * count * parts * owned * total * deep * piece,
            bytes_accessed=4 * sets * owned * total * piece,
            transcendentals=0,
        ),
    )(targets, *inputs, *acts)


def on_device(
    tokens,
    segments,
    expert_ids,
    w_query,
    w_key,
    w_value,
    w_out,
    w_router,
    attn_gain,
    query_gain,
    key_gain,
    ffn_gain,
    w_gate,
    w_up,
    w_down,
    out_grad,
):
    seq_size, batch_size = lax.axis_size("seq"), lax.axis_size("batch")
    seq_at, batch_at = lax.axis_index("seq"), lax.axis_index("batch")
    parts = 2 if batch_size % 2 == 0 else 1
    half = batch_size // parts
    part_at, in_group = batch_at // half, batch_at % half
    low_tokens = tokens[0]
    inputs = low_tokens.astype(F32)
    rows, width = inputs.shape
    total = rows * seq_size
    experts = w_router.shape[1]
    owned = w_gate.shape[0]
    wide = width // seq_size
    shard = w_query.shape[0]

    masks = masks_of(seq_size)
    order = seq_at ^ jnp.array(masks, jnp.int32)
    place = jnp.array([masks.index(m) for m in range(seq_size)], jnp.int32)[
        jnp.arange(seq_size, dtype=jnp.int32) ^ seq_at
    ]

    def reordered(values, by):
        return values.reshape(-1, seq_size, rows)[:, by].reshape(values.shape)

    masks = masks_of(seq_size)
    order = seq_at ^ jnp.array(masks, jnp.int32)
    place = jnp.array([masks.index(m) for m in range(seq_size)], jnp.int32)[
        jnp.arange(seq_size, dtype=jnp.int32) ^ seq_at
    ]
    here = jnp.concatenate([jnp.stack([seq_at, batch_at]).astype(jnp.int32), order])

    def reordered(values, by):
        return values.reshape(-1, seq_size, rows)[:, by].reshape(values.shape)

    masks = masks_of(seq_size)
    order = seq_at ^ jnp.array(masks, jnp.int32)
    place = jnp.array([masks.index(m) for m in range(seq_size)], jnp.int32)[
        jnp.arange(seq_size, dtype=jnp.int32) ^ seq_at
    ]
    here = jnp.concatenate([jnp.stack([seq_at, batch_at]).astype(jnp.int32), order])
    at = jnp.concatenate([jnp.stack([seq_at, part_at]).astype(jnp.int32), order])

    def reordered(values, by):
        return values.reshape(-1, seq_size, rows)[:, by].reshape(values.shape)

    near_tokens = gather_near(low_tokens)

    def cut_of(*weights):
        return jnp.concatenate(
            [w.reshape(shard, seq_size, wide).transpose(1, 0, 2) for w in weights], axis=2
        )

    def exchange(blocks):
        return lax.all_to_all(blocks, "seq", split_axis=0, concat_axis=0, tiled=True)

    small = jnp.concatenate(
        [jnp.stack([attn_gain, query_gain, key_gain, ffn_gain]), w_router.T], axis=0
    )
    items, fit = experts + 4, 2 * wide // shard
    deep = 8 * -(-items // (8 * fit))
    small = jnp.pad(small, ((0, deep * fit - items), (0, 0))).reshape(1, deep, 2 * wide)
    small = jnp.broadcast_to(small, (seq_size, deep, 2 * wide))
    pair_cut = exchange(jnp.concatenate([cut_of(w_query, w_key), small], axis=1))

    ids = expert_ids[0]
    lanes = 128 * -(-experts // 128)
    choices = jnp.any(ids[:, :, None] == jnp.arange(lanes, dtype=jnp.int32), axis=1)
    side = jnp.concatenate([out_grad[0], choices.astype(BF16)], axis=1)
    partner = [hop(side, "batch", half)] if parts == 2 else []
    token_pieces = near_tokens + [hop(after(piece, pair_cut, *partner), "seq", 1) for piece in near_tokens]
    value_cut = exchange(after(cut_of(w_value), pair_cut))
    pair_pieces = gather_batch(after(pair_cut, *token_pieces), value_cut)
    value_pieces = gather_batch(after(value_cut, *pair_pieces[2:3]), *pair_pieces)
    out_pieces = gather_batch(after(w_out, *pair_pieces), *value_pieces)
    small = jnp.stack([item[:, shard:] for item in pair_pieces])
    small = small.reshape(batch_size, seq_size, deep * fit, shard)[
        jnp.arange(batch_size, dtype=jnp.int32) ^ batch_at
    ]
    small = small.transpose(2, 1, 0, 3).reshape(deep * fit, width)
    gains = small[:4].astype(F32)
    attn_norm_gain, ffn_norm_gain = gains[0], gains[3]
    head_gains = lax.dynamic_slice_in_dim(gains[1:3], seq_at * wide, wide, 1)
    router = jnp.pad(small[4:items], ((0, lanes - experts), (0, 0)))
    w_mix = jnp.zeros((batch_size, shard, width), BF16)
    for t, piece in enumerate(out_pieces):
        w_mix = put(w_mix, piece[None], (batch_at ^ t, 0, 0))
    w_mix = w_mix.reshape(wide, width)

    sides = [
        lax.all_gather(after(item, *pins), "seq", axis=0)
        for item, pins in zip([side, *partner], ([value_cut, *pair_pieces[1:3]], pair_pieces))
    ]
    counts = jnp.sum(sides[0][:, :, width:].astype(F32), axis=(0, 1)).astype(jnp.int32)
    counts_here = lax.dynamic_slice_in_dim(counts, seq_at * owned, owned, 0)

    normed, pairs, squares, pair_weights = project_pairs(
        here, token_pieces, pair_pieces, shard, after(attn_norm_gain[None], *value_pieces[:3])
    )
    values, value_weights = project_values(here, normed, value_pieces)
    pair_weights, value_weights = (w.reshape(width, -1) for w in (pair_weights, value_weights))

    def sum_seq(values):
        return jnp.sum(lax.all_gather(values, "seq", axis=0), axis=0)

    scales = lax.rsqrt(sum_seq(squares) / width + EPSILON)
    rates = jnp.power(
        ROTARY_BASE, -jnp.arange(HEAD_DIM // 2, dtype=F32) * (2.0 / HEAD_DIM)
    )
    angles = jnp.arange(total, dtype=F32)[:, None] * rates[None, :]
    cosine, sine = jnp.cos(angles), jnp.sin(angles)
    tables = (
        jnp.concatenate([cosine, cosine], axis=1),
        jnp.concatenate([-sine, sine], axis=1),
    )
    attend = functools.partial(
        attention,
        place,
        pairs,
        values,
        scales.T,
        head_gains,
        tables,
        segments[0][:, None],
        segments[0][None, :],
    )
    mixed_low = after(attend(), sides[0])
    middle = total // 2
    far = dot(mixed_low[middle:], w_mix).astype(BF16)
    residual = inputs + scatter_seq(dot(mixed_low[:middle], w_mix).astype(BF16), far)[0]
    ffn_scale = norm_scale(residual)
    ffn_unit = residual * ffn_scale
    ffn_in = (ffn_unit * ffn_norm_gain).astype(BF16)

    def acts_of(k, pieces):
        return run_acts(at, pieces, sides[k], router, w_gate, w_up, w_down, experts, parts)

    ffn_pieces = gather_seq(ffn_in)
    results = [acts_of(0, ffn_pieces)]
    if parts == 2:
        partner = hop(ffn_in, "batch", half)
        near = gather_near(after(partner, *ffn_pieces))
        near = [after(piece, results[0][0]) for piece in near]
        results.append(acts_of(1, near + [hop(piece, "seq", 1) for piece in near]))
    all_ffn, upstreams, hiddens, gate_acts, up_acts, sums = zip(*results)
    own = in_group[None].astype(jnp.int32)
    others = jnp.stack([in_group ^ t for t in range(1, half)]).astype(jnp.int32) if half > 1 else None
    down = functools.partial(down_blocks, hiddens=hiddens, upstreams=upstreams, group=half, width=width)
    into = functools.partial(in_blocks, inputs=all_ffn, group=half, parts=parts)

    def send_group(theirs):
        return [hop(theirs[t - 1], "batch", t) for t in range(1, half)]

    def gather_group(theirs):
        groups = [list(range(first, first + half)) for first in range(0, batch_size, half)]
        blocks = lax.all_gather(theirs, "batch", axis=0, axis_index_groups=groups)
        return [take_block(blocks, in_group ^ t)[t - 1] for t in range(1, half)]

    def group_sum(mine, moved):
        total = mine[0].astype(F32)
        for item in moved:
            total = total + item.astype(F32)
        return total

    def swap_part(summed):
        return hop(take_block(summed, 1 - part_at).astype(BF16), "batch", half)

    gate_moved = up_moved = down_moved = ()
    at_back = at
    if half > 1:
        gate_theirs = into(others, acts=gate_acts)
        gate_moved = send_group(gate_theirs)
        at_back = after(at, gate_theirs)
    backs, sent = [], []
    for k in reversed(range(parts)):
        near, far = run_back(at_back, gate_acts[k], up_acts[k], sums[k], w_gate, w_up, rows)
        if half > 1 and not sent:
            up_theirs = into(after(others, near), acts=up_acts)
            near = after(near, up_theirs)
        if k == 0:
            mix = run_out(after(at, near), hiddens, w_down, rows)
            far = after(far, mix, *backs, *gate_moved)
        summed, low = scatter_chips(near, far)
        backs.insert(0, summed)
        sent.append(low)
        at_back = after(at, low)
    gate_mine = last = into(after(own, *sent), acts=gate_acts)
    other = hop(backs[1].astype(BF16), "batch", half) if parts == 2 else gate_mine
    if half > 1:
        last = down_theirs = down(after(others, gate_mine))
    gate_sum = group_sum(gate_mine, gate_moved)
    up_mine = into(after(own, last, other), acts=up_acts)
    gate_other = swap_part(gate_sum) if parts == 2 else gate_sum
    if half > 1:
        up_moved = gather_group(up_theirs)
        down_moved = gather_group(down_theirs)
    back = after(backs[0], up_mine, gate_sum)
    if parts == 2:
        back = back + other.astype(F32)

    grad_ffn_in = back[:, :width]
    grad_chances = choices[:, :experts] * (
        back[:, width : width + experts] + back[:, width + experts : width + 2 * experts]
    )
    chances = router_chances(ffn_in, router, experts)[:, :experts]
    grad_logits = (
        chances * (grad_chances - jnp.sum(chances * grad_chances, axis=-1, keepdims=True))
    ).astype(BF16)
    grad_ffn_in = grad_ffn_in + dot(grad_logits, router[:experts])
    scaled = grad_ffn_in * ffn_norm_gain
    inner = jnp.mean(scaled * ffn_unit, axis=-1, keepdims=True)
    grad_residual = out_grad[0].astype(F32) + ffn_scale * (scaled - ffn_unit * inner)
    grad_attn = grad_residual.astype(BF16)

    grad_near = gather_near(grad_attn)
    arrived = grad_near[1:]
    up_sum = group_sum(up_mine, [after(item, grad_attn) for item in up_moved])
    grad_near[0] = after(grad_attn, up_sum, *arrived)
    grad_pieces = grad_near + [hop(piece, "seq", 1) for piece in grad_near]
    up_other = swap_part(up_sum) if parts == 2 else up_sum
    grad_mixed, out_term = mix_back(grad_pieces, after(mixed_low, gate_other), w_mix)
    mix = lax.psum_scatter(after(mix, grad_mixed), "seq", scatter_dimension=0)
    scaled_q, scaled_k, value_low, inner, gain_terms = attend(grad_mixed=grad_mixed)

    def term_of(values):
        return dot_tn(normed, values).astype(BF16).reshape(seq_size * batch_size, shard, -1)

    value_term = term_of(value_low)
    inner = reordered(sum_seq(after(inner.T, value_term)), order).T / width
    rel_scales = reordered(scales, order).T
    lows = []
    for i, item in enumerate((scaled_q, scaled_k)):
        scale = rel_scales[:, i : i + 1]
        unit = pairs[:, i * wide : (i + 1) * wide] * scale
        lows.append((scale * (item - unit * inner[:, i : i + 1])).astype(BF16))
    pair_low = jnp.concatenate(lows, axis=1)
    pair_term = term_of(pair_low)
    late_low = after(pair_low, pair_term)

    def rows_of(at):
        return (dot_nt(late_low[at], pair_weights) + dot_nt(value_low[at], value_weights)).astype(BF16)

    far = rows_of(slice(middle, total))
    grad_normed, _ = scatter_seq(rows_of(slice(0, middle)), far)
    mix_other = hop(after(mix[1], value_low), "batch", half) if parts == 2 else mix
    grad_normed = after(grad_normed, mix_other)
    down_mine = down(after(own, grad_normed))

    def head_sums(term, extra):
        term = jnp.concatenate([term, *extra], axis=1)
        term = lax.all_to_all(term, ("seq", "batch"), split_axis=0, concat_axis=0, tiled=True)
        term = after(term, grad_normed)
        total = jnp.sum(term[:, :shard].reshape(seq_size, batch_size, shard, -1).astype(F32), axis=1)
        return total, jnp.sum(term[:, shard:].astype(F32), axis=0)

    def two_parts(values):
        high = values.astype(BF16)
        return jnp.concatenate([high, (values - high.astype(F32)).astype(BF16)], axis=0)

    def in_rows(items):
        fit = wide // shard
        deep = 8 * -(-items.shape[0] // (8 * fit))
        items = jnp.pad(items, ((0, deep * fit - items.shape[0]), (0, 0), (0, 0), (0, 0)))
        return items.transpose(1, 2, 0, 3).reshape(seq_size * batch_size, deep, wide)

    router_term = jnp.concatenate(
        [dot_tn(grad_logits, ffn_in), jnp.sum(grad_ffn_in * ffn_unit, axis=0)[None]], axis=0
    )
    router_items = two_parts(router_term).reshape(-1, seq_size, batch_size, shard)
    gain_items = two_parts(gain_terms).reshape(4, 1, batch_size, shard)
    mine_only = (jnp.arange(seq_size) == seq_at)[None, :, None, None]
    gain_items = jnp.where(mine_only, gain_items, jnp.zeros_like(gain_items))
    items = in_rows(jnp.concatenate([gain_items, router_items], axis=0))
    value_sums, items = head_sums(value_term, [items])
    items = items.reshape(-1, shard)
    gain_sum = items[0:2] + items[2:4]
    router_sum = items[4 : 5 + experts] + items[5 + experts : 6 + 2 * experts]
    router_grad, ffn_gain_grad = router_sum[:experts].T, router_sum[experts]
    pair_sums, _ = head_sums(pair_term, [])
    query_grad, key_grad, value_grad = (
        item.transpose(1, 0, 2).reshape(shard, width)
        for item in (pair_sums[:, :, :wide], pair_sums[:, :, wide:], value_sums)
    )

    def spread(summed, other):
        if parts == 1:
            return summed[0]
        keep, other = take_block(summed, part_at), other.astype(F32)
        return jnp.where(
            part_at == 0,
            jnp.concatenate([keep, other], axis=-1),
            jnp.concatenate([other, keep], axis=-1),
        )

    down_grad = group_sum(down_mine, [after(item, pair_term) for item in down_moved])
    gate_grad = spread(gate_sum, after(gate_other, pair_term))
    up_grad = spread(up_sum, after(up_other, grad_normed))
    out_proj_grad = scatter_batch(
        out_term.reshape(batch_size, shard, width), batch_at, BF16, far, grad_normed
    )

    mine = mix[0].astype(F32)
    if parts == 2:
        mine = mine + mix_other.astype(F32)
    block_out = (residual + mine).astype(BF16)

    attn_scale = norm_scale(inputs)
    attn_unit = inputs * attn_scale
    scaled = grad_normed * attn_norm_gain
    inner = jnp.mean(scaled * attn_unit, axis=-1, keepdims=True)
    grad_input = grad_residual + attn_scale * (scaled - attn_unit * inner)
    attn_gain_grad = (
        jnp.sum(
            query_grad * w_query.astype(F32)
            + key_grad * w_key.astype(F32)
            + value_grad * w_value.astype(F32),
            axis=1,
        )
        / attn_gain.astype(F32)
    )
    return (
        block_out[None],
        grad_input[None],
        query_grad,
        key_grad,
        value_grad,
        out_proj_grad,
        router_grad,
        attn_gain_grad,
        gain_sum[0],
        gain_sum[1],
        ffn_gain_grad,
        gate_grad,
        up_grad,
        down_grad,
        counts_here[None],
    )


def solution(mesh):
    in_specs = (
        P("batch", "seq", None),
        P("batch", None),
        P("batch", "seq", None),
        P(("seq", "batch"), None),
        P(("seq", "batch"), None),
        P(("seq", "batch"), None),
        P(("seq", "batch"), None),
        P(("seq", "batch"), None),
        P(("seq", "batch")),
        P(("seq", "batch")),
        P(("seq", "batch")),
        P(("seq", "batch")),
        P("seq", None, None),
        P("seq", None, None),
        P("seq", None, None),
        P("batch", "seq", None),
    )
    out_specs = (
        P("batch", "seq", None),
        P("batch", "seq", None),
        P(("seq", "batch"), None),
        P(("seq", "batch"), None),
        P(("seq", "batch"), None),
        P(("seq", "batch"), None),
        P(("seq", "batch"), None),
        P(("seq", "batch")),
        P(("seq", "batch")),
        P(("seq", "batch")),
        P(("seq", "batch")),
        P("seq", "batch", None),
        P("seq", "batch", None),
        P("seq", "batch", None),
        P("batch", "seq"),
    )
    return jax.shard_map(
        on_device, mesh=mesh, in_specs=in_specs, out_specs=out_specs, check_vma=False
    )
```

```python
import functools
import math

import jax
import jax.numpy as jnp
from jax import lax
from jax.experimental import pallas as pl
from jax.experimental.pallas import tpu as pltpu
from jax.sharding import PartitionSpec as P

HEAD_DIM = 128
EPSILON = 1e-05
ROTARY_BASE = 10000.0
MASKED = -1e30
BF16 = jnp.bfloat16
F32 = jnp.float32
VMEM_BYTES = 60 * 1024 * 1024


def dot(left, right):
    return lax.dot_general(left, right, (((1,), (0,)), ((), ())), preferred_element_type=F32)


def dot_nt(left, right):
    return lax.dot_general(left, right, (((1,), (1,)), ((), ())), preferred_element_type=F32)


def dot_tn(left, right):
    return lax.dot_general(left, right, (((0,), (0,)), ((), ())), preferred_element_type=F32)


def norm_scale(values):
    return lax.rsqrt(jnp.mean(values * values, axis=-1, keepdims=True) + EPSILON)


def hop(values, axis, mask):
    size = lax.axis_size(axis)
    return lax.ppermute(values, axis, [(i, i ^ mask) for i in range(size)])


def take_block(values, index, axis=0):
    return lax.dynamic_index_in_dim(values, index, axis, keepdims=False)


def put(buffer, values, starts):
    return lax.dynamic_update_slice(buffer, values, starts)


def after(values, *earlier):
    return lax.optimization_barrier((values, *earlier))[0]


def masks_of(size):
    return [2 * m for m in range(size // 2)] + [2 * m + 1 for m in range(size // 2)]


def gather_near(values):
    return [values] + [hop(values, "seq", 2 * m) for m in range(1, lax.axis_size("seq") // 2)]


def gather_seq(values):
    near = gather_near(values)
    near[0] = after(values, *near[1:2])
    return near + [hop(piece, "seq", 1) for piece in near]


def scatter_seq(near, far):
    chips = lax.axis_size("seq") // 2
    rows = near.shape[0] // chips
    moved = hop(far, "seq", 1)

    def both(m):
        at = slice(m * rows, (m + 1) * rows)
        return near[at].astype(F32) + moved[at].astype(F32)

    sent = [both(m).astype(BF16) for m in range(1, chips)]
    total = both(0)
    for m in range(1, chips):
        total = total + hop(sent[m - 1], "seq", 2 * m).astype(F32)
    return total, sent


def scatter_chips(near, far):
    size = lax.axis_size("seq")
    sent = (near.astype(F32) + hop(far, "seq", 1).astype(F32)).astype(BF16)
    groups = [list(range(core, size, 2)) for core in range(2)]
    moved = lax.all_to_all(
        sent, "seq", split_axis=0, concat_axis=0, axis_index_groups=groups, tiled=True
    )
    return jnp.sum(moved.astype(F32), axis=0), sent


def gather_batch(values, *pins):
    pieces = [values]
    for t in range(1, lax.axis_size("batch")):
        if t % 2 and t > 1:
            pieces.append(hop(after(pieces[t - 1], *pieces[1 : t - 1], *pins), "batch", 1))
        else:
            pieces.append(hop(values, "batch", t))
    return pieces


def scatter_batch(blocks, me, kind, *pins):
    size = blocks.shape[0]
    if size == 1:
        return blocks[0].astype(F32)
    theirs = jnp.stack([take_block(blocks, me ^ t ^ 1) for t in range(0, size, 2)])
    moved = after(hop(theirs, "batch", 1), pins[0])
    total = take_block(blocks, me).astype(F32) + moved[0].astype(F32)
    for i in range(1, size // 2):
        pair = take_block(blocks, me ^ (2 * i)).astype(F32) + moved[i].astype(F32)
        total = total + after(hop(pair.astype(kind), "batch", 2 * i), pins[1]).astype(F32)
    return total


def piece_copies(refs, block, per, buffer, slot, sems, first):
    rows = buffer.shape[1] // per
    return [
        pltpu.make_async_copy(
            refs[block * per + i],
            buffer.at[slot, pl.ds(i * rows, rows), :],
            sems.at[slot, first + i],
        )
        for i in range(per)
    ]


def stream(blocks, copies_of):
    step = pl.program_id(0)
    for block in range(blocks):

        @pl.when(step == block)
        def _():
            if block == 0:
                for copy in copies_of(0):
                    copy.start()
            if block + 1 < blocks:
                for copy in copies_of(block + 1):
                    copy.start()
            for copy in copies_of(block):
                copy.wait()


def weight_copies(at_ref, pieces, target, sems):
    shard = target.shape[2]
    return [
        pltpu.make_async_copy(piece.at[:, pl.ds(0, shard)], target.at[:, at_ref[1] ^ t], sems.at[t])
        for t, piece in enumerate(pieces)
    ]


def project_pairs_kernel(blocks, per, at_ref, *refs):
    count = blocks * per
    pieces, w_pieces = refs[:count], refs[count : -8]
    gain_ref, normed_ref, pair_ref, square_ref, weight_ref, buffer, sems, w_sems = refs[-8:]
    step = pl.program_id(0)

    @pl.when(step == 0)
    def _():
        for copy in weight_copies(at_ref, w_pieces, weight_ref, w_sems):
            copy.start()

    stream(blocks, lambda block: piece_copies(pieces, block, per, buffer, block % 2, sems, 0))

    @pl.when(step == 0)
    def _():
        for copy in weight_copies(at_ref, w_pieces, weight_ref, w_sems):
            copy.wait()

    values = buffer[step % 2].astype(F32)
    normed = (values * norm_scale(values) * gain_ref[...]).astype(BF16)
    normed_ref[...] = normed
    width = normed.shape[1]
    pair = dot(normed, weight_ref[...].reshape(width, -1))
    pair_ref[...] = pair
    wide = pair.shape[1] // 2
    squared = pair * pair
    high = squared.astype(BF16)
    low = (squared - high.astype(F32)).astype(BF16)
    lane = lax.broadcasted_iota(jnp.int32, (8, 2 * wide), 1)
    line = lax.broadcasted_iota(jnp.int32, (8, 2 * wide), 0)
    pick = (lane // wide == line).astype(BF16)
    sums = (dot_nt(pick, high) + dot_nt(pick, low))[:2]
    rows = normed.shape[0] // per
    for i in range(per):
        at = pl.multiple_of(at_ref[2 + step * per + i] * rows, rows)
        square_ref[:, pl.ds(at, rows)] = sums[:, i * rows : (i + 1) * rows]


def project_pairs(here, pieces, w_pieces, shard, gain):
    rows, width = pieces[0].shape
    seq_size, _, columns = w_pieces[0].shape
    batch_size = len(w_pieces)
    per = max(1, 256 // rows)
    blocks = len(pieces) // per
    total, size = rows * len(pieces), rows * per
    return pl.pallas_call(
        functools.partial(project_pairs_kernel, blocks, per),
        grid_spec=pltpu.PrefetchScalarGridSpec(
            num_scalar_prefetch=1,
            grid=(blocks,),
            in_specs=[pl.BlockSpec(memory_space=pl.ANY)] * (len(pieces) + batch_size)
            + [pl.BlockSpec((1, width), lambda i, at: (0, 0))],
            out_specs=[
                pl.BlockSpec((size, width), lambda i, at: (i, 0)),
                pl.BlockSpec((size, columns), lambda i, at: (i, 0)),
                pl.BlockSpec((2, total), lambda i, at: (0, 0)),
                pl.BlockSpec((seq_size, batch_size, shard, columns), lambda i, at: (0, 0, 0, 0)),
            ],
            scratch_shapes=[
                pltpu.VMEM((2, size, width), BF16),
                pltpu.SemaphoreType.DMA((2, per)),
                pltpu.SemaphoreType.DMA((batch_size,)),
            ],
        ),
        out_shape=[
            jax.ShapeDtypeStruct((total, width), BF16),
            jax.ShapeDtypeStruct((total, columns), F32),
            jax.ShapeDtypeStruct((2, total), F32),
            jax.ShapeDtypeStruct((seq_size, batch_size, shard, columns), BF16),
        ],
        compiler_params=pltpu.CompilerParams(vmem_limit_bytes=VMEM_BYTES),
        cost_estimate=pl.CostEstimate(
            flops=2 * total * width * columns, bytes_accessed=8 * total * width, transcendentals=0
        ),
    )(here, *pieces, *w_pieces, gain)


def project_values_kernel(at_ref, normed_ref, *refs):
    *w_pieces, value_ref, weight_ref, w_sems = refs

    @pl.when(pl.program_id(0) == 0)
    def _():
        copies = weight_copies(at_ref, w_pieces, weight_ref, w_sems)
        for copy in copies:
            copy.start()
        for copy in copies:
            copy.wait()

    width = normed_ref.shape[1]
    value_ref[...] = dot(normed_ref[...], weight_ref[...].reshape(width, -1)).astype(BF16)


def project_values(here, normed, w_pieces):
    total, width = normed.shape
    seq_size, shard, columns = w_pieces[0].shape
    batch_size = len(w_pieces)
    size = min(512, total)
    return pl.pallas_call(
        project_values_kernel,
        grid_spec=pltpu.PrefetchScalarGridSpec(
            num_scalar_prefetch=1,
            grid=(total // size,),
            in_specs=[pl.BlockSpec((size, width), lambda i, at: (i, 0))]
            + [pl.BlockSpec(memory_space=pl.ANY)] * batch_size,
            out_specs=[
                pl.BlockSpec((size, columns), lambda i, at: (i, 0)),
                pl.BlockSpec((seq_size, batch_size, shard, columns), lambda i, at: (0, 0, 0, 0)),
            ],
            scratch_shapes=[pltpu.SemaphoreType.DMA((batch_size,))],
        ),
        out_shape=[
            jax.ShapeDtypeStruct((total, columns), BF16),
            jax.ShapeDtypeStruct((seq_size, batch_size, shard, columns), BF16),
        ],
        compiler_params=pltpu.CompilerParams(vmem_limit_bytes=VMEM_BYTES),
        cost_estimate=pl.CostEstimate(
            flops=2 * total * width * columns, bytes_accessed=2 * total * width, transcendentals=0
        ),
    )(here, normed, *w_pieces)


def mix_back_kernel(blocks, per, *refs):
    pieces = refs[: blocks * per]
    mixed_ref, weight_ref, back_ref, grad_ref, buffer, total, sems = refs[blocks * per :]
    step = pl.program_id(0)
    stream(blocks, lambda block: piece_copies(pieces, block, per, buffer, block % 2, sems, 0))
    gradient = buffer[step % 2]
    back_ref[...] = dot_nt(gradient, weight_ref[...]).astype(BF16)
    term = dot_tn(mixed_ref[...], gradient)

    @pl.when(step == 0)
    def _():
        total[...] = term

    @pl.when(step > 0)
    def _():
        total[...] += term

    @pl.when(step == blocks - 1)
    def _():
        grad_ref[...] = total[...].astype(BF16)


def mix_back(pieces, mixed, weight):
    rows, width = pieces[0].shape
    wide = weight.shape[0]
    per = max(1, 256 // rows)
    blocks = len(pieces) // per
    total, size = rows * len(pieces), rows * per
    return pl.pallas_call(
        functools.partial(mix_back_kernel, blocks, per),
        grid=(blocks,),
        in_specs=[pl.BlockSpec(memory_space=pl.ANY)] * len(pieces)
        + [
            pl.BlockSpec((size, wide), lambda i: (i, 0)),
            pl.BlockSpec((wide, width), lambda i: (0, 0)),
        ],
        out_specs=[
            pl.BlockSpec((size, wide), lambda i: (i, 0)),
            pl.BlockSpec((wide, width), lambda i: (0, 0)),
        ],
        out_shape=[
            jax.ShapeDtypeStruct((total, wide), BF16),
            jax.ShapeDtypeStruct((wide, width), BF16),
        ],
        scratch_shapes=[
            pltpu.VMEM((2, size, width), BF16),
            pltpu.VMEM((wide, width), F32),
            pltpu.SemaphoreType.DMA((2, per)),
        ],
        compiler_params=pltpu.CompilerParams(vmem_limit_bytes=VMEM_BYTES),
        cost_estimate=pl.CostEstimate(
            flops=4 * total * width * wide, bytes_accessed=4 * total * width, transcendentals=0
        ),
    )(*pieces, mixed, weight)


def load_heads(place, blocks, refs, tables, queries, keys, values):
    q_ref, k_ref, v_ref, scale_ref, gain_ref = refs
    cos_ref, sin_ref = tables
    rows = q_ref.shape[0] // blocks
    for a in range(blocks):
        at = pl.ds(pl.multiple_of(place[a] * rows, rows), rows)
        to = slice(a * rows, (a + 1) * rows)
        for i, (source, target) in enumerate(((q_ref, queries), (k_ref, keys))):
            normed = source[at, :] * scale_ref[to, i : i + 1] * gain_ref[i : i + 1, :]
            turned = pltpu.roll(normed, HEAD_DIM // 2, 1)
            target[to, :] = (normed * cos_ref[to, :] + turned * sin_ref[to, :]).astype(BF16)
        values[to, :] = v_ref[at, :]


def raised_scores(queries, keys, row_ref, col_ref, start, size, factor):
    stop = start + size
    scores = dot_nt(queries[start:stop, :], keys[:stop, :]) * factor
    query_at = lax.broadcasted_iota(jnp.int32, (size, stop), 0) + start
    key_at = lax.broadcasted_iota(jnp.int32, (size, stop), 1)
    allowed = (key_at <= query_at) & (row_ref[start:stop, :] == col_ref[:, :stop])
    scores = jnp.where(allowed, scores, MASKED)
    raised = jnp.exp(scores - jnp.max(scores, axis=-1, keepdims=True))
    return raised, jnp.sum(raised, axis=-1, keepdims=True)


def attend_kernel(
    blocks, size, place, q_ref, k_ref, v_ref, scale_ref, gain_ref, cos_ref, sin_ref, row_ref, col_ref,
    out_ref, queries, keys, values,
):
    total = q_ref.shape[0]
    rows = total // blocks
    refs, tables = (q_ref, k_ref, v_ref, scale_ref, gain_ref), (cos_ref, sin_ref)
    load_heads(place, blocks, refs, tables, queries, keys, values)
    factor = 1.0 / math.sqrt(HEAD_DIM)
    for start in range(0, total, size):
        raised, sums = raised_scores(queries, keys, row_ref, col_ref, start, size, factor)
        mixed = dot(raised.astype(BF16), values[: start + size, :]) / sums
        for i in range(size // rows):
            at = pl.multiple_of(place[start // rows + i] * rows, rows)
            out_ref[pl.ds(at, rows), :] = mixed[i * rows : (i + 1) * rows].astype(BF16)


def attend_back_kernel(
    blocks, size, place, q_ref, k_ref, v_ref, scale_ref, gain_ref, cos_ref, sin_ref, row_ref, col_ref,
    grad_ref, gq_ref, gk_ref, gv_ref, inner_ref, gain_grad_ref, queries, keys, values, key_sum, value_sum,
):
    total = q_ref.shape[0]
    rows = total // blocks
    refs, tables = (q_ref, k_ref, v_ref, scale_ref, gain_ref), (cos_ref, sin_ref)
    load_heads(place, blocks, refs, tables, queries, keys, values)
    factor = 1.0 / math.sqrt(HEAD_DIM)
    key_sum[...] = jnp.zeros_like(key_sum)
    value_sum[...] = jnp.zeros_like(value_sum)
    gain_rows = [jnp.zeros((1, HEAD_DIM), F32), jnp.zeros((1, HEAD_DIM), F32)]

    def finish(i, a, gradient, target):
        at = pl.ds(pl.multiple_of(place[a] * rows, rows), rows)
        to = slice(a * rows, (a + 1) * rows)
        turned = pltpu.roll(gradient, HEAD_DIM // 2, 1)
        normed = gradient * cos_ref[to, :] - turned * sin_ref[to, :]
        unit = (q_ref, k_ref)[i][at, :] * scale_ref[to, i : i + 1]
        scaled = normed * gain_ref[i : i + 1, :]
        target[at, :] = scaled
        inner_ref[to, i : i + 1] += jnp.sum(scaled * unit, axis=-1, keepdims=True)
        gain_rows[i] += jnp.sum(normed * unit, axis=0, keepdims=True)

    @pl.when(pl.program_id(0) == 0)
    def _():
        inner_ref[...] = jnp.zeros_like(inner_ref)

    for start in range(0, total, size):
        stop = start + size
        raised, sums = raised_scores(queries, keys, row_ref, col_ref, start, size, factor)
        probs = raised * (1.0 / sums)
        pieces = []
        for i in range(size // rows):
            at = pl.multiple_of(place[start // rows + i] * rows, rows)
            pieces.append(grad_ref[pl.ds(at, rows), :])
        grad_mixed = jnp.concatenate(pieces, axis=0) if len(pieces) > 1 else pieces[0]
        grad_weights = dot_nt(grad_mixed, values[:stop, :])
        delta = jnp.sum(probs * grad_weights, axis=-1, keepdims=True)
        grad_scores = (probs * (grad_weights - delta)).astype(BF16)
        grad_queries = dot(grad_scores, keys[:stop, :]) * factor
        key_sum[:stop, :] += dot_tn(grad_scores, queries[start:stop, :])
        value_sum[:stop, :] += dot_tn(probs.astype(BF16), grad_mixed)
        for i in range(size // rows):
            finish(0, start // rows + i, grad_queries[i * rows : (i + 1) * rows], gq_ref)
    for a in range(blocks):
        to = slice(a * rows, (a + 1) * rows)
        finish(1, a, key_sum[to, :] * factor, gk_ref)
        gv_ref[pl.ds(pl.multiple_of(place[a] * rows, rows), rows), :] = value_sum[to, :].astype(BF16)
    gain_grad_ref[0:1, :] = gain_rows[0]
    gain_grad_ref[1:2, :] = gain_rows[1]


def attention(place, pairs, values, scales, gains, tables, row_docs, col_docs, grad_mixed=None):
    total = pairs.shape[0]
    blocks = place.shape[0]
    heads = values.shape[1] // HEAD_DIM
    size = max(256, total // blocks)
    whole = lambda h: (0, 0)
    column = lambda h: (0, h)
    in_specs = [
        pl.BlockSpec(memory_space=pltpu.SMEM),
        pl.BlockSpec((total, HEAD_DIM), lambda h: (0, h)),
        pl.BlockSpec((total, HEAD_DIM), lambda h: (0, heads + h)),
        pl.BlockSpec((total, HEAD_DIM), column),
        pl.BlockSpec((total, 2), whole),
        pl.BlockSpec((2, HEAD_DIM), column),
        pl.BlockSpec((total, HEAD_DIM), whole),
        pl.BlockSpec((total, HEAD_DIM), whole),
        pl.BlockSpec((total, 1), whole),
        pl.BlockSpec((1, total), whole),
    ]
    operands = [place, pairs, pairs, values, scales, gains, *tables, row_docs, col_docs]
    held = [pltpu.VMEM((total, HEAD_DIM), BF16)] * 3
    params = pltpu.CompilerParams(vmem_limit_bytes=VMEM_BYTES)
    work = total * total * HEAD_DIM * heads
    if grad_mixed is None:
        return pl.pallas_call(
            functools.partial(attend_kernel, blocks, size),
            grid=(heads,),
            in_specs=in_specs,
            out_specs=pl.BlockSpec((total, HEAD_DIM), column),
            out_shape=jax.ShapeDtypeStruct((total, heads * HEAD_DIM), BF16),
            scratch_shapes=held,
            compiler_params=params,
            cost_estimate=pl.CostEstimate(
                flops=4 * work, bytes_accessed=pairs.size * 8, transcendentals=total * total
            ),
        )(*operands)
    return pl.pallas_call(
        functools.partial(attend_back_kernel, blocks, size),
        grid=(heads,),
        in_specs=in_specs + [pl.BlockSpec((total, HEAD_DIM), column)],
        out_specs=[pl.BlockSpec((total, HEAD_DIM), column)] * 3
        + [pl.BlockSpec((total, 2), whole), pl.BlockSpec((2, HEAD_DIM), column)],
        out_shape=[
            jax.ShapeDtypeStruct((total, heads * HEAD_DIM), F32),
            jax.ShapeDtypeStruct((total, heads * HEAD_DIM), F32),
            jax.ShapeDtypeStruct((total, heads * HEAD_DIM), BF16),
            jax.ShapeDtypeStruct((total, 2), F32),
            jax.ShapeDtypeStruct((2, heads * HEAD_DIM), F32),
        ],
        scratch_shapes=held + [pltpu.VMEM((total, HEAD_DIM), F32)] * 2,
        compiler_params=params,
        cost_estimate=pl.CostEstimate(
            flops=10 * work, bytes_accessed=pairs.size * 16, transcendentals=total * total
        ),
    )(*operands, grad_mixed)


def router_chances(inputs, router, experts):
    logits = dot_nt(inputs, router)
    column = lax.broadcasted_iota(jnp.int32, logits.shape, 1)
    logits = jnp.where(column < experts, logits, MASKED)
    raised = jnp.exp(logits - jnp.max(logits, axis=-1, keepdims=True))
    return raised / jnp.sum(raised, axis=-1, keepdims=True)


def acts_kernel(experts, blocks, per, at_ref, *refs):
    count = blocks * per
    pieces = refs[:count]
    (
        side_ref, router_ref, wg_ref, wu_ref, wd_ref,
        x_out, u_out, hidden_ref, gate_grad_ref, up_grad_ref, sums_ref, x_buffer, u_buffer, sems,
    ) = refs[count:]
    step = pl.program_id(0)
    sides = [side_ref.at[at_ref[2 + r]] for r in range(count)]

    def copies_of(block):
        slot = block % 2
        return piece_copies(pieces, block, per, x_buffer, slot, sems, 0) + piece_copies(
            sides, block, per, u_buffer, slot, sems, per
        )

    stream(blocks, copies_of)
    owned, width, _ = wg_ref.shape
    inputs, upstream = x_buffer[step % 2], u_buffer[step % 2, :, :width]
    chosen = u_buffer[step % 2, :, width:].astype(F32)
    x_out[...] = inputs
    u_out[...] = upstream
    gates = router_chances(inputs, router_ref[...], experts) * chosen
    gate_at = lax.broadcasted_iota(jnp.int32, gates.shape, 1)
    column = lax.broadcasted_iota(jnp.int32, sums_ref.shape, 1)
    sums = jnp.zeros(sums_ref.shape, F32)
    for e in range(owned):
        gate_act = dot(inputs, wg_ref[e])
        up_act = dot(inputs, wu_ref[e])
        grad_raw = dot_nt(upstream, wd_ref[e])
        expert = at_ref[0] * owned + e
        gate = jnp.sum(jnp.where(gate_at == expert, gates, 0.0), axis=-1, keepdims=True)
        sigma = jax.nn.sigmoid(gate_act)
        active = gate_act * sigma
        hidden = active * up_act
        grad_gate = jnp.sum(hidden * grad_raw, axis=-1, keepdims=True)
        high = grad_gate.astype(BF16).astype(F32)
        sums = jnp.where(column == expert, high, sums)
        sums = jnp.where(column == expert + experts, grad_gate - high, sums)
        grad_hidden = grad_raw * gate
        hidden_ref[e] = (hidden * gate).astype(BF16)
        gate_grad_ref[e] = (grad_hidden * up_act * sigma * (1.0 + gate_act * (1.0 - sigma))).astype(BF16)
        up_grad_ref[e] = (grad_hidden * active).astype(BF16)
    sums_ref[...] = sums.astype(BF16)


def run_acts(at, pieces, sides, router, w_gate, w_up, w_down, experts, parts):
    rows, width = pieces[0].shape
    total = rows * len(pieces)
    owned, _, hidden = w_gate.shape
    piece = hidden // parts
    per = max(1, 256 // rows)
    blocks, size = len(pieces) // per, rows * per
    extra = 128 * -(-2 * experts // 128)
    lanes = router.shape[0]
    token = lambda i, at: (i, 0)
    once = pl.Buffered(1)
    acts = jax.ShapeDtypeStruct((owned, total, piece), BF16)
    act_spec = pl.BlockSpec((owned, size, piece), lambda i, at: (0, i, 0))
    return pl.pallas_call(
        functools.partial(acts_kernel, experts, blocks, per),
        grid_spec=pltpu.PrefetchScalarGridSpec(
            num_scalar_prefetch=1,
            grid=(blocks,),
            in_specs=[pl.BlockSpec(memory_space=pl.ANY)] * (len(pieces) + 1)
            + [
                pl.BlockSpec((lanes, width), lambda i, at: (0, 0), pipeline_mode=once),
                pl.BlockSpec((owned, width, piece), lambda i, at: (0, 0, at[1]), pipeline_mode=once),
                pl.BlockSpec((owned, width, piece), lambda i, at: (0, 0, at[1]), pipeline_mode=once),
                pl.BlockSpec((owned, piece, width), lambda i, at: (0, at[1], 0), pipeline_mode=once),
            ],
            out_specs=[pl.BlockSpec((size, width), token)] * 2
            + [act_spec] * 3
            + [pl.BlockSpec((size, extra), token)],
            scratch_shapes=[
                pltpu.VMEM((2, size, width), BF16),
                pltpu.VMEM((2, size, width + lanes), BF16),
                pltpu.SemaphoreType.DMA((2, 2 * per)),
            ],
        ),
        out_shape=[
            jax.ShapeDtypeStruct((total, width), BF16),
            jax.ShapeDtypeStruct((total, width), BF16),
            acts,
            acts,
            acts,
            jax.ShapeDtypeStruct((total, extra), BF16),
        ],
        compiler_params=pltpu.CompilerParams(vmem_limit_bytes=VMEM_BYTES),
        cost_estimate=pl.CostEstimate(
            flops=6 * total * width * piece * owned,
            bytes_accessed=2 * (4 * total * width + 3 * owned * piece * (total + width)),
            transcendentals=total * piece * owned,
        ),
    )(at, *pieces, sides, router, w_gate, w_up, w_down)


def rows_back_kernel(blocks, per, at_ref, gate_ref, up_ref, sums_ref, wg_ref, wu_ref, near_ref, far_ref):
    back = dot_nt(gate_ref[0], wg_ref[0]) + dot_nt(up_ref[0], wu_ref[0])
    for e in range(1, wg_ref.shape[0]):
        back += dot_nt(gate_ref[e], wg_ref[e]) + dot_nt(up_ref[e], wu_ref[e])
    back = back.astype(BF16)
    step = pl.program_id(0)
    rows, width = near_ref.shape[2], back.shape[1]

    def store(out_ref):
        for i in range(per):
            at = at_ref[2 + step * per + i] // 2 % per
            part = slice(i * rows, (i + 1) * rows)
            out_ref[0, at, :, :width] = back[part]
            out_ref[0, at, :, width:] = sums_ref[part, :]

    pl.when(step < blocks // 2)(lambda: store(near_ref))
    pl.when(step >= blocks // 2)(lambda: store(far_ref))


def rows_out_kernel(sets, blocks, per, at_ref, *refs):
    *hidden_refs, wd_ref, out_ref = refs
    step = pl.program_id(0)
    rows = out_ref.shape[4]
    for k, hidden_ref in enumerate(hidden_refs):

        @pl.when(step // blocks == k)
        def _():
            out = dot(hidden_ref[0], wd_ref[0])
            for e in range(1, wd_ref.shape[0]):
                out += dot(hidden_ref[e], wd_ref[e])
            for i in range(per):
                at = at_ref[2 + (step - k * blocks) * per + i] // 2 % per
                out_ref[0, at, 0, 0] = out[i * rows : (i + 1) * rows].astype(BF16)


def run_out(at, hiddens, w_down, rows):
    owned, total, piece = hiddens[0].shape
    sets, width = len(hiddens), w_down.shape[2]
    seq_size = total // rows
    per = max(1, 256 // rows)
    size, blocks = rows * per, seq_size // per

    def hidden_at(k):
        return lambda i, at: (0, jnp.clip(i - k * blocks, 0, blocks - 1), 0)

    def out_at(i, at):
        first = at[2 + (i % blocks) * per]
        return (first // (2 * per), 0, first % 2, i // blocks, 0, 0)

    out = pl.pallas_call(
        functools.partial(rows_out_kernel, sets, blocks, per),
        grid_spec=pltpu.PrefetchScalarGridSpec(
            num_scalar_prefetch=1,
            grid=(sets * blocks,),
            in_specs=[pl.BlockSpec((owned, size, piece), hidden_at(k)) for k in range(sets)]
            + [
                pl.BlockSpec(
                    (owned, piece, width), lambda i, at: (0, at[1], 0), pipeline_mode=pl.Buffered(1)
                )
            ],
            out_specs=pl.BlockSpec((1, per, 1, 1, rows, width), out_at),
        ),
        out_shape=jax.ShapeDtypeStruct((seq_size // (2 * per), per, 2, sets, rows, width), BF16),
        compiler_params=pltpu.CompilerParams(vmem_limit_bytes=VMEM_BYTES),
        cost_estimate=pl.CostEstimate(
            flops=2 * sets * total * width * piece * owned,
            bytes_accessed=2 * sets * total * (width + owned * piece),
            transcendentals=0,
        ),
    )(at, *hiddens, w_down)
    return out.reshape(seq_size, sets, rows, width)


def run_back(at, gates, ups, sums, w_gate, w_up, rows):
    owned, total, piece = gates.shape
    chips = total // (2 * rows)
    per = max(1, 256 // rows)
    size, blocks = rows * per, total // (rows * per)
    middle = blocks // 2
    width, extra = w_gate.shape[1], sums.shape[1]
    act_spec = pl.BlockSpec((owned, size, piece), lambda i, at: (0, i, 0))
    weight_spec = pl.BlockSpec(
        (owned, width, piece), lambda i, at: (0, 0, at[1]), pipeline_mode=pl.Buffered(1)
    )

    def out_spec(first, last):
        return pl.BlockSpec(
            (1, per, rows, width + extra),
            lambda i, at: (at[2 + jnp.clip(i, first, last) * per] // (2 * per), 0, 0, 0),
        )

    out = jax.ShapeDtypeStruct((chips // per, per, rows, width + extra), BF16)
    results = pl.pallas_call(
        functools.partial(rows_back_kernel, blocks, per),
        grid_spec=pltpu.PrefetchScalarGridSpec(
            num_scalar_prefetch=1,
            grid=(blocks,),
            in_specs=[act_spec] * 2
            + [pl.BlockSpec((size, extra), lambda i, at: (i, 0))]
            + [weight_spec] * 2,
            out_specs=[out_spec(0, middle - 1), out_spec(middle, blocks - 1)],
        ),
        out_shape=[out, out],
        compiler_params=pltpu.CompilerParams(vmem_limit_bytes=VMEM_BYTES),
        cost_estimate=pl.CostEstimate(
            flops=4 * total * width * piece * owned,
            bytes_accessed=2 * (total * width + 2 * owned * piece * (total + width)),
            transcendentals=0,
        ),
    )(at, gates, ups, sums, w_gate, w_up)
    return [item.reshape(chips, rows, width + extra) for item in results]


def down_kernel(sets, at_ref, *refs):
    out_ref = refs[-1]
    for e in range(out_ref.shape[1]):
        term = dot_tn(refs[0][e], refs[sets][...])
        for i in range(1, sets):
            term += dot_tn(refs[i][e], refs[sets + i][...])
        out_ref[0, e] = term.astype(BF16)


def down_blocks(targets, hiddens, upstreams, group, width):
    owned, total, piece = hiddens[0].shape
    deep = piece // group
    sets, count = len(hiddens), targets.shape[0]
    wide = min(512, width)
    return pl.pallas_call(
        functools.partial(down_kernel, sets),
        grid_spec=pltpu.PrefetchScalarGridSpec(
            num_scalar_prefetch=1,
            grid=(count, width // wide),
            in_specs=[pl.BlockSpec((owned, total, deep), lambda g, j, at: (0, 0, at[g]))] * sets
            + [pl.BlockSpec((total, wide), lambda g, j, at: (0, j))] * sets,
            out_specs=pl.BlockSpec((1, owned, deep, wide), lambda g, j, at: (g, 0, 0, j)),
        ),
        out_shape=jax.ShapeDtypeStruct((count, owned, deep, width), BF16),
        compiler_params=pltpu.CompilerParams(vmem_limit_bytes=VMEM_BYTES),
        cost_estimate=pl.CostEstimate(
            flops=2 * sets * count * owned * total * deep * width,
            bytes_accessed=2 * sets * total * (width + owned * deep),
            transcendentals=0,
        ),
    )(targets, *hiddens, *upstreams)


def in_kernel(sets, at_ref, *refs):
    out_ref = refs[-1]
    for e in range(out_ref.shape[2]):
        term = dot_tn(refs[0][...], refs[sets][e])
        for i in range(1, sets):
            term += dot_tn(refs[i][...], refs[sets + i][e])
        out_ref[0, 0, e] = term.astype(BF16)


def in_blocks(targets, inputs, acts, group, parts):
    owned, total, piece = acts[0].shape
    width = inputs[0].shape[1]
    deep = width // (group * parts)
    sets, count = len(inputs), targets.shape[0]
    held = pl.BlockSpec((owned, total, piece), lambda g, p, at: (0, 0, 0), pipeline_mode=pl.Buffered(1))
    return pl.pallas_call(
        functools.partial(in_kernel, sets),
        grid_spec=pltpu.PrefetchScalarGridSpec(
            num_scalar_prefetch=1,
            grid=(count, parts),
            in_specs=[pl.BlockSpec((total, deep), lambda g, p, at: (0, p * group + at[g]))] * sets
            + [held] * sets,
            out_specs=pl.BlockSpec((1, 1, owned, deep, piece), lambda g, p, at: (g, p, 0, 0, 0)),
        ),
        out_shape=jax.ShapeDtypeStruct((count, parts, owned, deep, piece), BF16),
        compiler_params=pltpu.CompilerParams(vmem_limit_bytes=VMEM_BYTES),
        cost_estimate=pl.CostEstimate(
            flops=2 * sets * count * parts * owned * total * deep * piece,
            bytes_accessed=4 * sets * owned * total * piece,
            transcendentals=0,
        ),
    )(targets, *inputs, *acts)


def on_device(
    tokens,
    segments,
    expert_ids,
    w_query,
    w_key,
    w_value,
    w_out,
    w_router,
    attn_gain,
    query_gain,
    key_gain,
    ffn_gain,
    w_gate,
    w_up,
    w_down,
    out_grad,
):
    seq_size, batch_size = lax.axis_size("seq"), lax.axis_size("batch")
    seq_at, batch_at = lax.axis_index("seq"), lax.axis_index("batch")
    parts = 2 if batch_size % 2 == 0 else 1
    half = batch_size // parts
    part_at, in_group = batch_at // half, batch_at % half
    low_tokens = tokens[0]
    inputs = low_tokens.astype(F32)
    rows, width = inputs.shape
    total = rows * seq_size
    experts = w_router.shape[1]
    owned = w_gate.shape[0]
    wide = width // seq_size
    shard = w_query.shape[0]

    masks = masks_of(seq_size)
    order = seq_at ^ jnp.array(masks, jnp.int32)
    place = jnp.array([masks.index(m) for m in range(seq_size)], jnp.int32)[
        jnp.arange(seq_size, dtype=jnp.int32) ^ seq_at
    ]

    def reordered(values, by):
        return values.reshape(-1, seq_size, rows)[:, by].reshape(values.shape)

    masks = masks_of(seq_size)
    order = seq_at ^ jnp.array(masks, jnp.int32)
    place = jnp.array([masks.index(m) for m in range(seq_size)], jnp.int32)[
        jnp.arange(seq_size, dtype=jnp.int32) ^ seq_at
    ]
    here = jnp.concatenate([jnp.stack([seq_at, batch_at]).astype(jnp.int32), order])

    def reordered(values, by):
        return values.reshape(-1, seq_size, rows)[:, by].reshape(values.shape)

    masks = masks_of(seq_size)
    order = seq_at ^ jnp.array(masks, jnp.int32)
    place = jnp.array([masks.index(m) for m in range(seq_size)], jnp.int32)[
        jnp.arange(seq_size, dtype=jnp.int32) ^ seq_at
    ]
    here = jnp.concatenate([jnp.stack([seq_at, batch_at]).astype(jnp.int32), order])
    at = jnp.concatenate([jnp.stack([seq_at, part_at]).astype(jnp.int32), order])

    def reordered(values, by):
        return values.reshape(-1, seq_size, rows)[:, by].reshape(values.shape)

    near_tokens = gather_near(low_tokens)

    def cut_of(*weights):
        return jnp.concatenate(
            [w.reshape(shard, seq_size, wide).transpose(1, 0, 2) for w in weights], axis=2
        )

    def exchange(blocks):
        return lax.all_to_all(blocks, "seq", split_axis=0, concat_axis=0, tiled=True)

    small = jnp.concatenate(
        [jnp.stack([attn_gain, query_gain, key_gain, ffn_gain]), w_router.T], axis=0
    )
    items, fit = experts + 4, 2 * wide // shard
    deep = 8 * -(-items // (8 * fit))
    small = jnp.pad(small, ((0, deep * fit - items), (0, 0))).reshape(1, deep, 2 * wide)
    small = jnp.broadcast_to(small, (seq_size, deep, 2 * wide))
    pair_cut = exchange(jnp.concatenate([cut_of(w_query, w_key), small], axis=1))

    ids = expert_ids[0]
    lanes = 128 * -(-experts // 128)
    choices = jnp.any(ids[:, :, None] == jnp.arange(lanes, dtype=jnp.int32), axis=1)
    side = jnp.concatenate([out_grad[0], choices.astype(BF16)], axis=1)
    partner = [hop(side, "batch", half)] if parts == 2 else []
    token_pieces = near_tokens + [hop(after(piece, pair_cut, *partner), "seq", 1) for piece in near_tokens]
    value_cut = exchange(after(cut_of(w_value), pair_cut))
    pair_pieces = gather_batch(after(pair_cut, *token_pieces), value_cut)
    value_pieces = gather_batch(after(value_cut, *pair_pieces[2:3]), *pair_pieces)
    out_pieces = gather_batch(after(w_out, *pair_pieces), *value_pieces)
    small = jnp.stack([item[:, shard:] for item in pair_pieces])
    small = small.reshape(batch_size, seq_size, deep * fit, shard)[
        jnp.arange(batch_size, dtype=jnp.int32) ^ batch_at
    ]
    small = small.transpose(2, 1, 0, 3).reshape(deep * fit, width)
    gains = small[:4].astype(F32)
    attn_norm_gain, ffn_norm_gain = gains[0], gains[3]
    head_gains = lax.dynamic_slice_in_dim(gains[1:3], seq_at * wide, wide, 1)
    router = jnp.pad(small[4:items], ((0, lanes - experts), (0, 0)))
    w_mix = jnp.zeros((batch_size, shard, width), BF16)
    for t, piece in enumerate(out_pieces):
        w_mix = put(w_mix, piece[None], (batch_at ^ t, 0, 0))
    w_mix = w_mix.reshape(wide, width)

    sides = [
        lax.all_gather(after(item, *pins), "seq", axis=0)
        for item, pins in zip([side, *partner], ([value_cut, *pair_pieces[1:3]], pair_pieces))
    ]
    counts = jnp.sum(sides[0][:, :, width:].astype(F32), axis=(0, 1)).astype(jnp.int32)
    counts_here = lax.dynamic_slice_in_dim(counts, seq_at * owned, owned, 0)

    normed, pairs, squares, pair_weights = project_pairs(
        here, token_pieces, pair_pieces, shard, attn_norm_gain[None]
    )
    values, value_weights = project_values(here, normed, value_pieces)
    pair_weights, value_weights = (w.reshape(width, -1) for w in (pair_weights, value_weights))

    def sum_seq(values):
        return jnp.sum(lax.all_gather(values, "seq", axis=0), axis=0)

    scales = lax.rsqrt(sum_seq(squares) / width + EPSILON)
    rates = jnp.power(
        ROTARY_BASE, -jnp.arange(HEAD_DIM // 2, dtype=F32) * (2.0 / HEAD_DIM)
    )
    angles = jnp.arange(total, dtype=F32)[:, None] * rates[None, :]
    cosine, sine = jnp.cos(angles), jnp.sin(angles)
    tables = (
        jnp.concatenate([cosine, cosine], axis=1),
        jnp.concatenate([-sine, sine], axis=1),
    )
    attend = functools.partial(
        attention,
        place,
        pairs,
        values,
        scales.T,
        head_gains,
        tables,
        segments[0][:, None],
        segments[0][None, :],
    )
    mixed_low = after(attend(), sides[0])
    middle = total // 2
    far = dot(mixed_low[middle:], w_mix).astype(BF16)
    residual = inputs + scatter_seq(dot(mixed_low[:middle], w_mix).astype(BF16), far)[0]
    ffn_scale = norm_scale(residual)
    ffn_unit = residual * ffn_scale
    ffn_in = (ffn_unit * ffn_norm_gain).astype(BF16)

    def acts_of(k, pieces):
        return run_acts(at, pieces, sides[k], router, w_gate, w_up, w_down, experts, parts)

    ffn_pieces = gather_seq(ffn_in)
    results = [acts_of(0, ffn_pieces)]
    if parts == 2:
        partner = hop(ffn_in, "batch", half)
        near = gather_near(after(partner, *ffn_pieces))
        near = [after(piece, results[0][0]) for piece in near]
        results.append(acts_of(1, near + [hop(piece, "seq", 1) for piece in near]))
    all_ffn, upstreams, hiddens, gate_acts, up_acts, sums = zip(*results)
    own = in_group[None].astype(jnp.int32)
    others = jnp.stack([in_group ^ t for t in range(1, half)]).astype(jnp.int32) if half > 1 else None
    down = functools.partial(down_blocks, hiddens=hiddens, upstreams=upstreams, group=half, width=width)
    into = functools.partial(in_blocks, inputs=all_ffn, group=half, parts=parts)

    def send_group(theirs):
        return [hop(theirs[t - 1], "batch", t) for t in range(1, half)]

    def gather_group(theirs):
        groups = [list(range(first, first + half)) for first in range(0, batch_size, half)]
        blocks = lax.all_gather(theirs, "batch", axis=0, axis_index_groups=groups)
        return [take_block(blocks, in_group ^ t)[t - 1] for t in range(1, half)]

    def group_sum(mine, moved):
        total = mine[0].astype(F32)
        for item in moved:
            total = total + item.astype(F32)
        return total

    def swap_part(summed):
        return hop(take_block(summed, 1 - part_at).astype(BF16), "batch", half)

    gate_moved = up_moved = down_moved = ()
    at_back = at
    if half > 1:
        gate_theirs = into(others, acts=gate_acts)
        gate_moved = send_group(gate_theirs)
        at_back = after(at, gate_theirs)
    backs, sent = [], []
    for k in reversed(range(parts)):
        near, far = run_back(at_back, gate_acts[k], up_acts[k], sums[k], w_gate, w_up, rows)
        if half > 1 and not sent:
            up_theirs = into(after(others, near), acts=up_acts)
            near = after(near, up_theirs)
        if k == 0:
            mix = run_out(after(at, near), hiddens, w_down, rows)
            far = after(far, mix, *backs, *gate_moved)
        summed, low = scatter_chips(near, far)
        backs.insert(0, summed)
        sent.append(low)
        at_back = after(at, low)
    gate_mine = last = into(after(own, *sent), acts=gate_acts)
    other = hop(backs[1].astype(BF16), "batch", half) if parts == 2 else gate_mine
    if half > 1:
        last = down_theirs = down(after(others, gate_mine))
    gate_sum = group_sum(gate_mine, gate_moved)
    up_mine = into(after(own, last, other), acts=up_acts)
    gate_other = swap_part(gate_sum) if parts == 2 else gate_sum
    if half > 1:
        up_moved = gather_group(up_theirs)
        down_moved = gather_group(down_theirs)
    back = after(backs[0], up_mine, gate_sum)
    if parts == 2:
        back = back + other.astype(F32)

    grad_ffn_in = back[:, :width]
    grad_chances = choices[:, :experts] * (
        back[:, width : width + experts] + back[:, width + experts : width + 2 * experts]
    )
    chances = router_chances(ffn_in, router, experts)[:, :experts]
    grad_logits = (
        chances * (grad_chances - jnp.sum(chances * grad_chances, axis=-1, keepdims=True))
    ).astype(BF16)
    grad_ffn_in = grad_ffn_in + dot(grad_logits, router[:experts])
    scaled = grad_ffn_in * ffn_norm_gain
    inner = jnp.mean(scaled * ffn_unit, axis=-1, keepdims=True)
    grad_residual = out_grad[0].astype(F32) + ffn_scale * (scaled - ffn_unit * inner)
    grad_attn = grad_residual.astype(BF16)

    grad_near = gather_near(grad_attn)
    arrived = grad_near[1:]
    up_sum = group_sum(up_mine, [after(item, grad_attn) for item in up_moved])
    grad_near[0] = after(grad_attn, up_sum, *arrived)
    grad_pieces = grad_near + [hop(piece, "seq", 1) for piece in grad_near]
    up_other = swap_part(up_sum) if parts == 2 else up_sum
    grad_mixed, out_term = mix_back(grad_pieces, after(mixed_low, gate_other), w_mix)
    mix = lax.psum_scatter(after(mix, grad_mixed), "seq", scatter_dimension=0)
    scaled_q, scaled_k, value_low, inner, gain_terms = attend(grad_mixed=grad_mixed)

    def term_of(values):
        return dot_tn(normed, values).astype(BF16).reshape(seq_size * batch_size, shard, -1)

    value_term = term_of(value_low)
    inner = reordered(sum_seq(after(inner.T, value_term)), order).T / width
    rel_scales = reordered(scales, order).T
    lows = []
    for i, item in enumerate((scaled_q, scaled_k)):
        scale = rel_scales[:, i : i + 1]
        unit = pairs[:, i * wide : (i + 1) * wide] * scale
        lows.append((scale * (item - unit * inner[:, i : i + 1])).astype(BF16))
    pair_low = jnp.concatenate(lows, axis=1)
    pair_term = term_of(pair_low)
    late_low = after(pair_low, pair_term)

    def rows_of(at):
        return (dot_nt(late_low[at], pair_weights) + dot_nt(value_low[at], value_weights)).astype(BF16)

    far = rows_of(slice(middle, total))
    grad_normed, low = scatter_seq(rows_of(slice(0, middle)), far)
    mix_other = hop(after(mix[1], value_low), "batch", half) if parts == 2 else mix
    grad_normed = after(grad_normed, mix_other)
    down_mine = down(after(own, *low))

    def head_sums(term, extra):
        term = jnp.concatenate([term, *extra], axis=1)
        term = lax.all_to_all(term, ("seq", "batch"), split_axis=0, concat_axis=0, tiled=True)
        term = after(term, grad_normed)
        total = jnp.sum(term[:, :shard].reshape(seq_size, batch_size, shard, -1).astype(F32), axis=1)
        return total, jnp.sum(term[:, shard:].astype(F32), axis=0)

    def two_parts(values):
        high = values.astype(BF16)
        return jnp.concatenate([high, (values - high.astype(F32)).astype(BF16)], axis=0)

    def in_rows(items):
        fit = wide // shard
        deep = 8 * -(-items.shape[0] // (8 * fit))
        items = jnp.pad(items, ((0, deep * fit - items.shape[0]), (0, 0), (0, 0), (0, 0)))
        return items.transpose(1, 2, 0, 3).reshape(seq_size * batch_size, deep, wide)

    router_term = jnp.concatenate(
        [dot_tn(grad_logits, ffn_in), jnp.sum(grad_ffn_in * ffn_unit, axis=0)[None]], axis=0
    )
    router_items = two_parts(router_term).reshape(-1, seq_size, batch_size, shard)
    gain_items = two_parts(gain_terms).reshape(4, 1, batch_size, shard)
    mine_only = (jnp.arange(seq_size) == seq_at)[None, :, None, None]
    gain_items = jnp.where(mine_only, gain_items, jnp.zeros_like(gain_items))
    items = in_rows(jnp.concatenate([gain_items, router_items], axis=0))
    value_sums, items = head_sums(value_term, [items])
    items = items.reshape(-1, shard)
    gain_sum = items[0:2] + items[2:4]
    router_sum = items[4 : 5 + experts] + items[5 + experts : 6 + 2 * experts]
    router_grad, ffn_gain_grad = router_sum[:experts].T, router_sum[experts]
    pair_sums, _ = head_sums(pair_term, [])
    query_grad, key_grad, value_grad = (
        item.transpose(1, 0, 2).reshape(shard, width)
        for item in (pair_sums[:, :, :wide], pair_sums[:, :, wide:], value_sums)
    )

    def spread(summed, other):
        if parts == 1:
            return summed[0]
        keep, other = take_block(summed, part_at), other.astype(F32)
        return jnp.where(
            part_at == 0,
            jnp.concatenate([keep, other], axis=-1),
            jnp.concatenate([other, keep], axis=-1),
        )

    down_grad = group_sum(down_mine, [after(item, pair_term) for item in down_moved])
    gate_grad = spread(gate_sum, after(gate_other, pair_term))
    up_grad = spread(up_sum, after(up_other, grad_normed))
    out_proj_grad = scatter_batch(
        out_term.reshape(batch_size, shard, width), batch_at, BF16, far, grad_normed
    )

    mine = mix[0].astype(F32)
    if parts == 2:
        mine = mine + mix_other.astype(F32)
    block_out = (residual + mine).astype(BF16)

    attn_scale = norm_scale(inputs)
    attn_unit = inputs * attn_scale
    scaled = grad_normed * attn_norm_gain
    inner = jnp.mean(scaled * attn_unit, axis=-1, keepdims=True)
    grad_input = grad_residual + attn_scale * (scaled - attn_unit * inner)
    attn_gain_grad = (
        jnp.sum(
            query_grad * w_query.astype(F32)
            + key_grad * w_key.astype(F32)
            + value_grad * w_value.astype(F32),
            axis=1,
        )
        / attn_gain.astype(F32)
    )
    return (
        block_out[None],
        grad_input[None],
        query_grad,
        key_grad,
        value_grad,
        out_proj_grad,
        router_grad,
        attn_gain_grad,
        gain_sum[0],
        gain_sum[1],
        ffn_gain_grad,
        gate_grad,
        up_grad,
        down_grad,
        counts_here[None],
    )


def solution(mesh):
    in_specs = (
        P("batch", "seq", None),
        P("batch", None),
        P("batch", "seq", None),
        P(("seq", "batch"), None),
        P(("seq", "batch"), None),
        P(("seq", "batch"), None),
        P(("seq", "batch"), None),
        P(("seq", "batch"), None),
        P(("seq", "batch")),
        P(("seq", "batch")),
        P(("seq", "batch")),
        P(("seq", "batch")),
        P("seq", None, None),
        P("seq", None, None),
        P("seq", None, None),
        P("batch", "seq", None),
    )
    out_specs = (
        P("batch", "seq", None),
        P("batch", "seq", None),
        P(("seq", "batch"), None),
        P(("seq", "batch"), None),
        P(("seq", "batch"), None),
        P(("seq", "batch"), None),
        P(("seq", "batch"), None),
        P(("seq", "batch")),
        P(("seq", "batch")),
        P(("seq", "batch")),
        P(("seq", "batch")),
        P("seq", "batch", None),
        P("seq", "batch", None),
        P("seq", "batch", None),
        P("batch", "seq"),
    )
    return jax.shard_map(
        on_device, mesh=mesh, in_specs=in_specs, out_specs=out_specs, check_vma=False
    )
```

```python
import functools
import math

import jax
import jax.numpy as jnp
from jax import lax
from jax.experimental import pallas as pl
from jax.experimental.pallas import tpu as pltpu
from jax.sharding import PartitionSpec as P

HEAD_DIM = 128
EPSILON = 1e-05
ROTARY_BASE = 10000.0
MASKED = -1e30
BF16 = jnp.bfloat16
F32 = jnp.float32
VMEM_BYTES = 60 * 1024 * 1024


def dot(left, right):
    return lax.dot_general(left, right, (((1,), (0,)), ((), ())), preferred_element_type=F32)


def dot_nt(left, right):
    return lax.dot_general(left, right, (((1,), (1,)), ((), ())), preferred_element_type=F32)


def dot_tn(left, right):
    return lax.dot_general(left, right, (((0,), (0,)), ((), ())), preferred_element_type=F32)


def norm_scale(values):
    return lax.rsqrt(jnp.mean(values * values, axis=-1, keepdims=True) + EPSILON)


def hop(values, axis, mask):
    size = lax.axis_size(axis)
    return lax.ppermute(values, axis, [(i, i ^ mask) for i in range(size)])


def take_block(values, index, axis=0):
    return lax.dynamic_index_in_dim(values, index, axis, keepdims=False)


def put(buffer, values, starts):
    return lax.dynamic_update_slice(buffer, values, starts)


def after(values, *earlier):
    return lax.optimization_barrier((values, *earlier))[0]


def masks_of(size):
    return [2 * m for m in range(size // 2)] + [2 * m + 1 for m in range(size // 2)]


def gather_near(values):
    return [values] + [hop(values, "seq", 2 * m) for m in range(1, lax.axis_size("seq") // 2)]


def gather_seq(values):
    near = gather_near(values)
    near[0] = after(values, *near[1:2])
    return near + [hop(piece, "seq", 1) for piece in near]


def scatter_seq(near, far):
    chips = lax.axis_size("seq") // 2
    rows = near.shape[0] // chips
    moved = hop(far, "seq", 1)

    def both(m):
        at = slice(m * rows, (m + 1) * rows)
        return near[at].astype(F32) + moved[at].astype(F32)

    sent = [both(m).astype(BF16) for m in range(1, chips)]
    total = both(0)
    for m in range(1, chips):
        total = total + hop(sent[m - 1], "seq", 2 * m).astype(F32)
    return total, sent


def scatter_chips(near, far):
    size = lax.axis_size("seq")
    sent = (near.astype(F32) + hop(far, "seq", 1).astype(F32)).astype(BF16)
    groups = [list(range(core, size, 2)) for core in range(2)]
    moved = lax.all_to_all(
        sent, "seq", split_axis=0, concat_axis=0, axis_index_groups=groups, tiled=True
    )
    return jnp.sum(moved.astype(F32), axis=0), sent


def gather_batch(values, *pins):
    pieces = [values]
    for t in range(1, lax.axis_size("batch")):
        if t % 2 and t > 1:
            pieces.append(hop(after(pieces[t - 1], *pieces[1 : t - 1], *pins), "batch", 1))
        else:
            pieces.append(hop(values, "batch", t))
    return pieces


def scatter_batch(blocks, me, kind, *pins):
    size = blocks.shape[0]
    if size == 1:
        return blocks[0].astype(F32)
    theirs = jnp.stack([take_block(blocks, me ^ t ^ 1) for t in range(0, size, 2)])
    moved = after(hop(theirs, "batch", 1), pins[0])
    total = take_block(blocks, me).astype(F32) + moved[0].astype(F32)
    for i in range(1, size // 2):
        pair = take_block(blocks, me ^ (2 * i)).astype(F32) + moved[i].astype(F32)
        total = total + after(hop(pair.astype(kind), "batch", 2 * i), pins[1]).astype(F32)
    return total


def piece_copies(refs, block, per, buffer, slot, sems, first):
    rows = buffer.shape[1] // per
    return [
        pltpu.make_async_copy(
            refs[block * per + i],
            buffer.at[slot, pl.ds(i * rows, rows), :],
            sems.at[slot, first + i],
        )
        for i in range(per)
    ]


def stream(blocks, copies_of):
    step = pl.program_id(0)
    for block in range(blocks):

        @pl.when(step == block)
        def _():
            if block == 0:
                for copy in copies_of(0):
                    copy.start()
            if block + 1 < blocks:
                for copy in copies_of(block + 1):
                    copy.start()
            for copy in copies_of(block):
                copy.wait()


def weight_copies(at_ref, pieces, target, sems):
    shard = target.shape[2]
    return [
        pltpu.make_async_copy(piece.at[:, pl.ds(0, shard)], target.at[:, at_ref[1] ^ t], sems.at[t])
        for t, piece in enumerate(pieces)
    ]


def project_pairs_kernel(blocks, per, at_ref, *refs):
    count = blocks * per
    pieces, w_pieces = refs[:count], refs[count : -8]
    gain_ref, normed_ref, pair_ref, square_ref, weight_ref, buffer, sems, w_sems = refs[-8:]
    step = pl.program_id(0)

    @pl.when(step == 0)
    def _():
        for copy in weight_copies(at_ref, w_pieces, weight_ref, w_sems):
            copy.start()

    stream(blocks, lambda block: piece_copies(pieces, block, per, buffer, block % 2, sems, 0))

    @pl.when(step == 0)
    def _():
        for copy in weight_copies(at_ref, w_pieces, weight_ref, w_sems):
            copy.wait()

    values = buffer[step % 2].astype(F32)
    normed = (values * norm_scale(values) * gain_ref[...]).astype(BF16)
    normed_ref[...] = normed
    width = normed.shape[1]
    pair = dot(normed, weight_ref[...].reshape(width, -1))
    pair_ref[...] = pair
    wide = pair.shape[1] // 2
    squared = pair * pair
    high = squared.astype(BF16)
    low = (squared - high.astype(F32)).astype(BF16)
    lane = lax.broadcasted_iota(jnp.int32, (8, 2 * wide), 1)
    line = lax.broadcasted_iota(jnp.int32, (8, 2 * wide), 0)
    pick = (lane // wide == line).astype(BF16)
    sums = (dot_nt(pick, high) + dot_nt(pick, low))[:2]
    rows = normed.shape[0] // per
    for i in range(per):
        at = pl.multiple_of(at_ref[2 + step * per + i] * rows, rows)
        square_ref[:, pl.ds(at, rows)] = sums[:, i * rows : (i + 1) * rows]


def project_pairs(here, pieces, w_pieces, shard, gain):
    rows, width = pieces[0].shape
    seq_size, _, columns = w_pieces[0].shape
    batch_size = len(w_pieces)
    per = max(1, 256 // rows)
    blocks = len(pieces) // per
    total, size = rows * len(pieces), rows * per
    return pl.pallas_call(
        functools.partial(project_pairs_kernel, blocks, per),
        grid_spec=pltpu.PrefetchScalarGridSpec(
            num_scalar_prefetch=1,
            grid=(blocks,),
            in_specs=[pl.BlockSpec(memory_space=pl.ANY)] * (len(pieces) + batch_size)
            + [pl.BlockSpec((1, width), lambda i, at: (0, 0))],
            out_specs=[
                pl.BlockSpec((size, width), lambda i, at: (i, 0)),
                pl.BlockSpec((size, columns), lambda i, at: (i, 0)),
                pl.BlockSpec((2, total), lambda i, at: (0, 0)),
                pl.BlockSpec((seq_size, batch_size, shard, columns), lambda i, at: (0, 0, 0, 0)),
            ],
            scratch_shapes=[
                pltpu.VMEM((2, size, width), BF16),
                pltpu.SemaphoreType.DMA((2, per)),
                pltpu.SemaphoreType.DMA((batch_size,)),
            ],
        ),
        out_shape=[
            jax.ShapeDtypeStruct((total, width), BF16),
            jax.ShapeDtypeStruct((total, columns), F32),
            jax.ShapeDtypeStruct((2, total), F32),
            jax.ShapeDtypeStruct((seq_size, batch_size, shard, columns), BF16),
        ],
        compiler_params=pltpu.CompilerParams(vmem_limit_bytes=VMEM_BYTES),
        cost_estimate=pl.CostEstimate(
            flops=2 * total * width * columns, bytes_accessed=8 * total * width, transcendentals=0
        ),
    )(here, *pieces, *w_pieces, gain)


def project_values_kernel(at_ref, normed_ref, *refs):
    *w_pieces, value_ref, weight_ref, w_sems = refs

    @pl.when(pl.program_id(0) == 0)
    def _():
        copies = weight_copies(at_ref, w_pieces, weight_ref, w_sems)
        for copy in copies:
            copy.start()
        for copy in copies:
            copy.wait()

    width = normed_ref.shape[1]
    value_ref[...] = dot(normed_ref[...], weight_ref[...].reshape(width, -1)).astype(BF16)


def project_values(here, normed, w_pieces):
    total, width = normed.shape
    seq_size, shard, columns = w_pieces[0].shape
    batch_size = len(w_pieces)
    size = min(512, total)
    return pl.pallas_call(
        project_values_kernel,
        grid_spec=pltpu.PrefetchScalarGridSpec(
            num_scalar_prefetch=1,
            grid=(total // size,),
            in_specs=[pl.BlockSpec((size, width), lambda i, at: (i, 0))]
            + [pl.BlockSpec(memory_space=pl.ANY)] * batch_size,
            out_specs=[
                pl.BlockSpec((size, columns), lambda i, at: (i, 0)),
                pl.BlockSpec((seq_size, batch_size, shard, columns), lambda i, at: (0, 0, 0, 0)),
            ],
            scratch_shapes=[pltpu.SemaphoreType.DMA((batch_size,))],
        ),
        out_shape=[
            jax.ShapeDtypeStruct((total, columns), BF16),
            jax.ShapeDtypeStruct((seq_size, batch_size, shard, columns), BF16),
        ],
        compiler_params=pltpu.CompilerParams(vmem_limit_bytes=VMEM_BYTES),
        cost_estimate=pl.CostEstimate(
            flops=2 * total * width * columns, bytes_accessed=2 * total * width, transcendentals=0
        ),
    )(here, normed, *w_pieces)


def mix_back_kernel(blocks, per, *refs):
    pieces = refs[: blocks * per]
    mixed_ref, weight_ref, back_ref, grad_ref, buffer, total, sems = refs[blocks * per :]
    step = pl.program_id(0)
    stream(blocks, lambda block: piece_copies(pieces, block, per, buffer, block % 2, sems, 0))
    gradient = buffer[step % 2]
    back_ref[...] = dot_nt(gradient, weight_ref[...]).astype(BF16)
    term = dot_tn(mixed_ref[...], gradient)

    @pl.when(step == 0)
    def _():
        total[...] = term

    @pl.when(step > 0)
    def _():
        total[...] += term

    @pl.when(step == blocks - 1)
    def _():
        grad_ref[...] = total[...].astype(BF16)


def mix_back(pieces, mixed, weight):
    rows, width = pieces[0].shape
    wide = weight.shape[0]
    per = max(1, 256 // rows)
    blocks = len(pieces) // per
    total, size = rows * len(pieces), rows * per
    return pl.pallas_call(
        functools.partial(mix_back_kernel, blocks, per),
        grid=(blocks,),
        in_specs=[pl.BlockSpec(memory_space=pl.ANY)] * len(pieces)
        + [
            pl.BlockSpec((size, wide), lambda i: (i, 0)),
            pl.BlockSpec((wide, width), lambda i: (0, 0)),
        ],
        out_specs=[
            pl.BlockSpec((size, wide), lambda i: (i, 0)),
            pl.BlockSpec((wide, width), lambda i: (0, 0)),
        ],
        out_shape=[
            jax.ShapeDtypeStruct((total, wide), BF16),
            jax.ShapeDtypeStruct((wide, width), BF16),
        ],
        scratch_shapes=[
            pltpu.VMEM((2, size, width), BF16),
            pltpu.VMEM((wide, width), F32),
            pltpu.SemaphoreType.DMA((2, per)),
        ],
        compiler_params=pltpu.CompilerParams(vmem_limit_bytes=VMEM_BYTES),
        cost_estimate=pl.CostEstimate(
            flops=4 * total * width * wide, bytes_accessed=4 * total * width, transcendentals=0
        ),
    )(*pieces, mixed, weight)


def load_heads(place, blocks, refs, tables, queries, keys, values):
    q_ref, k_ref, v_ref, scale_ref, gain_ref = refs
    cos_ref, sin_ref = tables
    rows = q_ref.shape[0] // blocks
    for a in range(blocks):
        at = pl.ds(pl.multiple_of(place[a] * rows, rows), rows)
        to = slice(a * rows, (a + 1) * rows)
        for i, (source, target) in enumerate(((q_ref, queries), (k_ref, keys))):
            normed = source[at, :] * scale_ref[to, i : i + 1] * gain_ref[i : i + 1, :]
            turned = pltpu.roll(normed, HEAD_DIM // 2, 1)
            target[to, :] = (normed * cos_ref[to, :] + turned * sin_ref[to, :]).astype(BF16)
        values[to, :] = v_ref[at, :]


def raised_scores(queries, keys, row_ref, col_ref, start, size, factor):
    stop = start + size
    scores = dot_nt(queries[start:stop, :], keys[:stop, :]) * factor
    query_at = lax.broadcasted_iota(jnp.int32, (size, stop), 0) + start
    key_at = lax.broadcasted_iota(jnp.int32, (size, stop), 1)
    allowed = (key_at <= query_at) & (row_ref[start:stop, :] == col_ref[:, :stop])
    scores = jnp.where(allowed, scores, MASKED)
    raised = jnp.exp(scores - jnp.max(scores, axis=-1, keepdims=True))
    return raised, jnp.sum(raised, axis=-1, keepdims=True)


def attend_kernel(
    blocks, size, place, q_ref, k_ref, v_ref, scale_ref, gain_ref, cos_ref, sin_ref, row_ref, col_ref,
    out_ref, queries, keys, values,
):
    total = q_ref.shape[0]
    rows = total // blocks
    refs, tables = (q_ref, k_ref, v_ref, scale_ref, gain_ref), (cos_ref, sin_ref)
    load_heads(place, blocks, refs, tables, queries, keys, values)
    factor = 1.0 / math.sqrt(HEAD_DIM)
    for start in range(0, total, size):
        raised, sums = raised_scores(queries, keys, row_ref, col_ref, start, size, factor)
        mixed = dot(raised.astype(BF16), values[: start + size, :]) / sums
        for i in range(size // rows):
            at = pl.multiple_of(place[start // rows + i] * rows, rows)
            out_ref[pl.ds(at, rows), :] = mixed[i * rows : (i + 1) * rows].astype(BF16)


def attend_back_kernel(
    blocks, size, place, q_ref, k_ref, v_ref, scale_ref, gain_ref, cos_ref, sin_ref, row_ref, col_ref,
    grad_ref, gq_ref, gk_ref, gv_ref, inner_ref, gain_grad_ref, queries, keys, values, key_sum, value_sum,
):
    total = q_ref.shape[0]
    rows = total // blocks
    refs, tables = (q_ref, k_ref, v_ref, scale_ref, gain_ref), (cos_ref, sin_ref)
    load_heads(place, blocks, refs, tables, queries, keys, values)
    factor = 1.0 / math.sqrt(HEAD_DIM)
    key_sum[...] = jnp.zeros_like(key_sum)
    value_sum[...] = jnp.zeros_like(value_sum)
    gain_rows = [jnp.zeros((1, HEAD_DIM), F32), jnp.zeros((1, HEAD_DIM), F32)]

    def finish(i, a, gradient, target):
        at = pl.ds(pl.multiple_of(place[a] * rows, rows), rows)
        to = slice(a * rows, (a + 1) * rows)
        turned = pltpu.roll(gradient, HEAD_DIM // 2, 1)
        normed = gradient * cos_ref[to, :] - turned * sin_ref[to, :]
        unit = (q_ref, k_ref)[i][at, :] * scale_ref[to, i : i + 1]
        scaled = normed * gain_ref[i : i + 1, :]
        target[at, :] = scaled
        inner_ref[to, i : i + 1] += jnp.sum(scaled * unit, axis=-1, keepdims=True)
        gain_rows[i] += jnp.sum(normed * unit, axis=0, keepdims=True)

    @pl.when(pl.program_id(0) == 0)
    def _():
        inner_ref[...] = jnp.zeros_like(inner_ref)

    for start in range(0, total, size):
        stop = start + size
        raised, sums = raised_scores(queries, keys, row_ref, col_ref, start, size, factor)
        probs = raised * (1.0 / sums)
        pieces = []
        for i in range(size // rows):
            at = pl.multiple_of(place[start // rows + i] * rows, rows)
            pieces.append(grad_ref[pl.ds(at, rows), :])
        grad_mixed = jnp.concatenate(pieces, axis=0) if len(pieces) > 1 else pieces[0]
        grad_weights = dot_nt(grad_mixed, values[:stop, :])
        delta = jnp.sum(probs * grad_weights, axis=-1, keepdims=True)
        grad_scores = (probs * (grad_weights - delta)).astype(BF16)
        grad_queries = dot(grad_scores, keys[:stop, :]) * factor
        key_sum[:stop, :] += dot_tn(grad_scores, queries[start:stop, :])
        value_sum[:stop, :] += dot_tn(probs.astype(BF16), grad_mixed)
        for i in range(size // rows):
            finish(0, start // rows + i, grad_queries[i * rows : (i + 1) * rows], gq_ref)
    for a in range(blocks):
        to = slice(a * rows, (a + 1) * rows)
        finish(1, a, key_sum[to, :] * factor, gk_ref)
        gv_ref[pl.ds(pl.multiple_of(place[a] * rows, rows), rows), :] = value_sum[to, :].astype(BF16)
    gain_grad_ref[0:1, :] = gain_rows[0]
    gain_grad_ref[1:2, :] = gain_rows[1]


def attention(place, pairs, values, scales, gains, tables, row_docs, col_docs, grad_mixed=None):
    total = pairs.shape[0]
    blocks = place.shape[0]
    heads = values.shape[1] // HEAD_DIM
    size = max(256, total // blocks)
    whole = lambda h: (0, 0)
    column = lambda h: (0, h)
    in_specs = [
        pl.BlockSpec(memory_space=pltpu.SMEM),
        pl.BlockSpec((total, HEAD_DIM), lambda h: (0, h)),
        pl.BlockSpec((total, HEAD_DIM), lambda h: (0, heads + h)),
        pl.BlockSpec((total, HEAD_DIM), column),
        pl.BlockSpec((total, 2), whole),
        pl.BlockSpec((2, HEAD_DIM), column),
        pl.BlockSpec((total, HEAD_DIM), whole),
        pl.BlockSpec((total, HEAD_DIM), whole),
        pl.BlockSpec((total, 1), whole),
        pl.BlockSpec((1, total), whole),
    ]
    operands = [place, pairs, pairs, values, scales, gains, *tables, row_docs, col_docs]
    held = [pltpu.VMEM((total, HEAD_DIM), BF16)] * 3
    params = pltpu.CompilerParams(vmem_limit_bytes=VMEM_BYTES)
    work = total * total * HEAD_DIM * heads
    if grad_mixed is None:
        return pl.pallas_call(
            functools.partial(attend_kernel, blocks, size),
            grid=(heads,),
            in_specs=in_specs,
            out_specs=pl.BlockSpec((total, HEAD_DIM), column),
            out_shape=jax.ShapeDtypeStruct((total, heads * HEAD_DIM), BF16),
            scratch_shapes=held,
            compiler_params=params,
            cost_estimate=pl.CostEstimate(
                flops=4 * work, bytes_accessed=pairs.size * 8, transcendentals=total * total
            ),
        )(*operands)
    return pl.pallas_call(
        functools.partial(attend_back_kernel, blocks, size),
        grid=(heads,),
        in_specs=in_specs + [pl.BlockSpec((total, HEAD_DIM), column)],
        out_specs=[pl.BlockSpec((total, HEAD_DIM), column)] * 3
        + [pl.BlockSpec((total, 2), whole), pl.BlockSpec((2, HEAD_DIM), column)],
        out_shape=[
            jax.ShapeDtypeStruct((total, heads * HEAD_DIM), F32),
            jax.ShapeDtypeStruct((total, heads * HEAD_DIM), F32),
            jax.ShapeDtypeStruct((total, heads * HEAD_DIM), BF16),
            jax.ShapeDtypeStruct((total, 2), F32),
            jax.ShapeDtypeStruct((2, heads * HEAD_DIM), F32),
        ],
        scratch_shapes=held + [pltpu.VMEM((total, HEAD_DIM), F32)] * 2,
        compiler_params=params,
        cost_estimate=pl.CostEstimate(
            flops=10 * work, bytes_accessed=pairs.size * 16, transcendentals=total * total
        ),
    )(*operands, grad_mixed)


def router_chances(inputs, router, experts):
    logits = dot_nt(inputs, router)
    column = lax.broadcasted_iota(jnp.int32, logits.shape, 1)
    logits = jnp.where(column < experts, logits, MASKED)
    raised = jnp.exp(logits - jnp.max(logits, axis=-1, keepdims=True))
    return raised / jnp.sum(raised, axis=-1, keepdims=True)


def acts_kernel(experts, blocks, per, at_ref, *refs):
    count = blocks * per
    pieces = refs[:count]
    (
        side_ref, router_ref, wg_ref, wu_ref, wd_ref,
        x_out, u_out, hidden_ref, gate_grad_ref, up_grad_ref, sums_ref, x_buffer, u_buffer, sems,
    ) = refs[count:]
    step = pl.program_id(0)
    sides = [side_ref.at[at_ref[2 + r]] for r in range(count)]

    def copies_of(block):
        slot = block % 2
        return piece_copies(pieces, block, per, x_buffer, slot, sems, 0) + piece_copies(
            sides, block, per, u_buffer, slot, sems, per
        )

    stream(blocks, copies_of)
    owned, width, _ = wg_ref.shape
    inputs, upstream = x_buffer[step % 2], u_buffer[step % 2, :, :width]
    chosen = u_buffer[step % 2, :, width:].astype(F32)
    x_out[...] = inputs
    u_out[...] = upstream
    gates = router_chances(inputs, router_ref[...], experts) * chosen
    gate_at = lax.broadcasted_iota(jnp.int32, gates.shape, 1)
    column = lax.broadcasted_iota(jnp.int32, sums_ref.shape, 1)
    sums = jnp.zeros(sums_ref.shape, F32)
    for e in range(owned):
        gate_act = dot(inputs, wg_ref[e])
        up_act = dot(inputs, wu_ref[e])
        grad_raw = dot_nt(upstream, wd_ref[e])
        expert = at_ref[0] * owned + e
        gate = jnp.sum(jnp.where(gate_at == expert, gates, 0.0), axis=-1, keepdims=True)
        sigma = jax.nn.sigmoid(gate_act)
        active = gate_act * sigma
        hidden = active * up_act
        grad_gate = jnp.sum(hidden * grad_raw, axis=-1, keepdims=True)
        high = grad_gate.astype(BF16).astype(F32)
        sums = jnp.where(column == expert, high, sums)
        sums = jnp.where(column == expert + experts, grad_gate - high, sums)
        grad_hidden = grad_raw * gate
        hidden_ref[e] = (hidden * gate).astype(BF16)
        gate_grad_ref[e] = (grad_hidden * up_act * sigma * (1.0 + gate_act * (1.0 - sigma))).astype(BF16)
        up_grad_ref[e] = (grad_hidden * active).astype(BF16)
    sums_ref[...] = sums.astype(BF16)


def run_acts(at, pieces, sides, router, w_gate, w_up, w_down, experts, parts):
    rows, width = pieces[0].shape
    total = rows * len(pieces)
    owned, _, hidden = w_gate.shape
    piece = hidden // parts
    per = max(1, 256 // rows)
    blocks, size = len(pieces) // per, rows * per
    extra = 128 * -(-2 * experts // 128)
    lanes = router.shape[0]
    token = lambda i, at: (i, 0)
    once = pl.Buffered(1)
    acts = jax.ShapeDtypeStruct((owned, total, piece), BF16)
    act_spec = pl.BlockSpec((owned, size, piece), lambda i, at: (0, i, 0))
    return pl.pallas_call(
        functools.partial(acts_kernel, experts, blocks, per),
        grid_spec=pltpu.PrefetchScalarGridSpec(
            num_scalar_prefetch=1,
            grid=(blocks,),
            in_specs=[pl.BlockSpec(memory_space=pl.ANY)] * (len(pieces) + 1)
            + [
                pl.BlockSpec((lanes, width), lambda i, at: (0, 0), pipeline_mode=once),
                pl.BlockSpec((owned, width, piece), lambda i, at: (0, 0, at[1]), pipeline_mode=once),
                pl.BlockSpec((owned, width, piece), lambda i, at: (0, 0, at[1]), pipeline_mode=once),
                pl.BlockSpec((owned, piece, width), lambda i, at: (0, at[1], 0), pipeline_mode=once),
            ],
            out_specs=[pl.BlockSpec((size, width), token)] * 2
            + [act_spec] * 3
            + [pl.BlockSpec((size, extra), token)],
            scratch_shapes=[
                pltpu.VMEM((2, size, width), BF16),
                pltpu.VMEM((2, size, width + lanes), BF16),
                pltpu.SemaphoreType.DMA((2, 2 * per)),
            ],
        ),
        out_shape=[
            jax.ShapeDtypeStruct((total, width), BF16),
            jax.ShapeDtypeStruct((total, width), BF16),
            acts,
            acts,
            acts,
            jax.ShapeDtypeStruct((total, extra), BF16),
        ],
        compiler_params=pltpu.CompilerParams(vmem_limit_bytes=VMEM_BYTES),
        cost_estimate=pl.CostEstimate(
            flops=6 * total * width * piece * owned,
            bytes_accessed=2 * (4 * total * width + 3 * owned * piece * (total + width)),
            transcendentals=total * piece * owned,
        ),
    )(at, *pieces, sides, router, w_gate, w_up, w_down)


def rows_back_kernel(blocks, per, at_ref, gate_ref, up_ref, sums_ref, wg_ref, wu_ref, near_ref, far_ref):
    back = dot_nt(gate_ref[0], wg_ref[0]) + dot_nt(up_ref[0], wu_ref[0])
    for e in range(1, wg_ref.shape[0]):
        back += dot_nt(gate_ref[e], wg_ref[e]) + dot_nt(up_ref[e], wu_ref[e])
    back = back.astype(BF16)
    step = pl.program_id(0)
    rows, width = near_ref.shape[2], back.shape[1]

    def store(out_ref):
        for i in range(per):
            at = at_ref[2 + step * per + i] // 2 % per
            part = slice(i * rows, (i + 1) * rows)
            out_ref[0, at, :, :width] = back[part]
            out_ref[0, at, :, width:] = sums_ref[part, :]

    pl.when(step < blocks // 2)(lambda: store(near_ref))
    pl.when(step >= blocks // 2)(lambda: store(far_ref))


def rows_out_kernel(sets, blocks, per, at_ref, *refs):
    *hidden_refs, wd_ref, out_ref = refs
    step = pl.program_id(0)
    rows = out_ref.shape[4]
    for k, hidden_ref in enumerate(hidden_refs):

        @pl.when(step // blocks == k)
        def _():
            out = dot(hidden_ref[0], wd_ref[0])
            for e in range(1, wd_ref.shape[0]):
                out += dot(hidden_ref[e], wd_ref[e])
            for i in range(per):
                at = at_ref[2 + (step - k * blocks) * per + i] // 2 % per
                out_ref[0, at, 0, 0] = out[i * rows : (i + 1) * rows].astype(BF16)


def run_out(at, hiddens, w_down, rows):
    owned, total, piece = hiddens[0].shape
    sets, width = len(hiddens), w_down.shape[2]
    seq_size = total // rows
    per = max(1, 256 // rows)
    size, blocks = rows * per, seq_size // per

    def hidden_at(k):
        return lambda i, at: (0, jnp.clip(i - k * blocks, 0, blocks - 1), 0)

    def out_at(i, at):
        first = at[2 + (i % blocks) * per]
        return (first // (2 * per), 0, first % 2, i // blocks, 0, 0)

    out = pl.pallas_call(
        functools.partial(rows_out_kernel, sets, blocks, per),
        grid_spec=pltpu.PrefetchScalarGridSpec(
            num_scalar_prefetch=1,
            grid=(sets * blocks,),
            in_specs=[pl.BlockSpec((owned, size, piece), hidden_at(k)) for k in range(sets)]
            + [
                pl.BlockSpec(
                    (owned, piece, width), lambda i, at: (0, at[1], 0), pipeline_mode=pl.Buffered(1)
                )
            ],
            out_specs=pl.BlockSpec((1, per, 1, 1, rows, width), out_at),
        ),
        out_shape=jax.ShapeDtypeStruct((seq_size // (2 * per), per, 2, sets, rows, width), BF16),
        compiler_params=pltpu.CompilerParams(vmem_limit_bytes=VMEM_BYTES),
        cost_estimate=pl.CostEstimate(
            flops=2 * sets * total * width * piece * owned,
            bytes_accessed=2 * sets * total * (width + owned * piece),
            transcendentals=0,
        ),
    )(at, *hiddens, w_down)
    return out.reshape(seq_size, sets, rows, width)


def run_back(at, gates, ups, sums, w_gate, w_up, rows):
    owned, total, piece = gates.shape
    chips = total // (2 * rows)
    per = max(1, 256 // rows)
    size, blocks = rows * per, total // (rows * per)
    middle = blocks // 2
    width, extra = w_gate.shape[1], sums.shape[1]
    act_spec = pl.BlockSpec((owned, size, piece), lambda i, at: (0, i, 0))
    weight_spec = pl.BlockSpec(
        (owned, width, piece), lambda i, at: (0, 0, at[1]), pipeline_mode=pl.Buffered(1)
    )

    def out_spec(first, last):
        return pl.BlockSpec(
            (1, per, rows, width + extra),
            lambda i, at: (at[2 + jnp.clip(i, first, last) * per] // (2 * per), 0, 0, 0),
        )

    out = jax.ShapeDtypeStruct((chips // per, per, rows, width + extra), BF16)
    results = pl.pallas_call(
        functools.partial(rows_back_kernel, blocks, per),
        grid_spec=pltpu.PrefetchScalarGridSpec(
            num_scalar_prefetch=1,
            grid=(blocks,),
            in_specs=[act_spec] * 2
            + [pl.BlockSpec((size, extra), lambda i, at: (i, 0))]
            + [weight_spec] * 2,
            out_specs=[out_spec(0, middle - 1), out_spec(middle, blocks - 1)],
        ),
        out_shape=[out, out],
        compiler_params=pltpu.CompilerParams(vmem_limit_bytes=VMEM_BYTES),
        cost_estimate=pl.CostEstimate(
            flops=4 * total * width * piece * owned,
            bytes_accessed=2 * (total * width + 2 * owned * piece * (total + width)),
            transcendentals=0,
        ),
    )(at, gates, ups, sums, w_gate, w_up)
    return [item.reshape(chips, rows, width + extra) for item in results]


def down_kernel(sets, at_ref, *refs):
    out_ref = refs[-1]
    for e in range(out_ref.shape[1]):
        term = dot_tn(refs[0][e], refs[sets][...])
        for i in range(1, sets):
            term += dot_tn(refs[i][e], refs[sets + i][...])
        out_ref[0, e] = term.astype(BF16)


def down_blocks(targets, hiddens, upstreams, group, width):
    owned, total, piece = hiddens[0].shape
    deep = piece // group
    sets, count = len(hiddens), targets.shape[0]
    wide = min(512, width)
    return pl.pallas_call(
        functools.partial(down_kernel, sets),
        grid_spec=pltpu.PrefetchScalarGridSpec(
            num_scalar_prefetch=1,
            grid=(count, width // wide),
            in_specs=[pl.BlockSpec((owned, total, deep), lambda g, j, at: (0, 0, at[g]))] * sets
            + [pl.BlockSpec((total, wide), lambda g, j, at: (0, j))] * sets,
            out_specs=pl.BlockSpec((1, owned, deep, wide), lambda g, j, at: (g, 0, 0, j)),
        ),
        out_shape=jax.ShapeDtypeStruct((count, owned, deep, width), BF16),
        compiler_params=pltpu.CompilerParams(vmem_limit_bytes=VMEM_BYTES),
        cost_estimate=pl.CostEstimate(
            flops=2 * sets * count * owned * total * deep * width,
            bytes_accessed=2 * sets * total * (width + owned * deep),
            transcendentals=0,
        ),
    )(targets, *hiddens, *upstreams)


def in_kernel(sets, at_ref, *refs):
    out_ref = refs[-1]
    for e in range(out_ref.shape[2]):
        term = dot_tn(refs[0][...], refs[sets][e])
        for i in range(1, sets):
            term += dot_tn(refs[i][...], refs[sets + i][e])
        out_ref[0, 0, e] = term.astype(BF16)


def in_blocks(targets, inputs, acts, group, parts):
    owned, total, piece = acts[0].shape
    width = inputs[0].shape[1]
    deep = width // (group * parts)
    sets, count = len(inputs), targets.shape[0]
    held = pl.BlockSpec((owned, total, piece), lambda g, p, at: (0, 0, 0), pipeline_mode=pl.Buffered(1))
    return pl.pallas_call(
        functools.partial(in_kernel, sets),
        grid_spec=pltpu.PrefetchScalarGridSpec(
            num_scalar_prefetch=1,
            grid=(count, parts),
            in_specs=[pl.BlockSpec((total, deep), lambda g, p, at: (0, p * group + at[g]))] * sets
            + [held] * sets,
            out_specs=pl.BlockSpec((1, 1, owned, deep, piece), lambda g, p, at: (g, p, 0, 0, 0)),
        ),
        out_shape=jax.ShapeDtypeStruct((count, parts, owned, deep, piece), BF16),
        compiler_params=pltpu.CompilerParams(vmem_limit_bytes=VMEM_BYTES),
        cost_estimate=pl.CostEstimate(
            flops=2 * sets * count * parts * owned * total * deep * piece,
            bytes_accessed=4 * sets * owned * total * piece,
            transcendentals=0,
        ),
    )(targets, *inputs, *acts)


def on_device(
    tokens,
    segments,
    expert_ids,
    w_query,
    w_key,
    w_value,
    w_out,
    w_router,
    attn_gain,
    query_gain,
    key_gain,
    ffn_gain,
    w_gate,
    w_up,
    w_down,
    out_grad,
):
    seq_size, batch_size = lax.axis_size("seq"), lax.axis_size("batch")
    seq_at, batch_at = lax.axis_index("seq"), lax.axis_index("batch")
    parts = 2 if batch_size % 2 == 0 else 1
    half = batch_size // parts
    part_at, in_group = batch_at // half, batch_at % half
    low_tokens = tokens[0]
    inputs = low_tokens.astype(F32)
    rows, width = inputs.shape
    total = rows * seq_size
    experts = w_router.shape[1]
    owned = w_gate.shape[0]
    wide = width // seq_size
    shard = w_query.shape[0]

    masks = masks_of(seq_size)
    order = seq_at ^ jnp.array(masks, jnp.int32)
    place = jnp.array([masks.index(m) for m in range(seq_size)], jnp.int32)[
        jnp.arange(seq_size, dtype=jnp.int32) ^ seq_at
    ]

    def reordered(values, by):
        return values.reshape(-1, seq_size, rows)[:, by].reshape(values.shape)

    masks = masks_of(seq_size)
    order = seq_at ^ jnp.array(masks, jnp.int32)
    place = jnp.array([masks.index(m) for m in range(seq_size)], jnp.int32)[
        jnp.arange(seq_size, dtype=jnp.int32) ^ seq_at
    ]
    here = jnp.concatenate([jnp.stack([seq_at, batch_at]).astype(jnp.int32), order])

    def reordered(values, by):
        return values.reshape(-1, seq_size, rows)[:, by].reshape(values.shape)

    masks = masks_of(seq_size)
    order = seq_at ^ jnp.array(masks, jnp.int32)
    place = jnp.array([masks.index(m) for m in range(seq_size)], jnp.int32)[
        jnp.arange(seq_size, dtype=jnp.int32) ^ seq_at
    ]
    here = jnp.concatenate([jnp.stack([seq_at, batch_at]).astype(jnp.int32), order])
    at = jnp.concatenate([jnp.stack([seq_at, part_at]).astype(jnp.int32), order])

    def reordered(values, by):
        return values.reshape(-1, seq_size, rows)[:, by].reshape(values.shape)

    near_tokens = gather_near(low_tokens)

    def cut_of(*weights):
        return jnp.concatenate(
            [w.reshape(shard, seq_size, wide).transpose(1, 0, 2) for w in weights], axis=2
        )

    def exchange(blocks):
        return lax.all_to_all(blocks, "seq", split_axis=0, concat_axis=0, tiled=True)

    small = jnp.concatenate(
        [jnp.stack([attn_gain, query_gain, key_gain, ffn_gain]), w_router.T], axis=0
    )
    items, fit = experts + 4, 2 * wide // shard
    deep = 8 * -(-items // (8 * fit))
    small = jnp.pad(small, ((0, deep * fit - items), (0, 0))).reshape(1, deep, 2 * wide)
    small = jnp.broadcast_to(small, (seq_size, deep, 2 * wide))
    pair_cut = exchange(jnp.concatenate([cut_of(w_query, w_key), small], axis=1))

    ids = expert_ids[0]
    lanes = 128 * -(-experts // 128)
    choices = jnp.any(ids[:, :, None] == jnp.arange(lanes, dtype=jnp.int32), axis=1)
    side = jnp.concatenate([out_grad[0], choices.astype(BF16)], axis=1)
    partner = [hop(side, "batch", half)] if parts == 2 else []
    token_pieces = near_tokens + [hop(after(piece, pair_cut, *partner), "seq", 1) for piece in near_tokens]
    value_cut = exchange(after(cut_of(w_value), pair_cut))
    pair_pieces = gather_batch(after(pair_cut, *token_pieces), value_cut)
    value_pieces = gather_batch(after(value_cut, *pair_pieces))
    out_pieces = gather_batch(after(w_out, *pair_pieces), *value_pieces)
    small = jnp.stack([item[:, shard:] for item in pair_pieces])
    small = small.reshape(batch_size, seq_size, deep * fit, shard)[
        jnp.arange(batch_size, dtype=jnp.int32) ^ batch_at
    ]
    small = small.transpose(2, 1, 0, 3).reshape(deep * fit, width)
    gains = small[:4].astype(F32)
    attn_norm_gain, ffn_norm_gain = gains[0], gains[3]
    head_gains = lax.dynamic_slice_in_dim(gains[1:3], seq_at * wide, wide, 1)
    router = jnp.pad(small[4:items], ((0, lanes - experts), (0, 0)))
    w_mix = jnp.zeros((batch_size, shard, width), BF16)
    for t, piece in enumerate(out_pieces):
        w_mix = put(w_mix, piece[None], (batch_at ^ t, 0, 0))
    w_mix = w_mix.reshape(wide, width)

    sides = [
        lax.all_gather(after(item, *pins), "seq", axis=0)
        for item, pins in zip([side, *partner], ([value_cut, *pair_pieces[1:3]], pair_pieces))
    ]
    counts = jnp.sum(sides[0][:, :, width:].astype(F32), axis=(0, 1)).astype(jnp.int32)
    counts_here = lax.dynamic_slice_in_dim(counts, seq_at * owned, owned, 0)

    normed, pairs, squares, pair_weights = project_pairs(
        here, token_pieces, pair_pieces, shard, attn_norm_gain[None]
    )
    values, value_weights = project_values(here, normed, value_pieces)
    pair_weights, value_weights = (w.reshape(width, -1) for w in (pair_weights, value_weights))

    def sum_seq(values):
        return jnp.sum(lax.all_gather(values, "seq", axis=0), axis=0)

    scales = lax.rsqrt(sum_seq(squares) / width + EPSILON)
    rates = jnp.power(
        ROTARY_BASE, -jnp.arange(HEAD_DIM // 2, dtype=F32) * (2.0 / HEAD_DIM)
    )
    angles = jnp.arange(total, dtype=F32)[:, None] * rates[None, :]
    cosine, sine = jnp.cos(angles), jnp.sin(angles)
    tables = (
        jnp.concatenate([cosine, cosine], axis=1),
        jnp.concatenate([-sine, sine], axis=1),
    )
    attend = functools.partial(
        attention,
        place,
        pairs,
        values,
        scales.T,
        head_gains,
        tables,
        segments[0][:, None],
        segments[0][None, :],
    )
    mixed_low = after(attend(), sides[0])
    middle = total // 2
    far = dot(mixed_low[middle:], w_mix).astype(BF16)
    residual = inputs + scatter_seq(dot(mixed_low[:middle], w_mix).astype(BF16), far)[0]
    ffn_scale = norm_scale(residual)
    ffn_unit = residual * ffn_scale
    ffn_in = (ffn_unit * ffn_norm_gain).astype(BF16)

    def acts_of(k, pieces):
        return run_acts(at, pieces, sides[k], router, w_gate, w_up, w_down, experts, parts)

    ffn_pieces = gather_seq(ffn_in)
    results = [acts_of(0, ffn_pieces)]
    if parts == 2:
        partner = hop(ffn_in, "batch", half)
        near = gather_near(after(partner, *ffn_pieces))
        near = [after(piece, results[0][0]) for piece in near]
        results.append(acts_of(1, near + [hop(piece, "seq", 1) for piece in near]))
    all_ffn, upstreams, hiddens, gate_acts, up_acts, sums = zip(*results)
    own = in_group[None].astype(jnp.int32)
    others = jnp.stack([in_group ^ t for t in range(1, half)]).astype(jnp.int32) if half > 1 else None
    down = functools.partial(down_blocks, hiddens=hiddens, upstreams=upstreams, group=half, width=width)
    into = functools.partial(in_blocks, inputs=all_ffn, group=half, parts=parts)

    def send_group(theirs):
        return [hop(theirs[t - 1], "batch", t) for t in range(1, half)]

    def gather_group(theirs):
        groups = [list(range(first, first + half)) for first in range(0, batch_size, half)]
        blocks = lax.all_gather(theirs, "batch", axis=0, axis_index_groups=groups)
        return [take_block(blocks, in_group ^ t)[t - 1] for t in range(1, half)]

    def group_sum(mine, moved):
        total = mine[0].astype(F32)
        for item in moved:
            total = total + item.astype(F32)
        return total

    def swap_part(summed):
        return hop(take_block(summed, 1 - part_at).astype(BF16), "batch", half)

    gate_moved = up_moved = down_moved = ()
    at_back = at
    if half > 1:
        gate_theirs = into(others, acts=gate_acts)
        gate_moved = send_group(gate_theirs)
        at_back = after(at, gate_theirs)
    backs, sent = [], []
    for k in reversed(range(parts)):
        near, far = run_back(at_back, gate_acts[k], up_acts[k], sums[k], w_gate, w_up, rows)
        if half > 1 and not sent:
            up_theirs = into(after(others, near), acts=up_acts)
            near = after(near, up_theirs)
        if k == 0:
            mix = run_out(after(at, near), hiddens, w_down, rows)
            far = after(far, mix, *backs, *gate_moved)
        summed, low = scatter_chips(near, far)
        backs.insert(0, summed)
        sent.append(low)
        at_back = after(at, low)
    gate_mine = last = into(after(own, *sent), acts=gate_acts)
    other = hop(backs[1].astype(BF16), "batch", half) if parts == 2 else gate_mine
    if half > 1:
        last = down_theirs = down(after(others, gate_mine))
    gate_sum = group_sum(gate_mine, gate_moved)
    up_mine = into(after(own, last, other), acts=up_acts)
    gate_other = swap_part(gate_sum) if parts == 2 else gate_sum
    if half > 1:
        up_moved = gather_group(up_theirs)
        down_moved = gather_group(down_theirs)
    back = after(backs[0], up_mine, gate_sum)
    if parts == 2:
        back = back + other.astype(F32)

    grad_ffn_in = back[:, :width]
    grad_chances = choices[:, :experts] * (
        back[:, width : width + experts] + back[:, width + experts : width + 2 * experts]
    )
    chances = router_chances(ffn_in, router, experts)[:, :experts]
    grad_logits = (
        chances * (grad_chances - jnp.sum(chances * grad_chances, axis=-1, keepdims=True))
    ).astype(BF16)
    grad_ffn_in = grad_ffn_in + dot(grad_logits, router[:experts])
    scaled = grad_ffn_in * ffn_norm_gain
    inner = jnp.mean(scaled * ffn_unit, axis=-1, keepdims=True)
    grad_residual = out_grad[0].astype(F32) + ffn_scale * (scaled - ffn_unit * inner)
    grad_attn = grad_residual.astype(BF16)

    grad_near = gather_near(grad_attn)
    arrived = grad_near[1:]
    up_sum = group_sum(up_mine, [after(item, grad_attn) for item in up_moved])
    grad_near[0] = after(grad_attn, up_sum, *arrived)
    grad_pieces = grad_near + [hop(piece, "seq", 1) for piece in grad_near]
    up_other = swap_part(up_sum) if parts == 2 else up_sum
    grad_mixed, out_term = mix_back(grad_pieces, after(mixed_low, gate_other), w_mix)
    mix = lax.psum_scatter(after(mix, grad_mixed), "seq", scatter_dimension=0)
    scaled_q, scaled_k, value_low, inner, gain_terms = attend(grad_mixed=grad_mixed)

    def term_of(values):
        return dot_tn(normed, values).astype(BF16).reshape(seq_size * batch_size, shard, -1)

    value_term = term_of(value_low)
    inner = reordered(sum_seq(after(inner.T, value_term)), order).T / width
    rel_scales = reordered(scales, order).T
    lows = []
    for i, item in enumerate((scaled_q, scaled_k)):
        scale = rel_scales[:, i : i + 1]
        unit = pairs[:, i * wide : (i + 1) * wide] * scale
        lows.append((scale * (item - unit * inner[:, i : i + 1])).astype(BF16))
    pair_low = jnp.concatenate(lows, axis=1)
    pair_term = term_of(pair_low)
    late_low = after(pair_low, pair_term)

    def rows_of(at):
        return (dot_nt(late_low[at], pair_weights) + dot_nt(value_low[at], value_weights)).astype(BF16)

    far = rows_of(slice(middle, total))
    grad_normed, low = scatter_seq(rows_of(slice(0, middle)), far)
    mix_other = hop(after(mix[1], value_low), "batch", half) if parts == 2 else mix
    grad_normed = after(grad_normed, mix_other)
    down_mine = down(after(own, *low))

    def head_sums(term, extra):
        term = jnp.concatenate([term, *extra], axis=1)
        term = lax.all_to_all(term, ("seq", "batch"), split_axis=0, concat_axis=0, tiled=True)
        term = after(term, grad_normed)
        total = jnp.sum(term[:, :shard].reshape(seq_size, batch_size, shard, -1).astype(F32), axis=1)
        return total, jnp.sum(term[:, shard:].astype(F32), axis=0)

    def two_parts(values):
        high = values.astype(BF16)
        return jnp.concatenate([high, (values - high.astype(F32)).astype(BF16)], axis=0)

    def in_rows(items):
        fit = wide // shard
        deep = 8 * -(-items.shape[0] // (8 * fit))
        items = jnp.pad(items, ((0, deep * fit - items.shape[0]), (0, 0), (0, 0), (0, 0)))
        return items.transpose(1, 2, 0, 3).reshape(seq_size * batch_size, deep, wide)

    router_term = jnp.concatenate(
        [dot_tn(grad_logits, ffn_in), jnp.sum(grad_ffn_in * ffn_unit, axis=0)[None]], axis=0
    )
    router_items = two_parts(router_term).reshape(-1, seq_size, batch_size, shard)
    gain_items = two_parts(gain_terms).reshape(4, 1, batch_size, shard)
    mine_only = (jnp.arange(seq_size) == seq_at)[None, :, None, None]
    gain_items = jnp.where(mine_only, gain_items, jnp.zeros_like(gain_items))
    items = in_rows(jnp.concatenate([gain_items, router_items], axis=0))
    value_sums, items = head_sums(value_term, [items])
    items = items.reshape(-1, shard)
    gain_sum = items[0:2] + items[2:4]
    router_sum = items[4 : 5 + experts] + items[5 + experts : 6 + 2 * experts]
    router_grad, ffn_gain_grad = router_sum[:experts].T, router_sum[experts]
    pair_sums, _ = head_sums(pair_term, [])
    query_grad, key_grad, value_grad = (
        item.transpose(1, 0, 2).reshape(shard, width)
        for item in (pair_sums[:, :, :wide], pair_sums[:, :, wide:], value_sums)
    )

    def spread(summed, other):
        if parts == 1:
            return summed[0]
        keep, other = take_block(summed, part_at), other.astype(F32)
        return jnp.where(
            part_at == 0,
            jnp.concatenate([keep, other], axis=-1),
            jnp.concatenate([other, keep], axis=-1),
        )

    down_grad = group_sum(down_mine, [after(item, pair_term) for item in down_moved])
    gate_grad = spread(gate_sum, after(gate_other, pair_term))
    up_grad = spread(up_sum, after(up_other, grad_normed))
    out_proj_grad = scatter_batch(
        out_term.reshape(batch_size, shard, width), batch_at, BF16, far, grad_normed
    )

    mine = mix[0].astype(F32)
    if parts == 2:
        mine = mine + mix_other.astype(F32)
    block_out = (residual + mine).astype(BF16)

    attn_scale = norm_scale(inputs)
    attn_unit = inputs * attn_scale
    scaled = grad_normed * attn_norm_gain
    inner = jnp.mean(scaled * attn_unit, axis=-1, keepdims=True)
    grad_input = grad_residual + attn_scale * (scaled - attn_unit * inner)
    attn_gain_grad = (
        jnp.sum(
            query_grad * w_query.astype(F32)
            + key_grad * w_key.astype(F32)
            + value_grad * w_value.astype(F32),
            axis=1,
        )
        / attn_gain.astype(F32)
    )
    return (
        block_out[None],
        grad_input[None],
        query_grad,
        key_grad,
        value_grad,
        out_proj_grad,
        router_grad,
        attn_gain_grad,
        gain_sum[0],
        gain_sum[1],
        ffn_gain_grad,
        gate_grad,
        up_grad,
        down_grad,
        counts_here[None],
    )


def solution(mesh):
    in_specs = (
        P("batch", "seq", None),
        P("batch", None),
        P("batch", "seq", None),
        P(("seq", "batch"), None),
        P(("seq", "batch"), None),
        P(("seq", "batch"), None),
        P(("seq", "batch"), None),
        P(("seq", "batch"), None),
        P(("seq", "batch")),
        P(("seq", "batch")),
        P(("seq", "batch")),
        P(("seq", "batch")),
        P("seq", None, None),
        P("seq", None, None),
        P("seq", None, None),
        P("batch", "seq", None),
    )
    out_specs = (
        P("batch", "seq", None),
        P("batch", "seq", None),
        P(("seq", "batch"), None),
        P(("seq", "batch"), None),
        P(("seq", "batch"), None),
        P(("seq", "batch"), None),
        P(("seq", "batch"), None),
        P(("seq", "batch")),
        P(("seq", "batch")),
        P(("seq", "batch")),
        P(("seq", "batch")),
        P("seq", "batch", None),
        P("seq", "batch", None),
        P("seq", "batch", None),
        P("batch", "seq"),
    )
    return jax.shard_map(
        on_device, mesh=mesh, in_specs=in_specs, out_specs=out_specs, check_vma=False
    )
```
